32 devices in a mesh: expert: 8 (over z, y), tensor: 4 (over x, core).
Axes of the slice: x: 2, y: 2, z: 4, core: 2. Of those that a mesh axis runs over, the one named last changes fastest.
Arguments:
- attn_heads: bfloat16 [1024, 4096], P('expert', 'tensor'), may hold values from -6 to 6
- out_proj: bfloat16 [4096, 4096], P('tensor', 'expert'), may hold values from -0.09375 to 0.09375
- residual: bfloat16 [1024, 4096], P('expert'), may hold values from -6 to 6
- norm_gain: float32 [4096], replicated, may hold values from 0.1 to 1.9
- route_ids: int32 [1024, 8], P('expert'), may hold values from 0 to 63, all different within a row; in each aligned block of 128 rows (0 to 127, 128 to 255, ...) at most 18 rows name the same one
- route_weights: float32 [1024, 8], P('expert'), may hold values from 0.05 to 1
- w_gate: bfloat16 [64, 4096, 1536], P('expert', None, 'tensor'), may hold values from -0.09375 to 0.09375
- w_up: bfloat16 [64, 4096, 1536], P('expert', None, 'tensor'), may hold values from -0.09375 to 0.09375
- w_down: bfloat16 [64, 1536, 4096], P('expert', 'tensor'), may hold values from -0.15625 to 0.15625
Outputs:
- layer_out: bfloat16 [1024, 4096], P('expert', 'tensor')
The draws below stay inside these ranges and needn't reach their ends.
Inputs may be any that keep to these rules, and one draw needn't show every extreme that they name: `route_ids`: each row names 8 different experts. In aligned blocks of 128 rows no expert is named more than 18 times, a bound that some block reaches.
All inputs are finite; a program needn't handle non-finite values.
Results may differ from the reference program's by a relative error of at most 0.015.
Values may be sent and summed in bfloat16 or wider, within the bound.
No kernel may reach another device: no remote copies, remote signals or barrier semaphores. Data moves between devices by JAX's collectives and lax.ppermute only.
A program may use at most 192 MiB of HBM per device.

```python
import math
import jax
import jax.numpy as jnp
import numpy as np
from jax import lax

D = 4096
HEADS = 32
HD = 128
FF = 1536
EXPERTS = 64
TOP = 8
TOK_DEV = 128
CAP = 18
TOKENS = 1024
N_EXPERT = 8
N_TENSOR = 4


def block_levels(rng, dims, cuts, least, top_value):
    def one(axis_at, blocks):
        draws = jax.random.uniform(jax.random.fold_in(jax.random.fold_in(rng, 6), axis_at), (blocks,), jnp.float32, least / len(cuts), top_value / len(cuts))
        return jnp.repeat(jnp.exp(draws), dims[axis_at] // blocks).reshape((-1,) + (1,) * (len(dims) - axis_at - 1))

    factor_of = one(*cuts[0])
    for cut in cuts[1:]:
        factor_of = factor_of * one(*cut)
    return factor_of


def deal_out(stream_key, own, number, rows, count, top, reach, slope):
    sequence = jax.random.permutation(stream_key, count)
    crowded, ordinary = load_shares(count, rows * top, reach, slope, True), load_shares(count, rows * top, reach, slope, False)
    places = jnp.arange(count)

    def named(sizes, turn):
        used = int((sizes > 0).sum())
        fixed = max(1, used // 4)
        passed = fixed + (places - fixed + turn * (used - fixed)) % max(1, count - fixed)
        return jnp.zeros((count,), jnp.int32).at[sequence[jnp.where(places < fixed, places, passed)]].set(jnp.asarray(sizes, jnp.int32))

    sizes = jnp.where(number % 4 == 0, named(crowded, number // 4), named(ordinary, number - number // 4 - 1))
    mixed = jax.random.permutation(jax.random.fold_in(own, 3), count)
    donor, receiver = mixed[0:count // 2 * 2:2], mixed[1:count // 2 * 2:2]
    margin = jnp.minimum(sizes[donor] - 1, reach - sizes[receiver]) // 2
    margin = jnp.where((donor == sequence[0]) | (receiver == sequence[0]) | (sizes[receiver] == 0), 0, jnp.maximum(margin, 0))
    passed = jax.random.randint(jax.random.fold_in(own, 4), (count // 2,), 0, 1 << 20) % (margin + 1)
    sizes = sizes.at[donor].add(-passed).at[receiver].add(passed)
    labels = jnp.searchsorted(jnp.cumsum(sizes), jnp.arange(rows * top), side="right").astype(jnp.int32)
    grid = labels.reshape(top, rows).T
    grid = grid[jax.random.permutation(jax.random.fold_in(own, 1), rows)]
    turn = jax.random.randint(jax.random.fold_in(own, 2), (rows, 1), 0, top)
    return jnp.take_along_axis(grid, (jnp.arange(top)[None, :] + turn) % top, axis=1)


def load_shares(number_of, total, reach, skew, full):
    loads = [(1 << 20) // math.isqrt(rank ** skew) + 1 for rank in range(1, number_of + 1)]
    largest = reach if full else min(reach, max(-(-total // number_of), total * loads[0] // sum(loads)))
    least = 1 if total - largest >= number_of - 1 else 0
    given, rest = [largest] + [least] * (number_of - 1), total - largest - least * (number_of - 1)
    while rest > 0:
        free = [i for i in range(1, number_of) if given[i] < largest] or [i for i in range(1, number_of) if given[i] < reach]
        mass, remaining = sum([loads[i] for i in free]), rest
        for i in free:
            extra = min(reach - given[i], max(1, remaining * loads[i] // mass), rest)
            given[i] = given[i] + extra
            rest = rest - extra
    return np.array(given)


def noise(rng, extent, spread, most, cuts=(), kind=jnp.bfloat16):
    level = block_levels(rng, extent, cuts, -0.22, 0.18) if cuts else 1.0
    drawn = jax.random.normal(rng, extent, jnp.float32) * spread * level
    return jnp.minimum(jnp.maximum(drawn, -most), most).astype(kind)


def setup_inputs(seed: int = 0) -> dict:
    arg_keys = jax.random.split(jax.random.key(seed), 10)
    attn_heads = noise(arg_keys[0], (TOKENS, HEADS * HD), 1.0, 6.0, ((0, 8), (1, 4)))
    out_proj = noise(arg_keys[1], (HEADS * HD, D), (HEADS * HD) ** -0.5, 0.09375, ((0, 4), (1, 8)))
    residual = noise(arg_keys[2], (TOKENS, D), 1.0, 6.0, ((0, 8),))
    norm_gain = jnp.clip(1.0 + 0.18 * jax.random.normal(arg_keys[3], (D,), jnp.float32), 0.1, 1.9)
    route_ids_keys = jax.random.split(jax.random.fold_in(arg_keys[4], 1), TOKENS // TOK_DEV)
    route_ids_turns = jax.random.permutation(jax.random.fold_in(arg_keys[4], 3), TOKENS // TOK_DEV)
    route_ids = jax.vmap(lambda own, number: deal_out(jax.random.fold_in(arg_keys[4], 2), own, number, TOK_DEV, EXPERTS, TOP, CAP, 2))(route_ids_keys, route_ids_turns).reshape((TOKENS, TOP))
    route_weights = jnp.clip(jnp.exp(math.log(1.0) - 2.9957323 * jax.random.uniform(arg_keys[5], (TOKENS, TOP), jnp.float32) ** block_levels(arg_keys[5], (TOKENS, TOP), ((0, 8),), -0.2, 0.2)), 0.05, 1.0)
    w_gate = noise(arg_keys[6], (EXPERTS, D, FF), D ** -0.5, 0.09375, ((0, 8), (2, 4)))
    w_up = noise(arg_keys[7], (EXPERTS, D, FF), D ** -0.5, 0.09375, ((0, 8), (2, 4)))
    w_down = noise(arg_keys[8], (EXPERTS, FF, D), FF ** -0.5, 0.15625, ((0, 8), (1, 4)))
    return {"attn_heads": attn_heads, "out_proj": out_proj, "residual": residual, "norm_gain": norm_gain, "route_ids": route_ids, "route_weights": route_weights, "w_gate": w_gate, "w_up": w_up, "w_down": w_down}


def slot_places(ids):
    row_count, top_count = ids.shape
    onehot = (ids[:, :, None] == jnp.arange(EXPERTS, dtype=jnp.int32)[None, None, :]).astype(jnp.int32)
    flattened = onehot.reshape(row_count * top_count, EXPERTS)
    before = jnp.cumsum(flattened, axis=0).astype(jnp.int32) - flattened
    return lax.optimization_barrier(jnp.sum(before * flattened, axis=1)).astype(jnp.int32).reshape(row_count, top_count)

def reference(attn_heads, out_proj, residual, norm_gain, route_ids, route_weights, w_gate, w_up, w_down):
    attn_out = jnp.dot(attn_heads.astype(jnp.float32), out_proj.astype(jnp.float32))
    hidden = residual.astype(jnp.float32) + attn_out
    normed = (hidden * lax.rsqrt(lax.optimization_barrier(jnp.mean(hidden * hidden, axis=-1, keepdims=True)) + 1e-06) * norm_gain).astype(jnp.bfloat16)
    weights = route_weights / lax.optimization_barrier(jnp.sum(route_weights, axis=-1, keepdims=True))
    group_count = N_EXPERT
    slot_rank = jax.vmap(slot_places)(route_ids.reshape(group_count, TOK_DEV, TOP)).reshape(TOKENS, TOP)
    owner_group = (jnp.arange(TOKENS, dtype=jnp.int32) // TOK_DEV)[:, None]
    flat_index = ((route_ids * group_count + owner_group) * CAP + slot_rank).astype(jnp.int32).reshape(-1)
    token_ids = jnp.broadcast_to(jnp.arange(TOKENS, dtype=jnp.int32)[:, None], (TOKENS, TOP)).reshape(-1)
    slot_token = jnp.full((EXPERTS * group_count * CAP,), TOKENS, dtype=jnp.int32).at[flat_index].set(token_ids)
    slot_weight = jnp.zeros((EXPERTS * group_count * CAP,), jnp.float32).at[flat_index].set(weights.reshape(-1))
    slot_token = slot_token.reshape(EXPERTS, group_count * CAP)
    slot_weight = slot_weight.reshape(EXPERTS, group_count * CAP)
    padded = jnp.concatenate([normed, jnp.zeros((1, D), jnp.bfloat16)], axis=0)
    block_size = FF // N_TENSOR

    def per_expert(mixture, expert):
        chosen = slot_token[expert]
        inputs = padded[chosen].astype(jnp.float32)
        gate_acc = jnp.dot(inputs, w_gate[expert].astype(jnp.float32))
        upper = jnp.dot(inputs, w_up[expert].astype(jnp.float32))
        activation = (jax.nn.silu(gate_acc) * upper).astype(jnp.bfloat16).astype(jnp.float32)
        pieces = jnp.einsum('rtf,tfd->trd', activation.reshape(-1, N_TENSOR, block_size), w_down[expert].astype(jnp.float32).reshape(N_TENSOR, block_size, D))
        summed = lax.optimization_barrier(jnp.sum(pieces.astype(jnp.bfloat16).astype(jnp.float32), axis=0))
        rounded = summed.astype(jnp.bfloat16).astype(jnp.float32)
        mixture = mixture.at[chosen].add(slot_weight[expert][:, None] * rounded)
        return (mixture, None)
    mixture, ignored = lax.scan(per_expert, jnp.zeros((TOKENS + 1, D), jnp.float32), jnp.arange(EXPERTS, dtype=jnp.int32))
    return (hidden + mixture[:TOKENS]).astype(jnp.bfloat16)
```

```python
import functools

import jax
import jax.numpy as jnp
from jax import lax
from jax.experimental import pallas as pl
from jax.experimental.pallas import tpu as pltpu
from jax.sharding import PartitionSpec as P

EXPERTS = 64
CAP = 18
BF16 = jnp.bfloat16
F32 = jnp.float32
PAIR = 2
LANES = 128
VMEM_BYTES = 56 * 1024 * 1024


def slot_places(ids, experts, capacity):
    row_count, top_count = ids.shape
    onehot = (ids[:, :, None] == jnp.arange(experts, dtype=jnp.int32)[None, None, :]).astype(
        jnp.int32
    )
    flattened = onehot.reshape(row_count * top_count, experts)
    before = jnp.cumsum(flattened, axis=0) - flattened
    slot_rank = jnp.sum(before * flattened, axis=1).reshape(row_count, top_count)
    return ids * capacity + slot_rank


def per_device_slots(
    attn_heads, out_proj, residual, norm_gain, route_ids, route_weights, w_gate, w_up, w_down
):
    model_width = residual.shape[1]
    groups = lax.axis_size("expert")
    members = lax.axis_size("tensor")
    member = lax.axis_index("tensor")
    per_group = w_gate.shape[0]
    slot_count = EXPERTS * CAP
    block_cols = model_width // members
    heads_out = jnp.dot(
        attn_heads,
        lax.all_gather(out_proj, "expert", axis=1, tiled=True),
        preferred_element_type=F32,
    )
    attn_out = lax.psum(heads_out.astype(BF16), "tensor").astype(F32)
    hidden = residual.astype(F32) + attn_out
    normed = (
        hidden * lax.rsqrt(jnp.mean(hidden * hidden, axis=-1, keepdims=True) + 1e-06) * norm_gain
    ).astype(BF16)
    slot_index = slot_places(route_ids, EXPERTS, CAP)
    slot_range = jnp.arange(slot_count, dtype=jnp.int32)
    slot_hits = jnp.sum(
        (slot_index[:, :, None] == slot_range[None, None, :]).astype(BF16), axis=1
    )
    buffer = jnp.einsum("rj,rd->jd", slot_hits, normed, preferred_element_type=F32).astype(BF16)
    buffer = buffer.reshape(groups, per_group, CAP, model_width)
    arrived = lax.all_to_all(buffer, "expert", split_axis=0, concat_axis=0, tiled=True)
    gate_acc = jnp.einsum("gxcd,xdf->gxcf", arrived, w_gate, preferred_element_type=F32)
    upper = jnp.einsum("gxcd,xdf->gxcf", arrived, w_up, preferred_element_type=F32)
    activation = (jax.nn.silu(gate_acc) * upper).astype(BF16)
    product_term = jnp.einsum("gxcf,xfd->gxcd", activation, w_down, preferred_element_type=F32)
    product_term = product_term.astype(BF16).reshape(groups, per_group, CAP, members, block_cols)
    expert_out = lax.psum_scatter(
        jnp.transpose(product_term, (3, 0, 1, 2, 4)), "tensor", scatter_dimension=0, tiled=True
    )[0]
    returned = lax.all_to_all(expert_out, "expert", split_axis=0, concat_axis=0, tiled=True)
    weights = route_weights / jnp.sum(route_weights, axis=-1, keepdims=True)
    picked = returned.reshape(slot_count, block_cols)[slot_index]
    mixture = jnp.sum(weights[:, :, None] * picked.astype(F32), axis=1)
    own_hidden = lax.dynamic_slice_in_dim(hidden, member * block_cols, block_cols, 1)
    return (own_hidden + mixture).astype(BF16)


def hits_of(slot_row, rows):
    places = lax.broadcasted_iota(jnp.int32, (rows, slot_row.shape[1]), 0)
    return places == slot_row


def gate_up_kernel(
    experts, rows, width, slot_ref, weight_ref, x_ref, invgain_ref, wg_ref, wu_ref, act_ref,
    xs_ref, acc_ref, sq_ref, scale_ref
):
    chunk, expert = pl.program_id(0), pl.program_id(1)
    blocks, tokens, lanes = x_ref.shape
    span = PAIR * 128
    parts = tokens // span

    @pl.when(expert == 0)
    def _():
        @pl.when(chunk == 0)
        def _():
            sq_ref[...] = jnp.zeros_like(sq_ref)

        for part in range(parts):
            window = slice(part * span, (part + 1) * span)
            hits = jnp.concatenate(
                [hits_of(slot_ref[e : e + 1, window], rows) for e in range(experts)], axis=0
            )
            pieces = [x_ref[b, window, :] for b in range(blocks)]
            total = sq_ref[window, :]
            for b in range(blocks):
                value = pieces[b].astype(F32) * invgain_ref[b : b + 1, :]
                total = total + value * value
            sq_ref[window, :] = total
            picked = jnp.dot(
                hits.astype(F32).astype(BF16),
                jnp.concatenate(pieces, axis=1),
                preferred_element_type=F32,
            ).astype(BF16)
            for e in range(experts):
                xs_ref[e, part * rows : (part + 1) * rows, :] = picked[e * rows : (e + 1) * rows, :]

    @pl.when((expert == 0) & (chunk == pl.num_programs(0) - 1))
    def _():
        total = jnp.sum(jnp.transpose(sq_ref[...]), axis=0, keepdims=True)
        scale_ref[...] = jnp.broadcast_to(lax.rsqrt(total / width + 1e-06), scale_ref.shape)

    both = jnp.dot(
        xs_ref[expert],
        jnp.concatenate([wg_ref[0], wu_ref[0]], axis=1),
        preferred_element_type=F32,
    )

    @pl.when(chunk == 0)
    def _():
        acc_ref[expert] = both

    @pl.when(chunk > 0)
    def _():
        acc_ref[expert] += both

    @pl.when(chunk == pl.num_programs(0) - 1)
    def _():
        hidden_units = wg_ref.shape[2]
        for part in range(parts):
            window = slice(part * span, (part + 1) * span)
            hits = hits_of(slot_ref[pl.ds(expert, 1), window], rows)
            scale = jnp.sum(
                jnp.where(hits, scale_ref[0:1, window], 0.0), axis=1, keepdims=True
            )
            weight = jnp.sum(
                jnp.where(hits, weight_ref[pl.ds(expert, 1), window], 0.0), axis=1, keepdims=True
            )
            both_part = acc_ref[expert, part * rows : (part + 1) * rows, :]
            gate = both_part[:, :hidden_units] * scale
            upper = both_part[:, hidden_units:] * scale
            act = gate / (1.0 + jnp.exp(-gate)) * upper * weight
            act_ref[expert, part * rows : (part + 1) * rows, :] = act.astype(BF16)


def gate_up(slots, weights, x, invgain, w_gate, w_up, rows, per_chunk):
    experts, width, hidden_units = w_gate.shape
    blocks, tokens, lanes = x.shape
    parts = tokens // (PAIR * 128)
    depth = per_chunk * lanes
    return pl.pallas_call(
        functools.partial(gate_up_kernel, experts, rows, width),
        grid=(blocks // per_chunk, experts),
        in_specs=[
            pl.BlockSpec((experts, tokens), lambda k, e: (0, 0)),
            pl.BlockSpec((experts, tokens), lambda k, e: (0, 0)),
            pl.BlockSpec((per_chunk, tokens, lanes), lambda k, e: (k, 0, 0)),
            pl.BlockSpec((per_chunk, lanes), lambda k, e: (k, 0)),
            pl.BlockSpec((1, depth, hidden_units), lambda k, e: (e, k, 0)),
            pl.BlockSpec((1, depth, hidden_units), lambda k, e: (e, k, 0)),
        ],
        out_specs=pl.BlockSpec((experts, parts * rows, hidden_units), lambda k, e: (0, 0, 0)),
        out_shape=jax.ShapeDtypeStruct((experts, parts * rows, hidden_units), BF16),
        scratch_shapes=[
            pltpu.VMEM((experts, parts * rows, depth), BF16),
            pltpu.VMEM((experts, parts * rows, 2 * hidden_units), F32),
            pltpu.VMEM((tokens, lanes), F32),
            pltpu.VMEM((8, tokens), F32),
        ],
        compiler_params=pltpu.CompilerParams(
            vmem_limit_bytes=VMEM_BYTES, dimension_semantics=("arbitrary", "arbitrary")
        ),
        cost_estimate=pl.CostEstimate(
            flops=2 * experts * parts * rows * width * 2 * hidden_units,
            bytes_accessed=4 * experts * width * hidden_units + 2 * x.size,
            transcendentals=0,
        ),
        name="gate_up",
    )(slots, weights, x, invgain, w_gate, w_up)


def down_kernel(rows, slot_ref, act_ref, wd_ref, out_ref, ys_ref):
    expert = pl.program_id(1)
    experts, all_rows, _ = act_ref.shape
    parts = all_rows // rows
    span = PAIR * 128
    result = jnp.dot(act_ref[expert], wd_ref[0], preferred_element_type=F32).astype(BF16)
    for part in range(parts):
        ys_ref[part, expert] = result[part * rows : (part + 1) * rows, :]

    @pl.when(expert == experts - 1)
    def _():
        for part in range(parts):
            window = slice(part * span, (part + 1) * span)
            hits = jnp.concatenate(
                [hits_of(slot_ref[e : e + 1, window], rows) for e in range(experts)], axis=0
            )
            spread = jnp.transpose(hits.astype(F32)).astype(BF16)
            picked = ys_ref[part].reshape(experts * rows, ys_ref.shape[3])
            mixed = jnp.dot(spread, picked, preferred_element_type=F32).astype(BF16)
            for i in range(PAIR):
                out_ref[part * PAIR + i, 0] = mixed[i * 128 : (i + 1) * 128, :]


def down(slots, act, w_down, rows, groups, members):
    experts, hidden_units, width = w_down.shape
    tokens = slots.shape[1]
    cols = width // members
    parts = act.shape[1] // rows
    return pl.pallas_call(
        functools.partial(down_kernel, rows),
        grid=(members, experts),
        in_specs=[
            pl.BlockSpec((experts, tokens), lambda c, e: (0, 0)),
            pl.BlockSpec(act.shape, lambda c, e: (0, 0, 0)),
            pl.BlockSpec((1, hidden_units, cols), lambda c, e: (e, 0, c)),
        ],
        out_specs=pl.BlockSpec((groups, 1, tokens // groups, cols), lambda c, e: (0, c, 0, 0)),
        out_shape=jax.ShapeDtypeStruct((groups, members, tokens // groups, cols), BF16),
        scratch_shapes=[pltpu.VMEM((parts, experts, rows, cols), BF16)],
        compiler_params=pltpu.CompilerParams(
            vmem_limit_bytes=VMEM_BYTES, dimension_semantics=("arbitrary", "arbitrary")
        ),
        cost_estimate=pl.CostEstimate(
            flops=2 * experts * parts * rows * width * hidden_units,
            bytes_accessed=2 * experts * width * hidden_units + 2 * tokens * width,
            transcendentals=0,
        ),
        name="down_mix",
    )(slots, act, w_down)


def route_tables(route_ids, route_weights, group, experts):
    rows_here = route_ids.shape[0]
    shares = route_weights / jnp.sum(route_weights, axis=-1, keepdims=True)
    ids = lax.all_gather(route_ids, "expert", axis=0, tiled=True)
    shares = lax.all_gather(shares, "expert", axis=0, tiled=True)
    tokens = ids.shape[0]
    own = group * experts + jnp.arange(experts, dtype=jnp.int32)
    match = ids.T[None, :, :] == own[:, None, None]
    named = jnp.any(match, axis=1)
    weights = jnp.sum(jnp.where(match, shares.T[None, :, :], 0.0), axis=1)
    span = PAIR * rows_here
    order = jnp.arange(span)
    earlier = (order[:, None] < order[None, :]).astype(BF16)
    rank = jnp.dot(
        named.astype(BF16).reshape(experts * tokens // span, span),
        earlier,
        preferred_element_type=F32,
    )
    slots = jnp.where(named, rank.reshape(experts, tokens).astype(jnp.int32), -1)
    return slots, weights


def per_device_tokens(
    attn_heads, out_proj, residual, norm_gain, route_ids, route_weights, w_gate, w_up, w_down
):
    groups, members = lax.axis_size("expert"), lax.axis_size("tensor")
    group, member = lax.axis_index("expert"), lax.axis_index("tensor")
    here, width = residual.shape
    experts = w_gate.shape[0]
    tokens = groups * here
    lanes = width // (groups * members)
    rows = -(-PAIR * CAP // 16) * 16

    slots, weights = route_tables(route_ids, route_weights, group, experts)

    own_cols = lax.dynamic_index_in_dim(
        residual.reshape(here, groups, members, lanes), member, 2, keepdims=False
    )
    moved = lax.all_to_all(
        jnp.transpose(own_cols, (1, 0, 2)), "expert", split_axis=0, concat_axis=0, tiled=True
    ).reshape(tokens, lanes)

    heads = lax.all_gather(attn_heads, "expert", axis=0, tiled=True)
    part = jnp.dot(heads, out_proj, preferred_element_type=F32).astype(BF16)
    part = jnp.transpose(part.reshape(tokens, members, lanes), (1, 0, 2))
    attn_out = lax.psum_scatter(part, "tensor", scatter_dimension=0, tiled=True)[0]
    hidden = moved.astype(F32) + attn_out.astype(F32)
    gain = lax.dynamic_index_in_dim(
        norm_gain.reshape(groups * members, lanes), group * members + member, 0, keepdims=True
    )
    x = lax.all_gather((hidden * gain).astype(BF16), ("expert", "tensor"), axis=0)

    invgain = (1.0 / norm_gain).reshape(groups * members, lanes)
    act = gate_up(slots, weights, x, invgain, w_gate, w_up, rows, per_chunk=8)
    mixed = down(slots, act, w_down, rows, groups, members)
    cols = width // members
    mixture = lax.psum_scatter(
        mixed.reshape(groups * members, here, cols),
        ("expert", "tensor"),
        scatter_dimension=0,
        tiled=True,
    )[0]
    per_member = groups
    own = lax.dynamic_slice(
        x, (member * per_member, group * here, 0), (per_member, here, lanes)
    ).astype(F32)
    own_invgain = lax.dynamic_slice(invgain, (member * per_member, 0), (per_member, lanes))
    own_hidden = jnp.transpose(own * own_invgain[:, None, :], (1, 0, 2)).reshape(here, cols)
    return (own_hidden + mixture.astype(F32)).astype(BF16)


def solution(mesh):
    groups, members = mesh.shape["expert"], mesh.shape["tensor"]
    placed = (
        P("expert", "tensor"),
        P("tensor", "expert"),
        P("expert", None),
        P(),
        P("expert", None),
        P("expert", None),
        P("expert", None, "tensor"),
        P("expert", None, "tensor"),
        P("expert", "tensor", None),
    )

    def run(*arrays):
        tokens, width = arrays[2].shape
        whole_tokens = tokens <= EXPERTS * CAP and width == groups * members * LANES
        body = per_device_tokens if whole_tokens else per_device_slots
        return jax.shard_map(
            body, mesh=mesh, in_specs=placed, out_specs=P("expert", "tensor"), check_vma=False
        )(*arrays)

    return run
```

```python
import functools

import jax
import jax.numpy as jnp
from jax import lax
from jax.experimental import pallas as pl
from jax.experimental.pallas import tpu as pltpu
from jax.sharding import PartitionSpec as P

EXPERTS = 64
CAP = 18
BF16 = jnp.bfloat16
F32 = jnp.float32
PAIR = 2
LANES = 128
VMEM_BYTES = 56 * 1024 * 1024


def slot_places(ids, experts, capacity):
    row_count, top_count = ids.shape
    onehot = (ids[:, :, None] == jnp.arange(experts, dtype=jnp.int32)[None, None, :]).astype(
        jnp.int32
    )
    flattened = onehot.reshape(row_count * top_count, experts)
    before = jnp.cumsum(flattened, axis=0) - flattened
    slot_rank = jnp.sum(before * flattened, axis=1).reshape(row_count, top_count)
    return ids * capacity + slot_rank


def per_device_slots(
    attn_heads, out_proj, residual, norm_gain, route_ids, route_weights, w_gate, w_up, w_down
):
    model_width = residual.shape[1]
    groups = lax.axis_size("expert")
    members = lax.axis_size("tensor")
    member = lax.axis_index("tensor")
    per_group = w_gate.shape[0]
    slot_count = EXPERTS * CAP
    block_cols = model_width // members
    heads_out = jnp.dot(
        attn_heads,
        lax.all_gather(out_proj, "expert", axis=1, tiled=True),
        preferred_element_type=F32,
    )
    attn_out = lax.psum(heads_out.astype(BF16), "tensor").astype(F32)
    hidden = residual.astype(F32) + attn_out
    normed = (
        hidden * lax.rsqrt(jnp.mean(hidden * hidden, axis=-1, keepdims=True) + 1e-06) * norm_gain
    ).astype(BF16)
    slot_index = slot_places(route_ids, EXPERTS, CAP)
    slot_range = jnp.arange(slot_count, dtype=jnp.int32)
    slot_hits = jnp.sum(
        (slot_index[:, :, None] == slot_range[None, None, :]).astype(BF16), axis=1
    )
    buffer = jnp.einsum("rj,rd->jd", slot_hits, normed, preferred_element_type=F32).astype(BF16)
    buffer = buffer.reshape(groups, per_group, CAP, model_width)
    arrived = lax.all_to_all(buffer, "expert", split_axis=0, concat_axis=0, tiled=True)
    gate_acc = jnp.einsum("gxcd,xdf->gxcf", arrived, w_gate, preferred_element_type=F32)
    upper = jnp.einsum("gxcd,xdf->gxcf", arrived, w_up, preferred_element_type=F32)
    activation = (jax.nn.silu(gate_acc) * upper).astype(BF16)
    product_term = jnp.einsum("gxcf,xfd->gxcd", activation, w_down, preferred_element_type=F32)
    product_term = product_term.astype(BF16).reshape(groups, per_group, CAP, members, block_cols)
    expert_out = lax.psum_scatter(
        jnp.transpose(product_term, (3, 0, 1, 2, 4)), "tensor", scatter_dimension=0, tiled=True
    )[0]
    returned = lax.all_to_all(expert_out, "expert", split_axis=0, concat_axis=0, tiled=True)
    weights = route_weights / jnp.sum(route_weights, axis=-1, keepdims=True)
    picked = returned.reshape(slot_count, block_cols)[slot_index]
    mixture = jnp.sum(weights[:, :, None] * picked.astype(F32), axis=1)
    own_hidden = lax.dynamic_slice_in_dim(hidden, member * block_cols, block_cols, 1)
    return (own_hidden + mixture).astype(BF16)


def hits_of(slot_row, rows):
    places = lax.broadcasted_iota(jnp.int32, (rows, slot_row.shape[1]), 0)
    return places == slot_row


def gate_up_kernel(
    experts, rows, width, slot_ref, weight_ref, x_ref, invgain_ref, wg_ref, wu_ref, act_ref,
    xs_ref, acc_ref, sq_ref, scale_ref
):
    chunk, expert = pl.program_id(0), pl.program_id(1)
    blocks, tokens, lanes = x_ref.shape
    span = PAIR * 128
    parts = tokens // span

    @pl.when(expert == 0)
    def _():
        @pl.when(chunk == 0)
        def _():
            sq_ref[...] = jnp.zeros_like(sq_ref)

        for part in range(parts):
            window = slice(part * span, (part + 1) * span)
            hits = jnp.concatenate(
                [hits_of(slot_ref[e : e + 1, window], rows) for e in range(experts)], axis=0
            )
            pieces = [x_ref[b, window, :] for b in range(blocks)]
            total = sq_ref[window, :]
            for b in range(blocks):
                value = pieces[b].astype(F32) * invgain_ref[b : b + 1, :]
                total = total + value * value
            sq_ref[window, :] = total
            picked = jnp.dot(
                hits.astype(F32).astype(BF16),
                jnp.concatenate(pieces, axis=1),
                preferred_element_type=F32,
            ).astype(BF16)
            for e in range(experts):
                xs_ref[e, part * rows : (part + 1) * rows, :] = picked[e * rows : (e + 1) * rows, :]

    @pl.when((expert == 0) & (chunk == pl.num_programs(0) - 1))
    def _():
        total = jnp.sum(jnp.transpose(sq_ref[...]), axis=0, keepdims=True)
        scale_ref[...] = jnp.broadcast_to(lax.rsqrt(total / width + 1e-06), scale_ref.shape)

    both = jnp.dot(
        xs_ref[expert],
        jnp.concatenate([wg_ref[0], wu_ref[0]], axis=1),
        preferred_element_type=F32,
    )

    @pl.when(chunk == 0)
    def _():
        acc_ref[expert] = both

    @pl.when(chunk > 0)
    def _():
        acc_ref[expert] += both

    @pl.when(chunk == pl.num_programs(0) - 1)
    def _():
        hidden_units = wg_ref.shape[2]
        for part in range(parts):
            window = slice(part * span, (part + 1) * span)
            hits = hits_of(slot_ref[pl.ds(expert, 1), window], rows)
            scale = jnp.sum(
                jnp.where(hits, scale_ref[0:1, window], 0.0), axis=1, keepdims=True
            )
            weight = jnp.sum(
                jnp.where(hits, weight_ref[pl.ds(expert, 1), window], 0.0), axis=1, keepdims=True
            )
            both_part = acc_ref[expert, part * rows : (part + 1) * rows, :]
            gate = both_part[:, :hidden_units] * scale
            upper = both_part[:, hidden_units:] * scale
            act = gate / (1.0 + jnp.exp(-gate)) * upper * weight
            act_ref[expert, part * rows : (part + 1) * rows, :] = act.astype(BF16)


def gate_up(slots, weights, x, invgain, w_gate, w_up, rows, per_chunk):
    experts, width, hidden_units = w_gate.shape
    blocks, tokens, lanes = x.shape
    parts = tokens // (PAIR * 128)
    depth = per_chunk * lanes
    return pl.pallas_call(
        functools.partial(gate_up_kernel, experts, rows, width),
        grid=(blocks // per_chunk, experts),
        in_specs=[
            pl.BlockSpec((experts, tokens), lambda k, e: (0, 0)),
            pl.BlockSpec((experts, tokens), lambda k, e: (0, 0)),
            pl.BlockSpec((per_chunk, tokens, lanes), lambda k, e: (k, 0, 0)),
            pl.BlockSpec((per_chunk, lanes), lambda k, e: (k, 0)),
            pl.BlockSpec(
                (1, depth, hidden_units), lambda k, e: (e, k, 0)
            ),
            pl.BlockSpec(
                (1, depth, hidden_units), lambda k, e: (e, k, 0)
            ),
        ],
        out_specs=pl.BlockSpec((experts, parts * rows, hidden_units), lambda k, e: (0, 0, 0)),
        out_shape=jax.ShapeDtypeStruct((experts, parts * rows, hidden_units), BF16),
        scratch_shapes=[
            pltpu.VMEM((experts, parts * rows, depth), BF16),
            pltpu.VMEM((experts, parts * rows, 2 * hidden_units), F32),
            pltpu.VMEM((tokens, lanes), F32),
            pltpu.VMEM((8, tokens), F32),
        ],
        compiler_params=pltpu.CompilerParams(
            vmem_limit_bytes=VMEM_BYTES, dimension_semantics=("arbitrary", "arbitrary")
        ),
        cost_estimate=pl.CostEstimate(
            flops=2 * experts * parts * rows * width * 2 * hidden_units,
            bytes_accessed=4 * experts * width * hidden_units + 2 * x.size,
            transcendentals=0,
        ),
        name="gate_up",
    )(slots, weights, x, invgain, w_gate, w_up)


def down_kernel(rows, place_ref, slot_ref, act_ref, wd0_ref, wd1_ref, *rest):
    out_refs, ys_ref = rest[:-1], rest[-1]
    out_cols = out_refs[0].shape[2]
    expert = pl.program_id(0)
    experts, all_rows, _ = act_ref.shape
    parts = all_rows // rows
    groups = parts * PAIR
    span = PAIR * 128
    for side, wd_ref in enumerate((wd0_ref, wd1_ref)):
        result = jnp.dot(act_ref[expert], wd_ref[0], preferred_element_type=F32).astype(BF16)
        for part in range(parts):
            ys_ref[side, part, expert] = result[part * rows : (part + 1) * rows, :]

    @pl.when(expert == experts - 1)
    def _():
        for part in range(parts):
            window = slice(part * span, (part + 1) * span)
            hits = jnp.concatenate(
                [hits_of(slot_ref[e : e + 1, window], rows) for e in range(experts)], axis=0
            )
            spread = jnp.transpose(hits.astype(F32)).astype(BF16)
            for side in range(2):
                picked = ys_ref[side, part].reshape(experts * rows, ys_ref.shape[4])
                mixed = jnp.dot(spread, picked, preferred_element_type=F32).astype(BF16)
                for i in range(PAIR):
                    target = place_ref[2 + side * groups + part * PAIR + i]
                    for number, out_ref in enumerate(out_refs):
                        out_ref[target] = mixed[
                            i * 128 : (i + 1) * 128, number * out_cols : (number + 1) * out_cols
                        ]


def down(place, slots, act, w_down, rows, groups, cols, chunks):
    experts, hidden_units, width = w_down.shape
    tokens = slots.shape[1]
    parts = act.shape[1] // rows
    return pl.pallas_call(
        functools.partial(down_kernel, rows),
        grid_spec=pltpu.PrefetchScalarGridSpec(
            num_scalar_prefetch=1,
            grid=(experts,),
            in_specs=[
                pl.BlockSpec((experts, tokens), lambda e, p: (0, 0)),
                pl.BlockSpec(act.shape, lambda e, p: (0, 0, 0)),
                pl.BlockSpec(
                    (1, hidden_units, cols),
                    lambda e, p: (e, 0, p[0])
                ),
                pl.BlockSpec(
                    (1, hidden_units, cols),
                    lambda e, p: (e, 0, p[1])
                ),
            ],
            out_specs=[
                pl.BlockSpec((2 * groups, tokens // groups, cols // chunks), lambda e, p: (0, 0, 0))
            ]
            * chunks,
            scratch_shapes=[pltpu.VMEM((2, parts, experts, rows, cols), BF16)],
        ),
        out_shape=[jax.ShapeDtypeStruct((2 * groups, tokens // groups, cols // chunks), BF16)]
        * chunks,
        compiler_params=pltpu.CompilerParams(
            vmem_limit_bytes=VMEM_BYTES, dimension_semantics=("arbitrary",)
        ),
        cost_estimate=pl.CostEstimate(
            flops=8 * experts * parts * rows * cols * hidden_units,
            bytes_accessed=4 * experts * cols * hidden_units + 4 * tokens * cols,
            transcendentals=0,
        ),
        name="down_mix",
    )(place, slots, act, w_down, w_down)


def flip(array, bits_of):
    pairs = []
    for index in range(32):
        pairs.append((index, index ^ bits_of(index & 1)))
    return lax.ppermute(array, ("expert", "tensor"), pairs)


CORE, X, Y, ZLOW, ZHIGH = 1, 2, 4, 8, 16


def first_axis(core):
    return Y if core else X


def last_axis(core):
    return X if core else Y


def halving_places(to_core, group, member, groups):
    g = jnp.arange(groups, dtype=jnp.int32)[None, :]
    y_kept = ((g & 1) == (group & 1)).astype(jnp.int32)
    low_kept = (((g >> 1) & 1) == ((group >> 1) & 1)).astype(jnp.int32)
    high_kept = ((g >> 2) == (group >> 2)).astype(jnp.int32)
    x_kept = jnp.arange(2, dtype=jnp.int32)[:, None]
    first = jnp.where(to_core == 0, x_kept, y_kept)
    last = jnp.where(to_core == 0, y_kept, x_kept)
    return (((first * 2 + low_kept) * 2 + high_kept) * 2 + last).reshape(-1)


def total_of(terms):
    total = terms[0].astype(F32)
    for term in terms[1:]:
        total = total + term.astype(F32)
    return total


HALVING = (first_axis, lambda core: ZLOW, lambda core: ZHIGH, last_axis)


def after(value, earlier):
    return lax.optimization_barrier((value, earlier))


def sent_half(terms):
    half = terms[0].shape[0] // 2
    return total_of([term[:half] for term in terms]).astype(BF16), [term[half:] for term in terms]


def reduce_chunks(makers):
    chunks, arrived, first_sent = [None] * len(makers), {}, None
    for tick in range(len(HALVING) + len(makers) - 1):
        for index, maker in enumerate(makers):
            stage = tick - index
            if not 0 <= stage < len(HALVING):
                continue
            if stage == 0:
                chunks[index] = maker(first_sent)
            sent, rest = sent_half(chunks[index])
            if index:
                sent, _ = after(sent, arrived[index - 1, stage])
            if stage == 0:
                first_sent = sent
            came = flip(sent, HALVING[stage])
            arrived[index, stage] = came
            chunks[index] = rest + [came]
    return [total_of([term[0] for term in terms]) for terms in chunks]


def route_tables(route_ids, route_weights, group, experts):
    rows_here = route_ids.shape[0]
    shares = route_weights / jnp.sum(route_weights, axis=-1, keepdims=True)
    table = jnp.concatenate([route_ids.astype(F32), shares], axis=1)
    table = lax.all_gather(table, "expert", axis=0, tiled=True)
    ids = table[:, : route_ids.shape[1]].astype(jnp.int32)
    shares = table[:, route_ids.shape[1] :]
    tokens = ids.shape[0]
    own = group * experts + jnp.arange(experts, dtype=jnp.int32)
    match = ids.T[None, :, :] == own[:, None, None]
    named = jnp.any(match, axis=1)
    weights = jnp.sum(jnp.where(match, shares.T[None, :, :], 0.0), axis=1)
    span = PAIR * rows_here
    order = jnp.arange(span)
    earlier = (order[:, None] < order[None, :]).astype(BF16)
    rank = jnp.dot(
        named.astype(BF16).reshape(experts * tokens // span, span),
        earlier,
        preferred_element_type=F32,
    )
    slots = jnp.where(named, rank.reshape(experts, tokens).astype(jnp.int32), -1)
    return slots, weights


def per_device_tokens(
    attn_heads, out_proj, residual, norm_gain, route_ids, route_weights, w_gate, w_up, w_down
):
    groups, members = lax.axis_size("expert"), lax.axis_size("tensor")
    group, member = lax.axis_index("expert"), lax.axis_index("tensor")
    here, width = residual.shape
    experts = w_gate.shape[0]
    tokens = groups * here
    lanes = width // (groups * members)
    rows = -(-PAIR * CAP // 16) * 16

    slots, weights = route_tables(route_ids, route_weights, group, experts)

    own_cols = lax.dynamic_index_in_dim(
        residual.reshape(here, groups, members, lanes), member, 2, keepdims=False
    )
    moved = lax.all_to_all(
        jnp.transpose(own_cols, (1, 0, 2)), "expert", split_axis=0, concat_axis=0, tiled=True
    ).reshape(tokens, lanes)

    heads = lax.all_gather(attn_heads, "expert", axis=0, tiled=True)
    part = jnp.dot(heads, out_proj, preferred_element_type=F32).astype(BF16)
    part = jnp.transpose(part.reshape(tokens, members, lanes), (1, 0, 2))
    part, slots, weights = lax.optimization_barrier((part, slots, weights))
    attn_out = lax.psum_scatter(part, "tensor", scatter_dimension=0, tiled=True)[0]
    hidden = moved.astype(F32) + attn_out.astype(F32)
    gain = lax.dynamic_index_in_dim(
        norm_gain.reshape(groups * members, lanes), group * members + member, 0, keepdims=True
    )
    x = lax.all_gather((hidden * gain).astype(BF16), ("expert", "tensor"), axis=0)

    invgain = (1.0 / norm_gain).reshape(groups * members, lanes)
    act = gate_up(slots, weights, x, invgain, w_gate, w_up, rows, per_chunk=16)
    cols = width // members
    x_side, core = member >> 1, member & 1

    def columns_of(to_core, chunk, chunks):
        sides = jnp.stack([1 - x_side, x_side])
        blocks = (sides * 2 + to_core) * chunks + chunk
        return jnp.concatenate([blocks, halving_places(to_core, group, member, groups)])

    chunks = 2
    chunk_cols = cols // chunks
    other = down(
        columns_of(1 - core, 0, 1), slots, act, w_down, rows, groups, cols, chunks
    )
    came = [flip(piece, lambda c: CORE) for piece in other]

    def terms_of(chunk, earlier):
        ready = act if earlier is None else after(act, earlier)[0]
        place = columns_of(core, chunk, chunks)
        (kept,) = down(place, slots, ready, w_down, rows, groups, chunk_cols, 1)
        return [kept, came[chunk]]

    sums = reduce_chunks([functools.partial(terms_of, chunk) for chunk in range(chunks)])
    mixture = jnp.concatenate(sums, axis=1)
    per_member = groups
    own = lax.dynamic_slice(
        x, (member * per_member, group * here, 0), (per_member, here, lanes)
    ).astype(F32)
    own_invgain = lax.dynamic_slice(invgain, (member * per_member, 0), (per_member, lanes))
    own_hidden = jnp.transpose(own * own_invgain[:, None, :], (1, 0, 2)).reshape(here, cols)
    return (own_hidden + mixture).astype(BF16)


def solution(mesh):
    groups, members = mesh.shape["expert"], mesh.shape["tensor"]
    placed = (
        P("expert", "tensor"),
        P("tensor", "expert"),
        P("expert", None),
        P(),
        P("expert", None),
        P("expert", None),
        P("expert", None, "tensor"),
        P("expert", None, "tensor"),
        P("expert", "tensor", None),
    )

    def run(*arrays):
        tokens, width = arrays[2].shape
        whole_tokens = (groups, members) == (8, 4) and width == groups * members * LANES
        body = per_device_tokens if whole_tokens else per_device_slots
        return jax.shard_map(
            body, mesh=mesh, in_specs=placed, out_specs=P("expert", "tensor"), check_vma=False
        )(*arrays)

    return run
```

```python
import functools

import jax
import jax.numpy as jnp
from jax import lax
from jax.experimental import pallas as pl
from jax.experimental.pallas import tpu as pltpu
from jax.sharding import PartitionSpec as P

EXPERTS = 64
CAP = 18
BF16 = jnp.bfloat16
F32 = jnp.float32
PAIR = 2
LANES = 128
HEAD_ORDER = (0, 2, 1, 3)


def slot_places(ids, experts, capacity):
    row_count, top_count = ids.shape
    onehot = (ids[:, :, None] == jnp.arange(experts, dtype=jnp.int32)[None, None, :]).astype(
        jnp.int32
    )
    flattened = onehot.reshape(row_count * top_count, experts)
    before = jnp.cumsum(flattened, axis=0) - flattened
    slot_rank = jnp.sum(before * flattened, axis=1).reshape(row_count, top_count)
    return ids * capacity + slot_rank


def per_device_slots(
    attn_heads, out_proj, residual, norm_gain, route_ids, route_weights, w_gate, w_up, w_down
):
    model_width = residual.shape[1]
    groups = lax.axis_size("expert")
    members = lax.axis_size("tensor")
    member = lax.axis_index("tensor")
    per_group = w_gate.shape[0]
    slot_count = EXPERTS * CAP
    block_cols = model_width // members
    heads_out = jnp.dot(
        attn_heads,
        lax.all_gather(out_proj, "expert", axis=1, tiled=True),
        preferred_element_type=F32,
    )
    attn_out = lax.psum(heads_out.astype(BF16), "tensor").astype(F32)
    hidden = residual.astype(F32) + attn_out
    normed = (
        hidden * lax.rsqrt(jnp.mean(hidden * hidden, axis=-1, keepdims=True) + 1e-06) * norm_gain
    ).astype(BF16)
    slot_index = slot_places(route_ids, EXPERTS, CAP)
    slot_range = jnp.arange(slot_count, dtype=jnp.int32)
    slot_hits = jnp.sum(
        (slot_index[:, :, None] == slot_range[None, None, :]).astype(BF16), axis=1
    )
    buffer = jnp.einsum("rj,rd->jd", slot_hits, normed, preferred_element_type=F32).astype(BF16)
    buffer = buffer.reshape(groups, per_group, CAP, model_width)
    arrived = lax.all_to_all(buffer, "expert", split_axis=0, concat_axis=0, tiled=True)
    gate_acc = jnp.einsum("gxcd,xdf->gxcf", arrived, w_gate, preferred_element_type=F32)
    upper = jnp.einsum("gxcd,xdf->gxcf", arrived, w_up, preferred_element_type=F32)
    activation = (jax.nn.silu(gate_acc) * upper).astype(BF16)
    product_term = jnp.einsum("gxcf,xfd->gxcd", activation, w_down, preferred_element_type=F32)
    product_term = product_term.astype(BF16).reshape(groups, per_group, CAP, members, block_cols)
    expert_out = lax.psum_scatter(
        jnp.transpose(product_term, (3, 0, 1, 2, 4)), "tensor", scatter_dimension=0, tiled=True
    )[0]
    returned = lax.all_to_all(expert_out, "expert", split_axis=0, concat_axis=0, tiled=True)
    weights = route_weights / jnp.sum(route_weights, axis=-1, keepdims=True)
    picked = returned.reshape(slot_count, block_cols)[slot_index]
    mixture = jnp.sum(weights[:, :, None] * picked.astype(F32), axis=1)
    own_hidden = lax.dynamic_slice_in_dim(hidden, member * block_cols, block_cols, 1)
    return (own_hidden + mixture).astype(BF16)


def hits_of(slot_row, rows):
    places = lax.broadcasted_iota(jnp.int32, (rows, slot_row.shape[1]), 0)
    return places == slot_row


def project_kernel(member_ref, head_refs, weight_ref, send_ref, keep_ref):
    core, x_side, z = member_ref[0], member_ref[1], member_ref[2]
    result = jnp.dot(
        jnp.concatenate([ref[...] for ref in head_refs], axis=0),
        weight_ref[...],
        preferred_element_type=F32,
    ).astype(BF16)
    here = head_refs[0].shape[0]
    for to_x in range(2):
        x_kept = (x_side == to_x).astype(jnp.int32)
        for to_core in range(2):
            start = (to_x * 2 + to_core) * LANES
            for out_ref, wanted in ((keep_ref, core == to_core), (send_ref, core != to_core)):

                @pl.when(wanted)
                def _(out_ref=out_ref, x_kept=x_kept, start=start):
                    for piece, z_bits in enumerate(HEAD_ORDER):
                        out_ref[x_kept, z ^ z_bits] = result[
                            piece * here : (piece + 1) * here, start : start + LANES
                        ]


def project(member_info, pieces, out_proj):
    here = pieces[0].shape[0]
    out = jax.ShapeDtypeStruct((2, len(pieces), here, LANES), BF16)
    vmem = pl.BlockSpec(memory_space=pltpu.VMEM)

    def kernel(member_ref, *refs):
        project_kernel(member_ref, refs[:4], refs[4], refs[5], refs[6])

    return pl.pallas_call(
        kernel,
        in_specs=[pl.BlockSpec(memory_space=pltpu.SMEM)] + [vmem] * 5,
        out_specs=[vmem, vmem],
        out_shape=[out, out],
        compiler_params=pltpu.CompilerParams(vmem_limit_bytes=24 * 1024 * 1024),
        cost_estimate=pl.CostEstimate(
            flops=2 * 4 * here * out_proj.size,
            bytes_accessed=2 * (out_proj.size + 5 * pieces[0].size),
            transcendentals=0,
        ),
        name="project",
    )(member_info, *pieces, out_proj)


def gate_up_kernel(
    experts, rows, width, info_ref, slot_ref, weight_ref, invgain_ref, x_refs, wg_ref, wu_ref,
    act_ref, hidden_ref, xs_ref, acc_ref, sq_ref, scale_ref, hits_ref
):
    expert, chunk = pl.program_id(0), pl.program_id(1)
    arrays = len(x_refs) // 2
    each, parts, here, lanes = x_refs[0].shape
    blocks = arrays * each
    span = 2 * here
    member, z = info_ref[2 * blocks], info_ref[2 * blocks + 1]
    depth = wg_ref.shape[1]

    @pl.when((expert == 0) & (chunk == 0))
    def _():
        sq_ref[...] = jnp.zeros_like(sq_ref)
        for part in range(parts):
            for e in range(experts):
                first = hits_of(slot_ref[e : e + 1, part * span : part * span + here], rows)
                second = hits_of(
                    slot_ref[e : e + 1, part * span + here : (part + 1) * span], rows
                )
                first = first.astype(F32).astype(BF16)
                second = second.astype(F32).astype(BF16)
                window = slice(e * rows, (e + 1) * rows)
                hits_ref[0, part, window, :] = jnp.concatenate([first, second], axis=1)
                hits_ref[1, part, window, :] = jnp.concatenate([second, first], axis=1)

        def pair_of_blocks(low, carry):
            for array in range(arrays):
                own, other = x_refs[2 * array], x_refs[2 * array + 1]
                swapped = info_ref[blocks + array * each + low]
                places = (low, low + each // 2)
                features = [info_ref[array * each + place] for place in places]
                for place, feature in zip(places, features):
                    invgain = invgain_ref[pl.ds(feature, 1), :]
                    for part in range(parts):
                        for half, ref in enumerate((own, other)):
                            value = ref[place, part].astype(F32) * invgain
                            sq_ref[swapped, part, half] += value * value

                    @pl.when(feature >> 3 == member)
                    def _(place=place, feature=feature, invgain=invgain):
                        mine = jnp.where(
                            swapped == 0, own[place, z].astype(F32), other[place, z].astype(F32)
                        )
                        column = pl.multiple_of((feature & 7) * lanes, lanes)
                        hidden_ref[:, pl.ds(column, lanes)] = mine * invgain

                for part in range(parts):
                    both = jnp.concatenate(
                        [
                            jnp.concatenate([own[place, part], other[place, part]], axis=0)
                            for place in places
                        ],
                        axis=1,
                    )
                    picked = jnp.dot(
                        hits_ref[swapped, part], both, preferred_element_type=F32
                    ).astype(BF16)
                    for number, feature in enumerate(features):
                        column = pl.multiple_of(feature * lanes, lanes)
                        for e in range(experts):
                            xs_ref[e, part * rows : (part + 1) * rows, pl.ds(column, lanes)] = (
                                picked[
                                    e * rows : (e + 1) * rows, number * lanes : (number + 1) * lanes
                                ]
                            )
            return carry

        lax.fori_loop(0, each // 2, pair_of_blocks, 0)
        pieces = [
            sq_ref[0, part, half] + sq_ref[1, part, 1 - half]
            for part in range(parts)
            for half in range(2)
        ]
        total = jnp.sum(
            jnp.transpose(jnp.concatenate(pieces, axis=0)), axis=0, keepdims=True
        )
        scale_ref[...] = jnp.broadcast_to(lax.rsqrt(total / width + 1e-06), scale_ref.shape)

    both = jnp.dot(
        xs_ref[expert, :, pl.ds(pl.multiple_of(chunk * depth, depth), depth)],
        jnp.concatenate([wg_ref[0], wu_ref[0]], axis=1),
        preferred_element_type=F32,
    )

    @pl.when(chunk == 0)
    def _():
        acc_ref[...] = both

    @pl.when((chunk > 0) & (chunk < pl.num_programs(1) - 1))
    def _():
        acc_ref[...] += both

    @pl.when(chunk == pl.num_programs(1) - 1)
    def _():
        hidden_units = wg_ref.shape[2]
        summed = acc_ref[...] + both
        for part in range(parts):
            window = slice(part * span, (part + 1) * span)
            hits = hits_of(slot_ref[pl.ds(expert, 1), window], rows)
            scale = jnp.sum(
                jnp.where(hits, scale_ref[0:1, window], 0.0), axis=1, keepdims=True
            )
            weight = jnp.sum(
                jnp.where(hits, weight_ref[pl.ds(expert, 1), window], 0.0), axis=1, keepdims=True
            )
            both_part = summed[part * rows : (part + 1) * rows, :]
            gate = both_part[:, :hidden_units] * scale
            upper = both_part[:, hidden_units:] * scale
            act = gate / (1.0 + jnp.exp(-gate)) * upper * weight
            act_ref[expert, part * rows : (part + 1) * rows, :] = act.astype(BF16)


def gate_up(info, slots, weights, invgain, x, w_gate, w_up, rows, chunks):
    experts, width, hidden_units = w_gate.shape
    each, parts, here, lanes = x[0].shape
    tokens = slots.shape[1]
    members = width // (each * lanes)
    depth = width // chunks

    def kernel(info_ref, slot_ref, weight_ref, invgain_ref, *rest):
        gate_up_kernel(
            experts, rows, width, info_ref, slot_ref, weight_ref, invgain_ref,
            rest[: len(x)], *rest[len(x) :]
        )

    def whole(shape):
        return pl.BlockSpec(
            shape, lambda e, k, info: (0,) * len(shape), pipeline_mode=pl.Buffered(1)
        )

    return pl.pallas_call(
        kernel,
        grid_spec=pltpu.PrefetchScalarGridSpec(
            num_scalar_prefetch=1,
            grid=(experts, chunks),
            in_specs=[whole(slots.shape), whole(weights.shape), whole(invgain.shape)]
            + [pl.BlockSpec(memory_space=pltpu.VMEM)] * len(x)
            + [pl.BlockSpec((1, depth, hidden_units), lambda e, k, info: (e, k, 0))] * 2,
            out_specs=[
                pl.BlockSpec((experts, parts * rows, hidden_units), lambda e, k, info: (0, 0, 0)),
                pl.BlockSpec((here, width // members), lambda e, k, info: (0, 0)),
            ],
            scratch_shapes=[
                pltpu.VMEM((experts, parts * rows, width), BF16),
                pltpu.VMEM((parts * rows, 2 * hidden_units), F32),
                pltpu.VMEM((2, parts, 2, here, lanes), F32),
                pltpu.VMEM((8, tokens), F32),
                pltpu.VMEM((2, parts, experts * rows, 2 * here), BF16),
            ],
        ),
        out_shape=[
            jax.ShapeDtypeStruct((experts, parts * rows, hidden_units), BF16),
            jax.ShapeDtypeStruct((here, width // members), F32),
        ],
        compiler_params=pltpu.CompilerParams(
            vmem_limit_bytes=40 * 1024 * 1024, dimension_semantics=("arbitrary", "arbitrary")
        ),
        cost_estimate=pl.CostEstimate(
            flops=2 * experts * parts * rows * width * 2 * hidden_units,
            bytes_accessed=4 * experts * width * hidden_units + 2 * len(x) * x[0].size,
            transcendentals=0,
        ),
        name="gate_up",
    )(info, slots, weights, invgain, *x, w_gate, w_up)


def down_kernel(rows, place_ref, slot_ref, act_ref, wd0_ref, wd1_ref, *rest):
    out_refs, ys_ref = rest[:-1], rest[-1]
    out_cols = out_refs[0].shape[2]
    expert = pl.program_id(0)
    experts, all_rows, _ = act_ref.shape
    parts = all_rows // rows
    groups = parts * PAIR
    span = PAIR * 128
    for side, wd_ref in enumerate((wd0_ref, wd1_ref)):
        result = jnp.dot(act_ref[expert], wd_ref[0], preferred_element_type=F32).astype(BF16)
        for part in range(parts):
            ys_ref[side, part, expert] = result[part * rows : (part + 1) * rows, :]

    @pl.when(expert == experts - 1)
    def _():
        for part in range(parts):
            window = slice(part * span, (part + 1) * span)
            hits = jnp.concatenate(
                [hits_of(slot_ref[e : e + 1, window], rows) for e in range(experts)], axis=0
            )
            spread = jnp.transpose(hits.astype(F32)).astype(BF16)
            for side in range(2):
                picked = ys_ref[side, part].reshape(experts * rows, ys_ref.shape[4])
                mixed = jnp.dot(spread, picked, preferred_element_type=F32).astype(BF16)
                for i in range(PAIR):
                    target = place_ref[2 + side * groups + part * PAIR + i]
                    for number, out_ref in enumerate(out_refs):
                        out_ref[target] = mixed[
                            i * 128 : (i + 1) * 128, number * out_cols : (number + 1) * out_cols
                        ]


def down(place, slots, act, w_down, rows, groups, cols, chunks):
    experts, hidden_units, width = w_down.shape
    tokens = slots.shape[1]
    parts = act.shape[1] // rows
    return pl.pallas_call(
        functools.partial(down_kernel, rows),
        grid_spec=pltpu.PrefetchScalarGridSpec(
            num_scalar_prefetch=1,
            grid=(experts,),
            in_specs=[
                pl.BlockSpec(memory_space=pltpu.VMEM),
                pl.BlockSpec(memory_space=pltpu.VMEM),
                pl.BlockSpec(
                    (1, hidden_units, cols),
                    lambda e, p: (e, 0, p[0])
                ),
                pl.BlockSpec(
                    (1, hidden_units, cols),
                    lambda e, p: (e, 0, p[1])
                ),
            ],
            out_specs=[
                pl.BlockSpec((2 * groups, tokens // groups, cols // chunks), lambda e, p: (0, 0, 0))
            ]
            * chunks,
            scratch_shapes=[pltpu.VMEM((2, parts, experts, rows, cols), BF16)],
        ),
        out_shape=[jax.ShapeDtypeStruct((2 * groups, tokens // groups, cols // chunks), BF16)]
        * chunks,
        compiler_params=pltpu.CompilerParams(
            vmem_limit_bytes=32 * 1024 * 1024, dimension_semantics=("arbitrary",)
        ),
        cost_estimate=pl.CostEstimate(
            flops=8 * experts * parts * rows * cols * hidden_units,
            bytes_accessed=4 * experts * cols * hidden_units + 4 * tokens * cols,
            transcendentals=0,
        ),
        name="down_mix",
    )(place, slots, act, w_down, w_down)


def flip(array, bits_of):
    pairs = []
    for index in range(32):
        pairs.append((index, index ^ bits_of(index & 1)))
    return lax.ppermute(array, ("expert", "tensor"), pairs)


CORE, X, Y, ZLOW, ZHIGH = 1, 2, 4, 8, 16


def first_axis(core):
    return Y if core else X


def last_axis(core):
    return X if core else Y


def own_order(groups, group):
    order = jnp.arange(groups, dtype=jnp.int32)
    return order ^ (group & 1)


def halving_places(to_core, group, groups):
    g = own_order(groups, group)[None, :]
    y_kept = ((g & 1) == (group & 1)).astype(jnp.int32)
    low_kept = (((g >> 1) & 1) == ((group >> 1) & 1)).astype(jnp.int32)
    high_kept = ((g >> 2) == (group >> 2)).astype(jnp.int32)
    x_kept = jnp.arange(2, dtype=jnp.int32)[:, None]
    first = jnp.where(to_core == 0, x_kept, y_kept)
    last = jnp.where(to_core == 0, y_kept, x_kept)
    return (((first * 2 + low_kept) * 2 + high_kept) * 2 + last).reshape(-1)


def total_of(terms):
    total = terms[0].astype(F32)
    for term in terms[1:]:
        total = total + term.astype(F32)
    return total


HALVING = (first_axis, lambda core: ZLOW, lambda core: ZHIGH, last_axis)


def after(value, earlier):
    return lax.optimization_barrier((value, earlier))


def sent_half(terms):
    half = terms[0].shape[0] // 2
    return total_of([term[:half] for term in terms]).astype(BF16), [term[half:] for term in terms]


def reduce_chunks(makers):
    chunks, arrived, first_sent = [None] * len(makers), {}, None
    for tick in range(len(HALVING) + len(makers) - 1):
        for index, maker in enumerate(makers):
            stage = tick - index
            if not 0 <= stage < len(HALVING):
                continue
            if stage == 0:
                chunks[index] = maker(first_sent)
            sent, rest = sent_half(chunks[index])
            if index:
                sent, _ = after(sent, arrived[index - 1, stage])
            if stage == 0:
                first_sent = sent
            came = flip(sent, HALVING[stage])
            arrived[index, stage] = came
            chunks[index] = rest + [came]
    return [total_of([term[0] for term in terms]) for terms in chunks]


def route_tables(route_ids, route_weights, group, experts, groups):
    here, top = route_ids.shape
    shares = route_weights / jnp.sum(route_weights, axis=-1, keepdims=True)
    table = jnp.concatenate([route_ids.astype(F32), shares], axis=1).T[None]
    for bits in (ZHIGH, ZLOW, Y):
        table = jnp.concatenate([table, flip(table, lambda core, bits=bits: bits)], axis=0)
    apart = own_order(groups, group) ^ group
    place = (apart >> 2) | (apart & 2) | ((apart & 1) << 2)
    table = jnp.take(table, place, axis=0, mode="clip")
    own = group * experts + jnp.arange(experts, dtype=jnp.int32)
    ids = table[:, :top, :].astype(jnp.int32)
    match = ids[None] == own[:, None, None, None]
    named = jnp.any(match, axis=2)
    weights = jnp.sum(jnp.where(match, table[None, :, top:, :], 0.0), axis=2)
    span = PAIR * here
    order = jnp.arange(span)
    earlier = (order[:, None] < order[None, :]).astype(BF16)
    rank = jnp.dot(
        named.astype(BF16).reshape(experts * groups // PAIR, span),
        earlier,
        preferred_element_type=F32,
    )
    slots = jnp.where(named, rank.reshape(named.shape).astype(jnp.int32), -1)
    return slots.reshape(experts, groups * here), weights.reshape(experts, groups * here)


def block_table(device, groups, member):
    number = jnp.arange(32, dtype=jnp.int32)
    array, place = number >> 3, number & 7
    source_core = (device & 1) ^ (array >> 1)
    first = jnp.where(source_core == 0, X, Y)
    last = jnp.where(source_core == 0, Y, X)
    feature = (
        device
        ^ (array >> 1)
        ^ jnp.where(array & 1 == 1, first, 0)
        ^ jnp.where(place & 1 == 1, last, 0)
        ^ jnp.where(place & 2 == 2, ZHIGH, 0)
        ^ jnp.where(place & 4 == 4, ZLOW, 0)
    )
    swapped = ((feature ^ device) >> 2) & 1
    return jnp.concatenate([feature, swapped, jnp.stack([member, device >> 3])])


def gather_chunks(starts):
    stages = (last_axis, lambda core: ZHIGH, lambda core: ZLOW, first_axis)
    held = [[start] for start in starts]
    arrived = {}
    for tick in range(len(stages) + len(starts) - 1):
        for index in range(len(starts)):
            stage = tick - index
            if not 0 <= stage < len(stages):
                continue
            block = held[index][-1]
            if index:
                block, _ = after(block, arrived[index - 1, stage])
            came = flip(block, stages[stage])
            arrived[index, stage] = came
            if stage < len(stages) - 1:
                held[index].append(jnp.concatenate([block, came], axis=0))
            else:
                other = flip(block, lambda core: CORE)
                held[index] = [block, came, other, flip(came, lambda core: CORE)]
    return held


def gather_heads(heads, beside):
    def along(bits, piece):
        return flip(piece, lambda core: bits)

    high = along(ZHIGH, heads)
    low = along(ZLOW, heads)
    high, beside = after(high, beside)
    both = along(ZLOW, high)
    own = [heads, high, low, both]
    other = [along(Y, piece) for piece in own]
    own, _ = after(own, (other[0], other[1]))
    return own, other, beside


def per_device_tokens(
    attn_heads, out_proj, residual, norm_gain, route_ids, route_weights, w_gate, w_up, w_down
):
    groups, members = lax.axis_size("expert"), lax.axis_size("tensor")
    group, member = lax.axis_index("expert"), lax.axis_index("tensor")
    device = group * members + member
    here, width = residual.shape
    experts = w_gate.shape[0]
    rows = -(-PAIR * CAP // 16) * 16
    x_side, core, y_side, z = member >> 1, member & 1, group & 1, group >> 1

    own_cols = lax.dynamic_index_in_dim(
        residual.reshape(here, groups, members, LANES), member, 2, keepdims=False
    )
    moved = lax.all_to_all(
        jnp.transpose(own_cols, (1, 0, 2)), "expert", split_axis=0, concat_axis=0, tiled=True
    ).reshape(groups // 2, 2, here, LANES)
    gain = lax.dynamic_index_in_dim(
        norm_gain.reshape(groups * members, LANES), device, 0, keepdims=False
    )

    member_info = jnp.stack([core, x_side, z])
    slots, weights = route_tables(route_ids, route_weights, group, experts, groups)
    starts = []
    own_heads, other_heads, moved = gather_heads(attn_heads, moved)
    for half, pieces in enumerate((own_heads, other_heads)):
        if half:
            (pieces, moved, gain), _ = after((pieces, moved, gain), (starts[0], slots, weights))
        send, keep = project(member_info, pieces, out_proj)
        came = flip(send, lambda c: CORE)
        to_x = (keep[0].astype(F32) + came[0].astype(F32)).astype(BF16)
        if not half:
            to_x, _ = after(to_x, other_heads[2])
        from_x = flip(to_x, lambda c: X)
        hidden = lax.dynamic_index_in_dim(moved, y_side ^ half, 1, keepdims=False).astype(F32)
        hidden = hidden + total_of([keep[1], came[1], from_x])
        starts.append((hidden * gain).astype(BF16)[None])

    own_x, other_x = gather_chunks(starts)
    x = [piece for pair in zip(own_x, other_x) for piece in pair]
    invgain = (1.0 / norm_gain).reshape(groups * members, LANES)
    act, own_hidden = gate_up(
        block_table(device, groups, member), slots, weights, invgain, x, w_gate, w_up, rows, 2
    )

    cols = width // members

    def columns_of(to_core, chunk, chunks):
        sides = jnp.stack([1 - x_side, x_side])
        blocks = (sides * 2 + to_core) * chunks + chunk
        return jnp.concatenate([blocks, halving_places(to_core, group, groups)])

    chunks = 2
    chunk_cols = cols // chunks
    other = down(
        columns_of(1 - core, 0, 1), slots, act, w_down, rows, groups, cols, chunks
    )
    came = [flip(piece, lambda c: CORE) for piece in other]

    def terms_of(chunk, earlier):
        ready = act if earlier is None else after(act, earlier)[0]
        place = columns_of(core, chunk, chunks)
        (kept,) = down(place, slots, ready, w_down, rows, groups, chunk_cols, 1)
        return [kept, came[chunk]]

    sums = reduce_chunks([functools.partial(terms_of, chunk) for chunk in range(chunks)])
    mixture = jnp.concatenate(sums, axis=1)
    return (own_hidden + mixture).astype(BF16)


def solution(mesh):
    groups, members = mesh.shape["expert"], mesh.shape["tensor"]
    placed = (
        P("expert", "tensor"),
        P("tensor", "expert"),
        P("expert", None),
        P(),
        P("expert", None),
        P("expert", None),
        P("expert", None, "tensor"),
        P("expert", None, "tensor"),
        P("expert", "tensor", None),
    )

    def run(*arrays):
        tokens, width = arrays[2].shape
        whole_tokens = (groups, members) == (8, 4) and width == groups * members * LANES
        body = per_device_tokens if whole_tokens else per_device_slots
        return jax.shard_map(
            body, mesh=mesh, in_specs=placed, out_specs=P("expert", "tensor"), check_vma=False
        )(*arrays)

    return run
```

```python
import functools

import jax
import jax.numpy as jnp
from jax import lax
from jax.experimental import pallas as pl
from jax.experimental.pallas import tpu as pltpu
from jax.sharding import PartitionSpec as P

EXPERTS = 64
CAP = 18
BF16 = jnp.bfloat16
F32 = jnp.float32
PAIR = 2
LANES = 128
HEAD_ORDER = (0, 2, 1, 3)


def slot_places(ids, experts, capacity):
    row_count, top_count = ids.shape
    onehot = (ids[:, :, None] == jnp.arange(experts, dtype=jnp.int32)[None, None, :]).astype(
        jnp.int32
    )
    flattened = onehot.reshape(row_count * top_count, experts)
    before = jnp.cumsum(flattened, axis=0) - flattened
    slot_rank = jnp.sum(before * flattened, axis=1).reshape(row_count, top_count)
    return ids * capacity + slot_rank


def per_device_slots(
    attn_heads, out_proj, residual, norm_gain, route_ids, route_weights, w_gate, w_up, w_down
):
    model_width = residual.shape[1]
    groups = lax.axis_size("expert")
    members = lax.axis_size("tensor")
    member = lax.axis_index("tensor")
    per_group = w_gate.shape[0]
    slot_count = EXPERTS * CAP
    block_cols = model_width // members
    heads_out = jnp.dot(
        attn_heads,
        lax.all_gather(out_proj, "expert", axis=1, tiled=True),
        preferred_element_type=F32,
    )
    attn_out = lax.psum(heads_out.astype(BF16), "tensor").astype(F32)
    hidden = residual.astype(F32) + attn_out
    normed = (
        hidden * lax.rsqrt(jnp.mean(hidden * hidden, axis=-1, keepdims=True) + 1e-06) * norm_gain
    ).astype(BF16)
    slot_index = slot_places(route_ids, EXPERTS, CAP)
    slot_range = jnp.arange(slot_count, dtype=jnp.int32)
    slot_hits = jnp.sum(
        (slot_index[:, :, None] == slot_range[None, None, :]).astype(BF16), axis=1
    )
    buffer = jnp.einsum("rj,rd->jd", slot_hits, normed, preferred_element_type=F32).astype(BF16)
    buffer = buffer.reshape(groups, per_group, CAP, model_width)
    arrived = lax.all_to_all(buffer, "expert", split_axis=0, concat_axis=0, tiled=True)
    gate_acc = jnp.einsum("gxcd,xdf->gxcf", arrived, w_gate, preferred_element_type=F32)
    upper = jnp.einsum("gxcd,xdf->gxcf", arrived, w_up, preferred_element_type=F32)
    activation = (jax.nn.silu(gate_acc) * upper).astype(BF16)
    product_term = jnp.einsum("gxcf,xfd->gxcd", activation, w_down, preferred_element_type=F32)
    product_term = product_term.astype(BF16).reshape(groups, per_group, CAP, members, block_cols)
    expert_out = lax.psum_scatter(
        jnp.transpose(product_term, (3, 0, 1, 2, 4)), "tensor", scatter_dimension=0, tiled=True
    )[0]
    returned = lax.all_to_all(expert_out, "expert", split_axis=0, concat_axis=0, tiled=True)
    weights = route_weights / jnp.sum(route_weights, axis=-1, keepdims=True)
    picked = returned.reshape(slot_count, block_cols)[slot_index]
    mixture = jnp.sum(weights[:, :, None] * picked.astype(F32), axis=1)
    own_hidden = lax.dynamic_slice_in_dim(hidden, member * block_cols, block_cols, 1)
    return (own_hidden + mixture).astype(BF16)


def hits_of(slot_row, rows):
    places = lax.broadcasted_iota(jnp.int32, (rows, slot_row.shape[1]), 0)
    return places == slot_row


def project_kernel(member_ref, head_refs, weight_ref, send_ref, keep_ref):
    core, x_side, z = member_ref[0], member_ref[1], member_ref[2]
    result = jnp.dot(
        jnp.concatenate([ref[...] for ref in head_refs], axis=0),
        weight_ref[...],
        preferred_element_type=F32,
    ).astype(BF16)
    here = head_refs[0].shape[0]
    for to_x in range(2):
        x_kept = (x_side == to_x).astype(jnp.int32)
        for to_core in range(2):
            start = (to_x * 2 + to_core) * LANES
            for out_ref, wanted in ((keep_ref, core == to_core), (send_ref, core != to_core)):

                @pl.when(wanted)
                def _(out_ref=out_ref, x_kept=x_kept, start=start):
                    for piece, z_bits in enumerate(HEAD_ORDER):
                        out_ref[x_kept, z ^ z_bits] = result[
                            piece * here : (piece + 1) * here, start : start + LANES
                        ]


def project(member_info, pieces, out_proj):
    here = pieces[0].shape[0]
    out = jax.ShapeDtypeStruct((2, len(pieces), here, LANES), BF16)
    vmem = pl.BlockSpec(memory_space=pltpu.VMEM)

    def kernel(member_ref, *refs):
        project_kernel(member_ref, refs[:4], refs[4], refs[5], refs[6])

    return pl.pallas_call(
        kernel,
        in_specs=[pl.BlockSpec(memory_space=pltpu.SMEM)] + [vmem] * 5,
        out_specs=[vmem, vmem],
        out_shape=[out, out],
        compiler_params=pltpu.CompilerParams(vmem_limit_bytes=24 * 1024 * 1024),
        cost_estimate=pl.CostEstimate(
            flops=2 * 4 * here * out_proj.size,
            bytes_accessed=2 * (out_proj.size + 5 * pieces[0].size),
            transcendentals=0,
        ),
        name="project",
    )(member_info, *pieces, out_proj)


def gate_up_kernel(
    experts, rows, width, info_ref, slot_ref, weight_ref, invgain_ref, x_refs, wg_ref, wu_ref,
    act_ref, hidden_ref, spread_ref, xs_ref, sq_ref, scale_ref, hits_ref
):
    expert = pl.program_id(0)
    arrays = len(x_refs) // 2
    each, parts, here, lanes = x_refs[0].shape
    blocks = arrays * each
    span = 2 * here
    member, z = info_ref[2 * blocks], info_ref[2 * blocks + 1]

    @pl.when(expert == 0)
    def _():
        sq_ref[...] = jnp.zeros_like(sq_ref)
        for part in range(parts):
            for e in range(experts):
                first = hits_of(slot_ref[e : e + 1, part * span : part * span + here], rows)
                second = hits_of(
                    slot_ref[e : e + 1, part * span + here : (part + 1) * span], rows
                )
                first = first.astype(F32).astype(BF16)
                second = second.astype(F32).astype(BF16)
                window = slice(e * rows, (e + 1) * rows)
                hits_ref[0, part, window, :] = jnp.concatenate([first, second], axis=1)
                hits_ref[1, part, window, :] = jnp.concatenate([second, first], axis=1)
            spread_ref[part] = jnp.transpose(hits_ref[0, part].astype(F32)).astype(BF16)

        def pair_of_blocks(low, carry):
            for array in range(arrays):
                own, other = x_refs[2 * array], x_refs[2 * array + 1]
                swapped = info_ref[blocks + array * each + low]
                places = (low, low + each // 2)
                features = [info_ref[array * each + place] for place in places]
                for place, feature in zip(places, features):
                    invgain = invgain_ref[pl.ds(feature, 1), :]
                    for part in range(parts):
                        for half, ref in enumerate((own, other)):
                            value = ref[place, part].astype(F32) * invgain
                            sq_ref[swapped, part, half] += value * value

                for part in range(parts):
                    both = jnp.concatenate(
                        [
                            jnp.concatenate([own[place, part], other[place, part]], axis=0)
                            for place in places
                        ],
                        axis=1,
                    )
                    picked = jnp.dot(
                        hits_ref[swapped, part], both, preferred_element_type=F32
                    ).astype(BF16)
                    for number, feature in enumerate(features):
                        column = pl.multiple_of(feature * lanes, lanes)
                        for e in range(experts):
                            xs_ref[e, part * rows : (part + 1) * rows, pl.ds(column, lanes)] = (
                                picked[
                                    e * rows : (e + 1) * rows, number * lanes : (number + 1) * lanes
                                ]
                            )
            return carry

        lax.fori_loop(0, each // 2, pair_of_blocks, 0)

        def own_block(place, carry):
            for array in range(arrays):
                feature = info_ref[array * each + place]

                @pl.when(feature >> 3 == member)
                def _(array=array, feature=feature):
                    own, other = x_refs[2 * array], x_refs[2 * array + 1]
                    mine = jnp.where(
                        info_ref[blocks + array * each + place] == 0,
                        own[place, z].astype(F32),
                        other[place, z].astype(F32),
                    )
                    column = pl.multiple_of((feature & 7) * lanes, lanes)
                    hidden_ref[:, pl.ds(column, lanes)] = mine * invgain_ref[pl.ds(feature, 1), :]

            return carry

        lax.fori_loop(0, each, own_block, 0)
        pieces = [
            sq_ref[0, part, half] + sq_ref[1, part, 1 - half]
            for part in range(parts)
            for half in range(2)
        ]
        total = jnp.sum(
            jnp.transpose(jnp.concatenate(pieces, axis=0)), axis=0, keepdims=True
        )
        scale_ref[...] = jnp.broadcast_to(lax.rsqrt(total / width + 1e-06), scale_ref.shape)

    summed = jnp.dot(
        xs_ref[expert],
        jnp.concatenate([wg_ref[0], wu_ref[0]], axis=1),
        preferred_element_type=F32,
    )
    hidden_units = wg_ref.shape[2]
    for part in range(parts):
        window = slice(part * span, (part + 1) * span)
        hits = hits_of(slot_ref[pl.ds(expert, 1), window], rows)
        scale = jnp.sum(jnp.where(hits, scale_ref[0:1, window], 0.0), axis=1, keepdims=True)
        weight = jnp.sum(
            jnp.where(hits, weight_ref[pl.ds(expert, 1), window], 0.0), axis=1, keepdims=True
        )
        both_part = summed[part * rows : (part + 1) * rows, :]
        gate = both_part[:, :hidden_units] * scale
        upper = both_part[:, hidden_units:] * scale
        act = gate / (1.0 + jnp.exp(-gate)) * upper * weight
        act_ref[expert, part * rows : (part + 1) * rows, :] = act.astype(BF16)


def gate_up(info, slots, weights, invgain, x, w_gate, w_up, rows):
    experts, width, hidden_units = w_gate.shape
    each, parts, here, lanes = x[0].shape
    tokens = slots.shape[1]
    members = width // (each * lanes)

    def kernel(info_ref, slot_ref, weight_ref, invgain_ref, *rest):
        gate_up_kernel(
            experts, rows, width, info_ref, slot_ref, weight_ref, invgain_ref,
            rest[: len(x)], *rest[len(x) :]
        )

    def whole(shape):
        return pl.BlockSpec(
            shape, lambda e, info: (0,) * len(shape), pipeline_mode=pl.Buffered(1)
        )

    return pl.pallas_call(
        kernel,
        grid_spec=pltpu.PrefetchScalarGridSpec(
            num_scalar_prefetch=1,
            grid=(experts,),
            in_specs=[whole(slots.shape), whole(weights.shape), whole(invgain.shape)]
            + [pl.BlockSpec(memory_space=pltpu.VMEM)] * len(x)
            + [pl.BlockSpec((1, width, hidden_units), lambda e, info: (e, 0, 0))] * 2,
            out_specs=[
                pl.BlockSpec(memory_space=pltpu.VMEM),
                pl.BlockSpec(memory_space=pltpu.VMEM),
                pl.BlockSpec(memory_space=pltpu.VMEM),
            ],
            scratch_shapes=[
                pltpu.VMEM((experts, parts * rows, width), BF16),
                pltpu.VMEM((2, parts, 2, here, lanes), F32),
                pltpu.VMEM((8, tokens), F32),
                pltpu.VMEM((2, parts, experts * rows, 2 * here), BF16),
            ],
        ),
        out_shape=[
            jax.ShapeDtypeStruct((experts, parts * rows, hidden_units), BF16),
            jax.ShapeDtypeStruct((here, width // members), F32),
            jax.ShapeDtypeStruct((parts, 2 * here, experts * rows), BF16),
        ],
        compiler_params=pltpu.CompilerParams(
            vmem_limit_bytes=44 * 1024 * 1024, dimension_semantics=("arbitrary",)
        ),
        cost_estimate=pl.CostEstimate(
            flops=2 * experts * parts * rows * width * 2 * hidden_units,
            bytes_accessed=4 * experts * width * hidden_units + 2 * len(x) * x[0].size,
            transcendentals=0,
        ),
        name="gate_up",
    )(info, slots, weights, invgain, *x, w_gate, w_up)


def down_kernel(rows, place_ref, spread_ref, act_ref, wd0_ref, wd1_ref, *rest):
    out_refs, ys_ref = rest[:-1], rest[-1]
    out_cols = out_refs[0].shape[2]
    step = pl.program_id(0)
    experts, all_rows, _ = act_ref.shape
    per_step = wd0_ref.shape[0]
    parts = all_rows // rows
    groups = parts * PAIR
    for number in range(per_step):
        expert = step * per_step + number
        for side, wd_ref in enumerate((wd0_ref, wd1_ref)):
            result = jnp.dot(
                act_ref[expert], wd_ref[number], preferred_element_type=F32
            ).astype(BF16)
            for part in range(parts):
                ys_ref[side, part, expert] = result[part * rows : (part + 1) * rows, :]

    @pl.when(step == pl.num_programs(0) - 1)
    def _():
        for part in range(parts):
            for side in range(2):
                picked = ys_ref[side, part].reshape(experts * rows, ys_ref.shape[4])
                mixed = jnp.dot(
                    spread_ref[part], picked, preferred_element_type=F32
                ).astype(BF16)
                for i in range(PAIR):
                    target = place_ref[2 + side * groups + part * PAIR + i]
                    for number, out_ref in enumerate(out_refs):
                        out_ref[target] = mixed[
                            i * 128 : (i + 1) * 128, number * out_cols : (number + 1) * out_cols
                        ]


def down(place, spread, act, w_down, rows, groups, cols, chunks, per_step=2):
    experts, hidden_units, width = w_down.shape
    parts, span, _ = spread.shape
    here = parts * span // groups
    out = jax.ShapeDtypeStruct((2 * groups, here, cols // chunks), BF16)
    return pl.pallas_call(
        functools.partial(down_kernel, rows),
        grid_spec=pltpu.PrefetchScalarGridSpec(
            num_scalar_prefetch=1,
            grid=(experts // per_step,),
            in_specs=[
                pl.BlockSpec(memory_space=pltpu.VMEM),
                pl.BlockSpec(memory_space=pltpu.VMEM),
                pl.BlockSpec((per_step, hidden_units, cols), lambda e, p: (e, 0, p[0])),
                pl.BlockSpec((per_step, hidden_units, cols), lambda e, p: (e, 0, p[1])),
            ],
            out_specs=[pl.BlockSpec(out.shape, lambda e, p: (0, 0, 0))] * chunks,
            scratch_shapes=[pltpu.VMEM((2, parts, experts, rows, cols), BF16)],
        ),
        out_shape=[out] * chunks,
        compiler_params=pltpu.CompilerParams(
            vmem_limit_bytes=36 * 1024 * 1024, dimension_semantics=("arbitrary",)
        ),
        cost_estimate=pl.CostEstimate(
            flops=8 * experts * parts * rows * cols * hidden_units,
            bytes_accessed=4 * experts * cols * hidden_units + 4 * parts * span * cols,
            transcendentals=0,
        ),
        name="down_mix",
    )(place, spread, act, w_down, w_down)


def flip(array, bits_of):
    pairs = []
    for index in range(32):
        pairs.append((index, index ^ bits_of(index & 1)))
    return lax.ppermute(array, ("expert", "tensor"), pairs)


CORE, X, Y, ZLOW, ZHIGH = 1, 2, 4, 8, 16


def first_axis(core):
    return Y if core else X


def last_axis(core):
    return X if core else Y


def own_order(groups, group):
    order = jnp.arange(groups, dtype=jnp.int32)
    return order ^ (group & 1)


def halving_places(to_core, group, groups):
    g = own_order(groups, group)[None, :]
    y_kept = ((g & 1) == (group & 1)).astype(jnp.int32)
    low_kept = (((g >> 1) & 1) == ((group >> 1) & 1)).astype(jnp.int32)
    high_kept = ((g >> 2) == (group >> 2)).astype(jnp.int32)
    x_kept = jnp.arange(2, dtype=jnp.int32)[:, None]
    first = jnp.where(to_core == 0, x_kept, y_kept)
    last = jnp.where(to_core == 0, y_kept, x_kept)
    return (((first * 2 + low_kept) * 2 + high_kept) * 2 + last).reshape(-1)


def total_of(terms):
    total = terms[0].astype(F32)
    for term in terms[1:]:
        total = total + term.astype(F32)
    return total


HALVING = (first_axis, lambda core: ZLOW, lambda core: ZHIGH, last_axis)


def after(value, earlier):
    return lax.optimization_barrier((value, earlier))


def sent_half(terms):
    half = terms[0].shape[0] // 2
    return total_of([term[:half] for term in terms]).astype(BF16), [term[half:] for term in terms]


def reduce_chunks(makers):
    chunks, arrived, first_sent = [None] * len(makers), {}, None
    for tick in range(len(HALVING) + len(makers) - 1):
        for index, maker in enumerate(makers):
            stage = tick - index
            if not 0 <= stage < len(HALVING):
                continue
            if stage == 0:
                chunks[index] = maker(first_sent)
            sent, rest = sent_half(chunks[index])
            if index:
                sent, _ = after(sent, arrived[index - 1, stage])
            if stage == 0:
                first_sent = sent
            came = flip(sent, HALVING[stage])
            arrived[index, stage] = came
            chunks[index] = rest + [came]
    return [total_of([term[0] for term in terms]) for terms in chunks]


def route_tables(route_ids, route_weights, group, experts, groups):
    here, top = route_ids.shape
    shares = route_weights / jnp.sum(route_weights, axis=-1, keepdims=True)
    table = jnp.concatenate([route_ids.astype(F32), shares], axis=1).T[None]
    for bits in (ZHIGH, ZLOW, Y):
        table = jnp.concatenate([table, flip(table, lambda core, bits=bits: bits)], axis=0)
    apart = own_order(groups, group) ^ group
    place = (apart >> 2) | (apart & 2) | ((apart & 1) << 2)
    table = jnp.take(table, place, axis=0, mode="clip")
    own = group * experts + jnp.arange(experts, dtype=jnp.int32)
    ids = table[:, :top, :].astype(jnp.int32)
    match = ids[None] == own[:, None, None, None]
    named = jnp.any(match, axis=2)
    weights = jnp.sum(jnp.where(match, table[None, :, top:, :], 0.0), axis=2)
    span = PAIR * here
    order = jnp.arange(span)
    earlier = (order[:, None] < order[None, :]).astype(BF16)
    rank = jnp.dot(
        named.astype(BF16).reshape(experts * groups // PAIR, span),
        earlier,
        preferred_element_type=F32,
    )
    slots = jnp.where(named, rank.reshape(named.shape).astype(jnp.int32), -1)
    return slots.reshape(experts, groups * here), weights.reshape(experts, groups * here)


def block_table(device, groups, member):
    number = jnp.arange(32, dtype=jnp.int32)
    array, place = number >> 3, number & 7
    source_core = (device & 1) ^ (array >> 1)
    first = jnp.where(source_core == 0, X, Y)
    last = jnp.where(source_core == 0, Y, X)
    feature = (
        device
        ^ (array >> 1)
        ^ jnp.where(array & 1 == 1, first, 0)
        ^ jnp.where(place & 1 == 1, last, 0)
        ^ jnp.where(place & 2 == 2, ZHIGH, 0)
        ^ jnp.where(place & 4 == 4, ZLOW, 0)
    )
    swapped = ((feature ^ device) >> 2) & 1
    return jnp.concatenate([feature, swapped, jnp.stack([member, device >> 3])])


def gather_chunks(starts, beside):
    stages = (last_axis, lambda core: ZHIGH, lambda core: ZLOW, first_axis)
    held = [[start] for start in starts]
    arrived = {}
    for tick in range(len(stages) + len(starts) - 1):
        for index in reversed(range(len(starts))):
            stage = tick - index
            if not 0 <= stage < len(stages):
                continue
            block = held[index][-1]
            if index:
                block, _ = after(block, arrived[index - 1, stage])
            if stage == len(stages) - 1 and index == len(starts) - 1:
                block, _ = after(block, beside)
            came = flip(block, stages[stage])
            if stage == 1 and (index + 1, 0) in arrived:
                came, _ = after(came, arrived[index + 1, 0])
            arrived[index, stage] = came
            if stage < len(stages) - 1:
                held[index].append(jnp.concatenate([block, came], axis=0))
            else:
                other = flip(block, lambda core: CORE)
                held[index] = [block, came, other, flip(came, lambda core: CORE)]
    return held


def gather_heads(heads, beside):
    def along(bits, piece):
        return flip(piece, lambda core: bits)

    high = along(ZHIGH, heads)
    low = along(ZLOW, heads)
    both, beside = after(along(ZLOW, high), beside)
    own = [heads, high, low, both]
    other = [along(Y, piece) for piece in own]
    own, _ = after(own, other[:3])
    return own, other, beside


def per_device_tokens(
    attn_heads, out_proj, residual, norm_gain, route_ids, route_weights, w_gate, w_up, w_down
):
    groups, members = lax.axis_size("expert"), lax.axis_size("tensor")
    group, member = lax.axis_index("expert"), lax.axis_index("tensor")
    device = group * members + member
    here, width = residual.shape
    experts = w_gate.shape[0]
    rows = -(-PAIR * CAP // 16) * 16
    x_side, core, y_side, z = member >> 1, member & 1, group & 1, group >> 1

    own_cols = lax.dynamic_index_in_dim(
        residual.reshape(here, groups, members, LANES), member, 2, keepdims=False
    )
    moved = lax.all_to_all(
        jnp.transpose(own_cols, (1, 0, 2)), "expert", split_axis=0, concat_axis=0, tiled=True
    ).reshape(groups // 2, 2, here, LANES)
    gain = lax.dynamic_index_in_dim(
        norm_gain.reshape(groups * members, LANES), device, 0, keepdims=False
    )

    member_info = jnp.stack([core, x_side, z])
    starts = []
    own_heads, other_heads, moved = gather_heads(attn_heads, moved)
    for half, pieces in enumerate((own_heads, other_heads)):
        if half:
            (pieces, moved, gain), _ = after((pieces, moved, gain), starts[0])
        send, keep = project(member_info, pieces, out_proj)
        came = flip(send, lambda c: CORE)
        to_x = (keep[0].astype(F32) + came[0].astype(F32)).astype(BF16)
        from_x = flip(to_x, lambda c: X)
        hidden = lax.dynamic_index_in_dim(moved, y_side ^ half, 1, keepdims=False).astype(F32)
        hidden = hidden + total_of([keep[1], came[1], from_x])
        starts.append((hidden * gain).astype(BF16)[None])

    route_ids, _ = after(route_ids, starts[1])
    slots, weights = route_tables(route_ids, route_weights, group, experts, groups)
    own_x, other_x = gather_chunks(starts, (slots, weights))
    x = [piece for pair in zip(own_x, other_x) for piece in pair]
    invgain = (1.0 / norm_gain).reshape(groups * members, LANES)
    act, own_hidden, spread = gate_up(
        block_table(device, groups, member), slots, weights, invgain, x, w_gate, w_up, rows
    )

    cols = width // members

    def columns_of(to_core, chunk, chunks):
        sides = jnp.stack([1 - x_side, x_side])
        blocks = (sides * 2 + to_core) * chunks + chunk
        return jnp.concatenate([blocks, halving_places(to_core, group, groups)])

    chunks = 2
    chunk_cols = cols // chunks
    other = down(
        columns_of(1 - core, 0, 1), spread, act, w_down, rows, groups, cols, chunks
    )
    came = [flip(piece, lambda c: CORE) for piece in other]

    def terms_of(chunk, earlier):
        ready = act if earlier is None else after(act, earlier)[0]
        place = columns_of(core, chunk, chunks)
        (kept,) = down(place, spread, ready, w_down, rows, groups, chunk_cols, 1)
        return [kept, came[chunk]]

    sums = reduce_chunks([functools.partial(terms_of, chunk) for chunk in range(chunks)])
    mixture = jnp.concatenate(sums, axis=1)
    return (own_hidden + mixture).astype(BF16)


def solution(mesh):
    groups, members = mesh.shape["expert"], mesh.shape["tensor"]
    placed = (
        P("expert", "tensor"),
        P("tensor", "expert"),
        P("expert", None),
        P(),
        P("expert", None),
        P("expert", None),
        P("expert", None, "tensor"),
        P("expert", None, "tensor"),
        P("expert", "tensor", None),
    )

    def run(*arrays):
        tokens, width = arrays[2].shape
        whole_tokens = (groups, members) == (8, 4) and width == groups * members * LANES
        body = per_device_tokens if whole_tokens else per_device_slots
        return jax.shard_map(
            body, mesh=mesh, in_specs=placed, out_specs=P("expert", "tensor"), check_vma=False
        )(*arrays)

    return run
```

```python
import functools

import jax
import jax.numpy as jnp
from jax import lax
from jax.experimental import pallas as pl
from jax.experimental.pallas import tpu as pltpu
from jax.sharding import PartitionSpec as P

EXPERTS = 64
CAP = 18
BF16 = jnp.bfloat16
F32 = jnp.float32
PAIR = 2
LANES = 128
HEAD_ORDER = (0, 2, 1, 3)


def slot_places(ids, experts, capacity):
    row_count, top_count = ids.shape
    onehot = (ids[:, :, None] == jnp.arange(experts, dtype=jnp.int32)[None, None, :]).astype(
        jnp.int32
    )
    flattened = onehot.reshape(row_count * top_count, experts)
    before = jnp.cumsum(flattened, axis=0) - flattened
    slot_rank = jnp.sum(before * flattened, axis=1).reshape(row_count, top_count)
    return ids * capacity + slot_rank


def per_device_slots(
    attn_heads, out_proj, residual, norm_gain, route_ids, route_weights, w_gate, w_up, w_down
):
    model_width = residual.shape[1]
    groups = lax.axis_size("expert")
    members = lax.axis_size("tensor")
    member = lax.axis_index("tensor")
    per_group = w_gate.shape[0]
    slot_count = EXPERTS * CAP
    block_cols = model_width // members
    heads_out = jnp.dot(
        attn_heads,
        lax.all_gather(out_proj, "expert", axis=1, tiled=True),
        preferred_element_type=F32,
    )
    attn_out = lax.psum(heads_out.astype(BF16), "tensor").astype(F32)
    hidden = residual.astype(F32) + attn_out
    normed = (
        hidden * lax.rsqrt(jnp.mean(hidden * hidden, axis=-1, keepdims=True) + 1e-06) * norm_gain
    ).astype(BF16)
    slot_index = slot_places(route_ids, EXPERTS, CAP)
    slot_range = jnp.arange(slot_count, dtype=jnp.int32)
    slot_hits = jnp.sum(
        (slot_index[:, :, None] == slot_range[None, None, :]).astype(BF16), axis=1
    )
    buffer = jnp.einsum("rj,rd->jd", slot_hits, normed, preferred_element_type=F32).astype(BF16)
    buffer = buffer.reshape(groups, per_group, CAP, model_width)
    arrived = lax.all_to_all(buffer, "expert", split_axis=0, concat_axis=0, tiled=True)
    gate_acc = jnp.einsum("gxcd,xdf->gxcf", arrived, w_gate, preferred_element_type=F32)
    upper = jnp.einsum("gxcd,xdf->gxcf", arrived, w_up, preferred_element_type=F32)
    activation = (jax.nn.silu(gate_acc) * upper).astype(BF16)
    product_term = jnp.einsum("gxcf,xfd->gxcd", activation, w_down, preferred_element_type=F32)
    product_term = product_term.astype(BF16).reshape(groups, per_group, CAP, members, block_cols)
    expert_out = lax.psum_scatter(
        jnp.transpose(product_term, (3, 0, 1, 2, 4)), "tensor", scatter_dimension=0, tiled=True
    )[0]
    returned = lax.all_to_all(expert_out, "expert", split_axis=0, concat_axis=0, tiled=True)
    weights = route_weights / jnp.sum(route_weights, axis=-1, keepdims=True)
    picked = returned.reshape(slot_count, block_cols)[slot_index]
    mixture = jnp.sum(weights[:, :, None] * picked.astype(F32), axis=1)
    own_hidden = lax.dynamic_slice_in_dim(hidden, member * block_cols, block_cols, 1)
    return (own_hidden + mixture).astype(BF16)


def hits_of(slot_row, rows):
    places = lax.broadcasted_iota(jnp.int32, (rows, slot_row.shape[1]), 0)
    return places == slot_row


def project_kernel(member_ref, head_refs, weight_ref, send_ref, keep_ref):
    core, x_side, z = member_ref[0], member_ref[1], member_ref[2]
    here = head_refs[0].shape[0]
    each = len(HEAD_ORDER)
    for half in range(2):
        result = jnp.dot(
            jnp.concatenate([ref[...] for ref in head_refs[half * each : (half + 1) * each]]),
            weight_ref[...],
            preferred_element_type=F32,
        ).astype(BF16)
        for to_x in range(2):
            x_kept = (x_side == to_x).astype(jnp.int32)
            for to_core in range(2):
                start = (to_x * 2 + to_core) * LANES
                for out_ref, wanted in ((keep_ref, core == to_core), (send_ref, core != to_core)):

                    @pl.when(wanted)
                    def _(out_ref=out_ref, x_kept=x_kept, start=start, half=half, result=result):
                        for piece, z_bits in enumerate(HEAD_ORDER):
                            out_ref[x_kept, half, z ^ z_bits] = result[
                                piece * here : (piece + 1) * here, start : start + LANES
                            ]


def project(member_info, pieces, out_proj):
    here = pieces[0].shape[0]
    out = jax.ShapeDtypeStruct((2, 2, len(HEAD_ORDER), here, LANES), BF16)
    vmem = pl.BlockSpec(memory_space=pltpu.VMEM)

    def kernel(member_ref, *refs):
        project_kernel(member_ref, refs[: len(pieces)], *refs[len(pieces) :])

    return pl.pallas_call(
        kernel,
        in_specs=[pl.BlockSpec(memory_space=pltpu.SMEM)] + [vmem] * (len(pieces) + 1),
        out_specs=[vmem, vmem],
        out_shape=[out, out],
        compiler_params=pltpu.CompilerParams(vmem_limit_bytes=24 * 1024 * 1024),
        cost_estimate=pl.CostEstimate(
            flops=2 * len(pieces) * here * out_proj.size,
            bytes_accessed=2 * (out_proj.size + 2 * len(pieces) * pieces[0].size),
            transcendentals=0,
        ),
        name="project",
    )(member_info, *pieces, out_proj)


def other_place(place):
    return (place >> 1) | ((place & 1) << 2)


def gate_up_kernel(
    experts, rows, width, info_ref, slot_ref, weight_ref, invgain_ref, x_refs, wg_ref, wu_ref,
    act_ref, hidden_ref, spread_ref, xs_ref, sq_ref, scale_ref, hits_ref
):
    expert = pl.program_id(0)
    arrays = len(x_refs) // 2
    each, parts, here, lanes = x_refs[0].shape
    blocks = arrays * each
    span = 2 * here
    member, z = info_ref[2 * blocks], info_ref[2 * blocks + 1]

    @pl.when(expert == 0)
    def _():
        sq_ref[...] = jnp.zeros_like(sq_ref)
        for part in range(parts):
            for e in range(experts):
                first = hits_of(slot_ref[e : e + 1, part * span : part * span + here], rows)
                second = hits_of(
                    slot_ref[e : e + 1, part * span + here : (part + 1) * span], rows
                )
                first = first.astype(F32).astype(BF16)
                second = second.astype(F32).astype(BF16)
                window = slice(e * rows, (e + 1) * rows)
                hits_ref[0, part, window, :] = jnp.concatenate([first, second], axis=1)
                hits_ref[1, part, window, :] = jnp.concatenate([second, first], axis=1)
            spread_ref[part] = jnp.transpose(hits_ref[0, part].astype(F32)).astype(BF16)

        def pair_of_blocks(low, carry):
            for array in range(arrays):
                own, other = x_refs[2 * array], x_refs[2 * array + 1]
                swapped = info_ref[blocks + array * each + low]
                places = (low, low + each // 2)
                features = [info_ref[array * each + place] for place in places]
                for place, feature in zip(places, features):
                    invgain = invgain_ref[pl.ds(feature, 1), :]
                    for part in range(parts):
                        for half, block in enumerate(
                            (own[place, part], other[other_place(place), part])
                        ):
                            value = block.astype(F32) * invgain
                            sq_ref[swapped, part, half] += value * value

                for part in range(parts):
                    both = jnp.concatenate(
                        [
                            jnp.concatenate([own[place, part], other[other_place(place), part]])
                            for place in places
                        ],
                        axis=1,
                    )
                    picked = jnp.dot(
                        hits_ref[swapped, part], both, preferred_element_type=F32
                    ).astype(BF16)
                    for number, feature in enumerate(features):
                        column = pl.multiple_of(feature * lanes, lanes)
                        for e in range(experts):
                            xs_ref[e, part * rows : (part + 1) * rows, pl.ds(column, lanes)] = (
                                picked[
                                    e * rows : (e + 1) * rows, number * lanes : (number + 1) * lanes
                                ]
                            )
            return carry

        lax.fori_loop(0, each // 2, pair_of_blocks, 0)

        def own_block(place, carry):
            for array in range(arrays):
                feature = info_ref[array * each + place]

                @pl.when(feature >> 3 == member)
                def _(array=array, feature=feature):
                    own, other = x_refs[2 * array], x_refs[2 * array + 1]
                    mine = jnp.where(
                        info_ref[blocks + array * each + place] == 0,
                        own[place, z].astype(F32),
                        other[other_place(place), z].astype(F32),
                    )
                    column = pl.multiple_of((feature & 7) * lanes, lanes)
                    hidden_ref[:, pl.ds(column, lanes)] = mine * invgain_ref[pl.ds(feature, 1), :]

            return carry

        lax.fori_loop(0, each, own_block, 0)
        pieces = [
            sq_ref[0, part, half] + sq_ref[1, part, 1 - half]
            for part in range(parts)
            for half in range(2)
        ]
        total = jnp.sum(
            jnp.transpose(jnp.concatenate(pieces, axis=0)), axis=0, keepdims=True
        )
        scale_ref[...] = jnp.broadcast_to(lax.rsqrt(total / width + 1e-06), scale_ref.shape)

    summed = jnp.dot(
        xs_ref[expert],
        jnp.concatenate([wg_ref[0], wu_ref[0]], axis=1),
        preferred_element_type=F32,
    )
    hidden_units = wg_ref.shape[2]
    for part in range(parts):
        window = slice(part * span, (part + 1) * span)
        hits = hits_of(slot_ref[pl.ds(expert, 1), window], rows)
        scale = jnp.sum(jnp.where(hits, scale_ref[0:1, window], 0.0), axis=1, keepdims=True)
        weight = jnp.sum(
            jnp.where(hits, weight_ref[pl.ds(expert, 1), window], 0.0), axis=1, keepdims=True
        )
        both_part = summed[part * rows : (part + 1) * rows, :]
        gate = both_part[:, :hidden_units] * scale
        upper = both_part[:, hidden_units:] * scale
        act = gate / (1.0 + jnp.exp(-gate)) * upper * weight
        act_ref[expert, part * rows : (part + 1) * rows, :] = act.astype(BF16)


def gate_up(info, slots, weights, invgain, x, w_gate, w_up, rows):
    experts, width, hidden_units = w_gate.shape
    each, parts, here, lanes = x[0].shape
    tokens = slots.shape[1]
    members = width // (each * lanes)

    def kernel(info_ref, slot_ref, weight_ref, invgain_ref, *rest):
        gate_up_kernel(
            experts, rows, width, info_ref, slot_ref, weight_ref, invgain_ref,
            rest[: len(x)], *rest[len(x) :]
        )

    def whole(shape):
        return pl.BlockSpec(
            shape, lambda e, info: (0,) * len(shape), pipeline_mode=pl.Buffered(1)
        )

    return pl.pallas_call(
        kernel,
        grid_spec=pltpu.PrefetchScalarGridSpec(
            num_scalar_prefetch=1,
            grid=(experts,),
            in_specs=[whole(slots.shape), whole(weights.shape), whole(invgain.shape)]
            + [pl.BlockSpec(memory_space=pltpu.VMEM)] * len(x)
            + [pl.BlockSpec((1, width, hidden_units), lambda e, info: (e, 0, 0))] * 2,
            out_specs=[
                pl.BlockSpec(memory_space=pltpu.VMEM),
                pl.BlockSpec(memory_space=pltpu.VMEM),
                pl.BlockSpec(memory_space=pltpu.VMEM),
            ],
            scratch_shapes=[
                pltpu.VMEM((experts, parts * rows, width), BF16),
                pltpu.VMEM((2, parts, 2, here, lanes), F32),
                pltpu.VMEM((8, tokens), F32),
                pltpu.VMEM((2, parts, experts * rows, 2 * here), BF16),
            ],
        ),
        out_shape=[
            jax.ShapeDtypeStruct((experts, parts * rows, hidden_units), BF16),
            jax.ShapeDtypeStruct((here, width // members), F32),
            jax.ShapeDtypeStruct((parts, 2 * here, experts * rows), BF16),
        ],
        compiler_params=pltpu.CompilerParams(
            vmem_limit_bytes=44 * 1024 * 1024, dimension_semantics=("arbitrary",)
        ),
        cost_estimate=pl.CostEstimate(
            flops=2 * experts * parts * rows * width * 2 * hidden_units,
            bytes_accessed=4 * experts * width * hidden_units + 2 * len(x) * x[0].size,
            transcendentals=0,
        ),
        name="gate_up",
    )(info, slots, weights, invgain, *x, w_gate, w_up)


def down_kernel(rows, place_ref, spread_ref, act_ref, wd0_ref, wd1_ref, *rest):
    out_refs, ys_ref = rest[:-1], rest[-1]
    out_cols = out_refs[0].shape[2]
    step = pl.program_id(0)
    experts, all_rows, _ = act_ref.shape
    per_step = wd0_ref.shape[0]
    parts = all_rows // rows
    groups = parts * PAIR
    for number in range(per_step):
        expert = step * per_step + number
        for side, wd_ref in enumerate((wd0_ref, wd1_ref)):
            result = jnp.dot(
                act_ref[expert], wd_ref[number], preferred_element_type=F32
            ).astype(BF16)
            for part in range(parts):
                ys_ref[side, part, expert] = result[part * rows : (part + 1) * rows, :]

    @pl.when(step == pl.num_programs(0) - 1)
    def _():
        for part in range(parts):
            for side in range(2):
                picked = ys_ref[side, part].reshape(experts * rows, ys_ref.shape[4])
                mixed = jnp.dot(
                    spread_ref[part], picked, preferred_element_type=F32
                ).astype(BF16)
                for i in range(PAIR):
                    for number, out_ref in enumerate(out_refs):
                        block = (number * 2 + side) * groups + part * PAIR + i
                        target = place_ref[2 + block]
                        out_ref[target] = mixed[
                            i * 128 : (i + 1) * 128, number * out_cols : (number + 1) * out_cols
                        ]


def down(place, spread, act, w_down, rows, groups, cols, chunks, per_step=2):
    experts, hidden_units, width = w_down.shape
    parts, span, _ = spread.shape
    here = parts * span // groups
    out = jax.ShapeDtypeStruct((2 * groups, here, cols // chunks), BF16)
    return pl.pallas_call(
        functools.partial(down_kernel, rows),
        grid_spec=pltpu.PrefetchScalarGridSpec(
            num_scalar_prefetch=1,
            grid=(experts // per_step,),
            in_specs=[
                pl.BlockSpec(memory_space=pltpu.VMEM),
                pl.BlockSpec(memory_space=pltpu.VMEM),
                pl.BlockSpec((per_step, hidden_units, cols), lambda e, p: (e, 0, p[0])),
                pl.BlockSpec((per_step, hidden_units, cols), lambda e, p: (e, 0, p[1])),
            ],
            out_specs=[pl.BlockSpec(out.shape, lambda e, p: (0, 0, 0))] * chunks,
            scratch_shapes=[pltpu.VMEM((2, parts, experts, rows, cols), BF16)],
        ),
        out_shape=[out] * chunks,
        compiler_params=pltpu.CompilerParams(
            vmem_limit_bytes=36 * 1024 * 1024, dimension_semantics=("arbitrary",)
        ),
        cost_estimate=pl.CostEstimate(
            flops=8 * experts * parts * rows * cols * hidden_units,
            bytes_accessed=4 * experts * cols * hidden_units + 4 * parts * span * cols,
            transcendentals=0,
        ),
        name="down_mix",
    )(place, spread, act, w_down, w_down)


def flip(array, bits_of):
    pairs = []
    for index in range(32):
        pairs.append((index, index ^ bits_of(index & 1)))
    return lax.ppermute(array, ("expert", "tensor"), pairs)


CORE, X, Y, ZLOW, ZHIGH = 1, 2, 4, 8, 16


def first_axis(core):
    return Y if core else X


def last_axis(core):
    return X if core else Y


def own_order(groups, group):
    order = jnp.arange(groups, dtype=jnp.int32)
    return order ^ (group & 1)


HALVING = {
    "first": first_axis,
    "last": last_axis,
    "low": lambda core: ZLOW,
    "high": lambda core: ZHIGH,
}
ORDERS = (("first", "low", "high", "last"), ("first", "last", "low", "high"))


def halving_places(to_core, group, groups, order):
    g = own_order(groups, group)[None, :]
    y_kept = ((g & 1) == (group & 1)).astype(jnp.int32)
    x_kept = jnp.arange(2, dtype=jnp.int32)[:, None]
    kept = {
        "first": jnp.where(to_core == 0, x_kept, y_kept),
        "last": jnp.where(to_core == 0, y_kept, x_kept),
        "low": (((g >> 1) & 1) == ((group >> 1) & 1)).astype(jnp.int32),
        "high": ((g >> 2) == (group >> 2)).astype(jnp.int32),
    }
    place = 0
    for axis in order:
        place = place * 2 + kept[axis]
    return place.reshape(-1)


def total_of(terms):
    total = terms[0].astype(F32)
    for term in terms[1:]:
        total = total + term.astype(F32)
    return total


def after(value, earlier):
    return lax.optimization_barrier((value, earlier))


def reduce_chunks(makers):
    terms, came = [None, None], {}

    def exchange(chunk, stage, earlier=None):
        half = terms[chunk][0].shape[0] // 2
        sent = total_of([term[:half] for term in terms[chunk]]).astype(BF16)
        if earlier is not None:
            sent, _ = after(sent, earlier)
        came[chunk, stage] = flip(sent, HALVING[ORDERS[chunk][stage]])
        terms[chunk] = [term[half:] for term in terms[chunk]] + [came[chunk, stage]]
        return sent

    terms[0] = makers[0](None)
    terms[1] = makers[1](exchange(0, 0))
    exchange(1, 0, came[0, 0])
    exchange(0, 1)
    exchange(1, 1, came[0, 1])
    exchange(0, 2)
    exchange(1, 2)
    exchange(0, 3, came[1, 2])
    exchange(1, 3)
    return [total_of([term[0] for term in chunk]) for chunk in terms]


def route_tables(route_ids, route_weights, group, experts, groups):
    here, top = route_ids.shape
    shares = route_weights / jnp.sum(route_weights, axis=-1, keepdims=True)
    table = jnp.concatenate([route_ids.astype(F32), shares], axis=1).T[None]
    for bits in (ZHIGH, ZLOW, Y):
        table = jnp.concatenate([table, flip(table, lambda core, bits=bits: bits)], axis=0)
    apart = own_order(groups, group) ^ group
    place = (apart >> 2) | (apart & 2) | ((apart & 1) << 2)
    table = jnp.take(table, place, axis=0, mode="clip")
    own = group * experts + jnp.arange(experts, dtype=jnp.int32)
    ids = table[:, :top, :].astype(jnp.int32)
    match = ids[None] == own[:, None, None, None]
    named = jnp.any(match, axis=2)
    weights = jnp.sum(jnp.where(match, table[None, :, top:, :], 0.0), axis=2)
    span = PAIR * here
    order = jnp.arange(span)
    earlier = (order[:, None] < order[None, :]).astype(BF16)
    rank = jnp.dot(
        named.astype(BF16).reshape(experts * groups // PAIR, span),
        earlier,
        preferred_element_type=F32,
    )
    slots = jnp.where(named, rank.reshape(named.shape).astype(jnp.int32), -1)
    return slots.reshape(experts, groups * here), weights.reshape(experts, groups * here)


def block_table(device, groups, member):
    number = jnp.arange(32, dtype=jnp.int32)
    array, place = number >> 3, number & 7
    source_core = (device & 1) ^ (array >> 1)
    first = jnp.where(source_core == 0, X, Y)
    last = jnp.where(source_core == 0, Y, X)
    feature = (
        device
        ^ (array >> 1)
        ^ jnp.where(array & 1 == 1, first, 0)
        ^ jnp.where(place & 1 == 1, last, 0)
        ^ jnp.where(place & 2 == 2, ZHIGH, 0)
        ^ jnp.where(place & 4 == 4, ZLOW, 0)
    )
    swapped = ((feature ^ device) >> 2) & 1
    return jnp.concatenate([feature, swapped, jnp.stack([member, device >> 3])])


def gather_blocks(first, second, make_beside):
    def along(bits, block):
        return flip(block, lambda core: bits)

    def joined(held, came):
        return jnp.concatenate([held, came], axis=0)

    first_last = flip(first, last_axis)
    second_high = along(ZHIGH, second)
    second = joined(second, second_high)
    second_low = along(ZLOW, second)
    first, _ = after(joined(first, first_last), second_high)
    beside = make_beside((first_last, second_high))
    first_high = along(ZHIGH, first)
    second = joined(second, second_low)
    second_last = flip(second, last_axis)
    first, _ = after(joined(first, first_high), second_low)
    first_low = along(ZLOW, first)
    second = joined(second, second_last)
    second_first = flip(second, first_axis)
    first, _ = after(joined(first, first_low), (second_last, beside))
    first_first = flip(first, first_axis)
    return [
        [block, came, along(CORE, block), along(CORE, came)]
        for block, came in ((first, first_first), (second, second_first))
    ] + [beside]


def gather_heads(heads):
    def along(bits, piece):
        return flip(piece, lambda core: bits)

    high = along(ZHIGH, heads)
    low = along(ZLOW, heads)
    own = [heads, high, low, along(ZLOW, high)]
    return own + [along(Y, piece) for piece in own]


def per_device_tokens(
    attn_heads, out_proj, residual, norm_gain, route_ids, route_weights, w_gate, w_up, w_down
):
    groups, members = lax.axis_size("expert"), lax.axis_size("tensor")
    group, member = lax.axis_index("expert"), lax.axis_index("tensor")
    device = group * members + member
    here, width = residual.shape
    experts = w_gate.shape[0]
    rows = -(-PAIR * CAP // 16) * 16
    x_side, core, y_side, z = member >> 1, member & 1, group & 1, group >> 1

    own_cols = lax.dynamic_index_in_dim(
        residual.reshape(here, groups, members, LANES), member, 2, keepdims=False
    )
    moved = lax.all_to_all(
        jnp.transpose(own_cols, (1, 0, 2)), "expert", split_axis=0, concat_axis=0, tiled=True
    ).reshape(groups // 2, 2, here, LANES)
    gain = lax.dynamic_index_in_dim(
        norm_gain.reshape(groups * members, LANES), device, 0, keepdims=False
    )

    member_info = jnp.stack([core, x_side, z])
    pieces, moved = after(gather_heads(attn_heads), moved)
    send, keep = project(member_info, pieces, out_proj)
    came = flip(send, lambda c: CORE)
    from_x = flip(total_of([keep[0], came[0]]).astype(BF16), lambda c: X)
    starts = []
    for half in range(2):
        hidden = lax.dynamic_index_in_dim(moved, y_side ^ half, 1, keepdims=False).astype(F32)
        hidden = hidden + total_of([keep[1, half], came[1, half], from_x[half]])
        starts.append((hidden * gain).astype(BF16)[None])

    def tables(earlier):
        ids, _ = after(route_ids, earlier)
        return route_tables(ids, route_weights, group, experts, groups)

    own_x, other_x, (slots, weights) = gather_blocks(*starts, tables)
    x = [piece for pair in zip(own_x, other_x) for piece in pair]
    invgain = (1.0 / norm_gain).reshape(groups * members, LANES)
    act, own_hidden, spread = gate_up(
        block_table(device, groups, member), slots, weights, invgain, x, w_gate, w_up, rows
    )

    cols = width // members

    def columns_of(to_core, chunk, chunks, orders):
        sides = jnp.stack([1 - x_side, x_side])
        blocks = (sides * 2 + to_core) * chunks + chunk
        places = [halving_places(to_core, group, groups, order) for order in orders]
        return jnp.concatenate([blocks] + places)

    chunks = len(ORDERS)
    chunk_cols = cols // chunks
    other = down(
        columns_of(1 - core, 0, 1, ORDERS), spread, act, w_down, rows, groups, cols, chunks
    )
    came = [flip(piece, lambda c: CORE) for piece in other]

    def terms_of(chunk, earlier):
        ready = act if earlier is None else after(act, earlier)[0]
        place = columns_of(core, chunk, chunks, ORDERS[chunk : chunk + 1])
        (kept,) = down(place, spread, ready, w_down, rows, groups, chunk_cols, 1)
        return [kept, came[chunk]]

    sums = reduce_chunks([functools.partial(terms_of, chunk) for chunk in range(chunks)])
    mixture = jnp.concatenate(sums, axis=1)
    return (own_hidden + mixture).astype(BF16)


def solution(mesh):
    groups, members = mesh.shape["expert"], mesh.shape["tensor"]
    placed = (
        P("expert", "tensor"),
        P("tensor", "expert"),
        P("expert", None),
        P(),
        P("expert", None),
        P("expert", None),
        P("expert", None, "tensor"),
        P("expert", None, "tensor"),
        P("expert", "tensor", None),
    )

    def run(*arrays):
        tokens, width = arrays[2].shape
        whole_tokens = (groups, members) == (8, 4) and width == groups * members * LANES
        body = per_device_tokens if whole_tokens else per_device_slots
        return jax.shard_map(
            body, mesh=mesh, in_specs=placed, out_specs=P("expert", "tensor"), check_vma=False
        )(*arrays)

    return run
```

```python
import functools

import jax
import jax.numpy as jnp
from jax import lax
from jax.experimental import pallas as pl
from jax.experimental.pallas import tpu as pltpu
from jax.sharding import PartitionSpec as P

EXPERTS = 64
CAP = 18
BF16 = jnp.bfloat16
F32 = jnp.float32
PAIR = 2
LANES = 128


def slot_places(ids, experts, capacity):
    row_count, top_count = ids.shape
    onehot = (ids[:, :, None] == jnp.arange(experts, dtype=jnp.int32)[None, None, :]).astype(
        jnp.int32
    )
    flattened = onehot.reshape(row_count * top_count, experts)
    before = jnp.cumsum(flattened, axis=0) - flattened
    slot_rank = jnp.sum(before * flattened, axis=1).reshape(row_count, top_count)
    return ids * capacity + slot_rank


def per_device_slots(
    attn_heads, out_proj, residual, norm_gain, route_ids, route_weights, w_gate, w_up, w_down
):
    model_width = residual.shape[1]
    groups = lax.axis_size("expert")
    members = lax.axis_size("tensor")
    member = lax.axis_index("tensor")
    per_group = w_gate.shape[0]
    slot_count = EXPERTS * CAP
    block_cols = model_width // members
    heads_out = jnp.dot(
        attn_heads,
        lax.all_gather(out_proj, "expert", axis=1, tiled=True),
        preferred_element_type=F32,
    )
    attn_out = lax.psum(heads_out.astype(BF16), "tensor").astype(F32)
    hidden = residual.astype(F32) + attn_out
    normed = (
        hidden * lax.rsqrt(jnp.mean(hidden * hidden, axis=-1, keepdims=True) + 1e-06) * norm_gain
    ).astype(BF16)
    slot_index = slot_places(route_ids, EXPERTS, CAP)
    slot_range = jnp.arange(slot_count, dtype=jnp.int32)
    slot_hits = jnp.sum(
        (slot_index[:, :, None] == slot_range[None, None, :]).astype(BF16), axis=1
    )
    buffer = jnp.einsum("rj,rd->jd", slot_hits, normed, preferred_element_type=F32).astype(BF16)
    buffer = buffer.reshape(groups, per_group, CAP, model_width)
    arrived = lax.all_to_all(buffer, "expert", split_axis=0, concat_axis=0, tiled=True)
    gate_acc = jnp.einsum("gxcd,xdf->gxcf", arrived, w_gate, preferred_element_type=F32)
    upper = jnp.einsum("gxcd,xdf->gxcf", arrived, w_up, preferred_element_type=F32)
    activation = (jax.nn.silu(gate_acc) * upper).astype(BF16)
    product_term = jnp.einsum("gxcf,xfd->gxcd", activation, w_down, preferred_element_type=F32)
    product_term = product_term.astype(BF16).reshape(groups, per_group, CAP, members, block_cols)
    expert_out = lax.psum_scatter(
        jnp.transpose(product_term, (3, 0, 1, 2, 4)), "tensor", scatter_dimension=0, tiled=True
    )[0]
    returned = lax.all_to_all(expert_out, "expert", split_axis=0, concat_axis=0, tiled=True)
    weights = route_weights / jnp.sum(route_weights, axis=-1, keepdims=True)
    picked = returned.reshape(slot_count, block_cols)[slot_index]
    mixture = jnp.sum(weights[:, :, None] * picked.astype(F32), axis=1)
    own_hidden = lax.dynamic_slice_in_dim(hidden, member * block_cols, block_cols, 1)
    return (own_hidden + mixture).astype(BF16)


def hits_of(slot_row, rows):
    places = lax.broadcasted_iota(jnp.int32, (rows, slot_row.shape[1]), 0)
    return places == slot_row


def project_kernel(info_ref, head_refs, weight_ref, send_ref, keep_ref):
    core, x_side = info_ref[0], info_ref[1]
    pieces = [ref.at[i] for ref in head_refs for i in range(ref.shape[0])]
    here = pieces[0].shape[0]
    each = len(pieces) // 2
    for part in range(2):
        result = jnp.dot(
            jnp.concatenate([ref[...] for ref in pieces[part * each : (part + 1) * each]]),
            weight_ref[...],
            preferred_element_type=F32,
        ).astype(BF16)
        for to_x in range(2):
            x_kept = (x_side == to_x).astype(jnp.int32)
            for to_core in range(2):
                start = (to_x * 2 + to_core) * LANES
                for out_ref, wanted in ((keep_ref, core == to_core), (send_ref, core != to_core)):

                    @pl.when(wanted)
                    def _(out_ref=out_ref, x_kept=x_kept, start=start, part=part, result=result):
                        for piece in range(each):
                            out_ref[x_kept, info_ref[2 + part * each + piece]] = result[
                                piece * here : (piece + 1) * here, start : start + LANES
                            ]


def project(info, pieces, out_proj):
    here = pieces[0].shape[1]
    groups = sum(piece.shape[0] for piece in pieces)
    out = jax.ShapeDtypeStruct((2, groups, here, LANES), BF16)
    vmem = pl.BlockSpec(memory_space=pltpu.VMEM)

    def kernel(info_ref, *refs):
        project_kernel(info_ref, refs[: len(pieces)], *refs[len(pieces) :])

    return pl.pallas_call(
        kernel,
        in_specs=[pl.BlockSpec(memory_space=pltpu.SMEM)] + [vmem] * (len(pieces) + 1),
        out_specs=[vmem, vmem],
        out_shape=[out, out],
        compiler_params=pltpu.CompilerParams(vmem_limit_bytes=24 * 1024 * 1024),
        cost_estimate=pl.CostEstimate(
            flops=2 * groups * here * out_proj.size,
            bytes_accessed=2 * (out_proj.size + 2 * groups * pieces[0][0].size),
            transcendentals=0,
        ),
        name="project",
    )(info, *pieces, out_proj)


def other_place(place):
    return (place >> 1) | ((place & 1) << 2)


def gate_up_kernel(
    experts, rows, width, info_ref, slot_ref, weight_ref, invgain_ref, x_refs, wg_ref, wu_ref,
    act_ref, hidden_ref, spread_ref, xs_ref, sq_ref, scale_ref, hits_ref
):
    expert = pl.program_id(0)
    arrays = len(x_refs) // 2
    each, parts, here, lanes = x_refs[0].shape
    blocks = arrays * each
    span = 2 * here
    member, z = info_ref[2 * blocks], info_ref[2 * blocks + 1]

    @pl.when(expert == 0)
    def _():
        sq_ref[...] = jnp.zeros_like(sq_ref)
        for part in range(parts):
            for e in range(experts):
                first = hits_of(slot_ref[e : e + 1, part * span : part * span + here], rows)
                second = hits_of(
                    slot_ref[e : e + 1, part * span + here : (part + 1) * span], rows
                )
                first = first.astype(F32).astype(BF16)
                second = second.astype(F32).astype(BF16)
                window = slice(e * rows, (e + 1) * rows)
                hits_ref[0, part, window, :] = jnp.concatenate([first, second], axis=1)
                hits_ref[1, part, window, :] = jnp.concatenate([second, first], axis=1)
            spread_ref[part] = jnp.transpose(hits_ref[0, part].astype(F32)).astype(BF16)

        def pair_of_blocks(low, carry):
            for array in range(arrays):
                own, other = x_refs[2 * array], x_refs[2 * array + 1]
                swapped = info_ref[blocks + array * each + low]
                places = (low, low + each // 2)
                features = [info_ref[array * each + place] for place in places]
                for place, feature in zip(places, features):
                    invgain = invgain_ref[pl.ds(feature, 1), :]
                    for part in range(parts):
                        for half, block in enumerate(
                            (own[place, part], other[other_place(place), part])
                        ):
                            value = block.astype(F32) * invgain
                            sq_ref[swapped, part, half] += value * value

                for part in range(parts):
                    both = jnp.concatenate(
                        [
                            jnp.concatenate([own[place, part], other[other_place(place), part]])
                            for place in places
                        ],
                        axis=1,
                    )
                    picked = jnp.dot(
                        hits_ref[swapped, part], both, preferred_element_type=F32
                    ).astype(BF16)
                    for number, feature in enumerate(features):
                        column = pl.multiple_of(feature * lanes, lanes)
                        for e in range(experts):
                            xs_ref[e, part * rows : (part + 1) * rows, pl.ds(column, lanes)] = (
                                picked[
                                    e * rows : (e + 1) * rows, number * lanes : (number + 1) * lanes
                                ]
                            )
            return carry

        lax.fori_loop(0, each // 2, pair_of_blocks, 0)

        def own_block(place, carry):
            for array in range(arrays):
                feature = info_ref[array * each + place]

                @pl.when(feature >> 3 == member)
                def _(array=array, feature=feature):
                    own, other = x_refs[2 * array], x_refs[2 * array + 1]
                    mine = jnp.where(
                        info_ref[blocks + array * each + place] == 0,
                        own[place, z].astype(F32),
                        other[other_place(place), z].astype(F32),
                    )
                    column = pl.multiple_of((feature & 7) * lanes, lanes)
                    hidden_ref[:, pl.ds(column, lanes)] = mine * invgain_ref[pl.ds(feature, 1), :]

            return carry

        lax.fori_loop(0, each, own_block, 0)
        pieces = [
            sq_ref[0, part, half] + sq_ref[1, part, 1 - half]
            for part in range(parts)
            for half in range(2)
        ]
        total = jnp.sum(
            jnp.transpose(jnp.concatenate(pieces, axis=0)), axis=0, keepdims=True
        )
        scale_ref[...] = jnp.broadcast_to(lax.rsqrt(total / width + 1e-06), scale_ref.shape)

    summed = jnp.dot(
        xs_ref[expert],
        jnp.concatenate([wg_ref[0], wu_ref[0]], axis=1),
        preferred_element_type=F32,
    )
    hidden_units = wg_ref.shape[2]
    for part in range(parts):
        window = slice(part * span, (part + 1) * span)
        hits = hits_of(slot_ref[pl.ds(expert, 1), window], rows)
        scale = jnp.sum(jnp.where(hits, scale_ref[0:1, window], 0.0), axis=1, keepdims=True)
        weight = jnp.sum(
            jnp.where(hits, weight_ref[pl.ds(expert, 1), window], 0.0), axis=1, keepdims=True
        )
        both_part = summed[part * rows : (part + 1) * rows, :]
        gate = both_part[:, :hidden_units] * scale
        upper = both_part[:, hidden_units:] * scale
        act = gate / (1.0 + jnp.exp(-gate)) * upper * weight
        act_ref[expert, part * rows : (part + 1) * rows, :] = act.astype(BF16)


def gate_up(info, slots, weights, invgain, x, w_gate, w_up, rows):
    experts, width, hidden_units = w_gate.shape
    each, parts, here, lanes = x[0].shape
    tokens = slots.shape[1]
    members = width // (each * lanes)

    def kernel(info_ref, slot_ref, weight_ref, invgain_ref, *rest):
        gate_up_kernel(
            experts, rows, width, info_ref, slot_ref, weight_ref, invgain_ref,
            rest[: len(x)], *rest[len(x) :]
        )

    def whole(shape):
        return pl.BlockSpec(
            shape, lambda e, info: (0,) * len(shape), pipeline_mode=pl.Buffered(1)
        )

    return pl.pallas_call(
        kernel,
        grid_spec=pltpu.PrefetchScalarGridSpec(
            num_scalar_prefetch=1,
            grid=(experts,),
            in_specs=[whole(slots.shape), whole(weights.shape), whole(invgain.shape)]
            + [pl.BlockSpec(memory_space=pltpu.VMEM)] * len(x)
            + [pl.BlockSpec((1, width, hidden_units), lambda e, info: (e, 0, 0))] * 2,
            out_specs=[
                pl.BlockSpec(memory_space=pltpu.VMEM),
                pl.BlockSpec(memory_space=pltpu.VMEM),
                pl.BlockSpec(memory_space=pltpu.VMEM),
            ],
            scratch_shapes=[
                pltpu.VMEM((experts, parts * rows, width), BF16),
                pltpu.VMEM((2, parts, 2, here, lanes), F32),
                pltpu.VMEM((8, tokens), F32),
                pltpu.VMEM((2, parts, experts * rows, 2 * here), BF16),
            ],
        ),
        out_shape=[
            jax.ShapeDtypeStruct((experts, parts * rows, hidden_units), BF16),
            jax.ShapeDtypeStruct((here, width // members), F32),
            jax.ShapeDtypeStruct((parts, 2 * here, experts * rows), BF16),
        ],
        compiler_params=pltpu.CompilerParams(
            vmem_limit_bytes=36 * 1024 * 1024, dimension_semantics=("arbitrary",)
        ),
        cost_estimate=pl.CostEstimate(
            flops=2 * experts * parts * rows * width * 2 * hidden_units,
            bytes_accessed=4 * experts * width * hidden_units + 2 * len(x) * x[0].size,
            transcendentals=0,
        ),
        name="gate_up",
    )(info, slots, weights, invgain, *x, w_gate, w_up)


def down_kernel(rows, place_ref, spread_ref, act_ref, wd0_ref, wd1_ref, *rest):
    out_refs, ys_ref = rest[:-1], rest[-1]
    out_cols = out_refs[0].shape[2]
    step = pl.program_id(0)
    experts, all_rows, _ = act_ref.shape
    per_step = wd0_ref.shape[0]
    parts = all_rows // rows
    groups = parts * PAIR
    for number in range(per_step):
        expert = step * per_step + number
        for side, wd_ref in enumerate((wd0_ref, wd1_ref)):
            result = jnp.dot(
                act_ref[expert], wd_ref[number], preferred_element_type=F32
            ).astype(BF16)
            for part in range(parts):
                ys_ref[side, part, expert] = result[part * rows : (part + 1) * rows, :]

    @pl.when(step == pl.num_programs(0) - 1)
    def _():
        for part in range(parts):
            for side in range(2):
                picked = ys_ref[side, part].reshape(experts * rows, ys_ref.shape[4])
                mixed = jnp.dot(
                    spread_ref[part], picked, preferred_element_type=F32
                ).astype(BF16)
                for i in range(PAIR):
                    for number, out_ref in enumerate(out_refs):
                        block = (number * 2 + side) * groups + part * PAIR + i
                        target = place_ref[2 + block]
                        out_ref[target] = mixed[
                            i * 128 : (i + 1) * 128, number * out_cols : (number + 1) * out_cols
                        ]


def down(place, spread, act, w_down, rows, groups, cols, chunks, per_step=2):
    experts, hidden_units, width = w_down.shape
    parts, span, _ = spread.shape
    here = parts * span // groups
    out = jax.ShapeDtypeStruct((2 * groups, here, cols // chunks), BF16)
    return pl.pallas_call(
        functools.partial(down_kernel, rows),
        grid_spec=pltpu.PrefetchScalarGridSpec(
            num_scalar_prefetch=1,
            grid=(experts // per_step,),
            in_specs=[
                pl.BlockSpec(memory_space=pltpu.VMEM),
                pl.BlockSpec(memory_space=pltpu.VMEM),
                pl.BlockSpec((per_step, hidden_units, cols), lambda e, p: (e, 0, p[0])),
                pl.BlockSpec((per_step, hidden_units, cols), lambda e, p: (e, 0, p[1])),
            ],
            out_specs=[pl.BlockSpec(out.shape, lambda e, p: (0, 0, 0))] * chunks,
            scratch_shapes=[pltpu.VMEM((2, parts, experts, rows, cols), BF16)],
        ),
        out_shape=[out] * chunks,
        compiler_params=pltpu.CompilerParams(
            vmem_limit_bytes=36 * 1024 * 1024, dimension_semantics=("arbitrary",)
        ),
        cost_estimate=pl.CostEstimate(
            flops=8 * experts * parts * rows * cols * hidden_units,
            bytes_accessed=4 * experts * cols * hidden_units + 4 * parts * span * cols,
            transcendentals=0,
        ),
        name="down_mix",
    )(place, spread, act, w_down, w_down)


def flip(array, bits_of):
    pairs = []
    for index in range(32):
        pairs.append((index, index ^ bits_of(index & 1)))
    return lax.ppermute(array, ("expert", "tensor"), pairs)


CORE, X, Y, ZLOW, ZHIGH = 1, 2, 4, 8, 16


def first_axis(core):
    return Y if core else X


def last_axis(core):
    return X if core else Y


def own_order(groups, group):
    order = jnp.arange(groups, dtype=jnp.int32)
    return order ^ (group & 1)


HALVING = {
    "first": first_axis,
    "last": last_axis,
    "low": lambda core: ZLOW,
    "high": lambda core: ZHIGH,
}
ORDERS = (("first", "low", "high", "last"), ("first", "last", "low", "high"))


def halving_places(to_core, group, groups, order):
    g = own_order(groups, group)[None, :]
    y_kept = ((g & 1) == (group & 1)).astype(jnp.int32)
    x_kept = jnp.arange(2, dtype=jnp.int32)[:, None]
    kept = {
        "first": jnp.where(to_core == 0, x_kept, y_kept),
        "last": jnp.where(to_core == 0, y_kept, x_kept),
        "low": (((g >> 1) & 1) == ((group >> 1) & 1)).astype(jnp.int32),
        "high": ((g >> 2) == (group >> 2)).astype(jnp.int32),
    }
    place = 0
    for axis in order:
        place = place * 2 + kept[axis]
    return place.reshape(-1)


def total_of(terms):
    total = terms[0].astype(F32)
    for term in terms[1:]:
        total = total + term.astype(F32)
    return total


def after(value, earlier):
    return lax.optimization_barrier((value, earlier))


def reduce_chunks(makers):
    terms, came = [None, None], {}

    def exchange(chunk, stage, earlier=None):
        half = terms[chunk][0].shape[0] // 2
        sent = total_of([term[:half] for term in terms[chunk]]).astype(BF16)
        if earlier is not None:
            sent, _ = after(sent, earlier)
        came[chunk, stage] = flip(sent, HALVING[ORDERS[chunk][stage]])
        terms[chunk] = [term[half:] for term in terms[chunk]] + [came[chunk, stage]]
        return sent

    terms[0] = makers[0](None)
    terms[1] = makers[1](exchange(0, 0))
    exchange(1, 0, came[0, 0])
    exchange(0, 1)
    exchange(1, 1, came[0, 1])
    exchange(0, 2)
    exchange(1, 2, came[0, 2])
    exchange(0, 3, came[1, 2])
    exchange(1, 3)
    return [total_of([term[0] for term in chunk]) for chunk in terms]


HEAD_STAGES = (
    lambda core: ZHIGH if core else Y,
    lambda core: ZLOW if core else ZHIGH,
    lambda core: Y if core else ZLOW,
)


def head_bits(place, core):
    bits = [(place >> stage) & 1 for stage in range(3)]
    return jnp.where(
        core == 0,
        bits[0] | (bits[1] << 2) | (bits[2] << 1),
        (bits[0] << 2) | (bits[1] << 1) | bits[2],
    )


def gather_heads(heads):
    heads = heads[None]
    for number, bits_of in enumerate(HEAD_STAGES):
        came = flip(heads, bits_of)
        if number == len(HEAD_STAGES) - 1:
            return [heads, came]
        heads = jnp.concatenate([heads, came], axis=0)


def route_table(route_ids, route_weights):
    shares = route_weights / jnp.sum(route_weights, axis=-1, keepdims=True)
    return jnp.concatenate([route_ids.astype(F32), shares], axis=1).T


def own_routes(table, group, experts):
    groups, both, here = table.shape
    top = both // 2
    own = group * experts + jnp.arange(experts, dtype=jnp.int32)
    ids = table[:, :top, :].astype(jnp.int32)
    match = ids[None] == own[:, None, None, None]
    named = jnp.any(match, axis=2)
    weights = jnp.sum(jnp.where(match, table[None, :, top:, :], 0.0), axis=2)
    span = PAIR * here
    order = jnp.arange(span)
    earlier = (order[:, None] < order[None, :]).astype(BF16)
    rank = jnp.dot(
        named.astype(BF16).reshape(experts * groups // PAIR, span),
        earlier,
        preferred_element_type=F32,
    )
    slots = jnp.where(named, rank.reshape(named.shape).astype(jnp.int32), -1)
    return slots.reshape(experts, groups * here), weights.reshape(experts, groups * here)


def block_table(device, groups, member):
    number = jnp.arange(32, dtype=jnp.int32)
    array, place = number >> 3, number & 7
    source_core = (device & 1) ^ (array >> 1)
    first = jnp.where(source_core == 0, X, Y)
    last = jnp.where(source_core == 0, Y, X)
    feature = (
        device
        ^ (array >> 1)
        ^ jnp.where(array & 1 == 1, first, 0)
        ^ jnp.where(place & 1 == 1, last, 0)
        ^ jnp.where(place & 2 == 2, ZHIGH, 0)
        ^ jnp.where(place & 4 == 4, ZLOW, 0)
    )
    swapped = ((feature ^ device) >> 2) & 1
    return jnp.concatenate([feature, swapped, jnp.stack([member, device >> 3])])


def gather_blocks(first, second, make_table, own_tables):
    def along(bits, block):
        return flip(block, lambda core: bits)

    def joined(held, came):
        return jnp.concatenate([held, came], axis=0)

    first_last = flip(first, last_axis)
    second_high = along(ZHIGH, second)
    second, _ = after(joined(second, second_high), first_last)
    second_low = along(ZLOW, second)
    first, _ = after(joined(first, first_last), second_high)
    first_high = along(ZHIGH, first)
    table = make_table(second_high)
    for bits in (ZHIGH, ZLOW, Y):
        table = joined(table, along(bits, table))
    second = joined(second, second_low)
    second_last = flip(second, last_axis)
    first = joined(first, first_high)
    first_low = along(ZLOW, first)
    second = joined(second, second_last)
    second_first = flip(second, first_axis)
    first_low, _ = after(first_low, second)
    beside = own_tables(table)
    first, (second_first, beside) = after(joined(first, first_low), (second_first, beside))
    first_first = flip(first, first_axis)
    return [
        [block, came, along(CORE, block), along(CORE, came)]
        for block, came in ((first, first_first), (second, second_first))
    ] + [beside]


def per_device_tokens(
    attn_heads, out_proj, residual, norm_gain, route_ids, route_weights, w_gate, w_up, w_down
):
    groups, members = lax.axis_size("expert"), lax.axis_size("tensor")
    group, member = lax.axis_index("expert"), lax.axis_index("tensor")
    device = group * members + member
    here, width = residual.shape
    experts = w_gate.shape[0]
    rows = -(-PAIR * CAP // 16) * 16
    x_side, core, y_side = member >> 1, member & 1, group & 1

    own_cols = lax.dynamic_index_in_dim(
        residual.reshape(here, groups, members, LANES), member, 2, keepdims=False
    )
    moved = lax.all_to_all(
        jnp.transpose(own_cols, (1, 0, 2)), "expert", split_axis=0, concat_axis=0, tiled=True
    ).reshape(groups // 2, 2, here, LANES)
    gain = lax.dynamic_index_in_dim(
        norm_gain.reshape(groups * members, LANES), device, 0, keepdims=False
    )

    pieces = gather_heads(attn_heads)
    numbers = jnp.arange(groups, dtype=jnp.int32)
    arrival = (head_bits(numbers, core) ^ group) ^ y_side
    info = jnp.concatenate(
        [jnp.stack([core, x_side]), ((arrival & 1) << 2) | (arrival >> 1)]
    )
    info, moved = after(info, moved)
    send, keep = project(info, pieces, out_proj)
    came = flip(send, lambda c: CORE)
    from_x = flip(total_of([keep[0], came[0]]).astype(BF16), lambda c: X)
    starts = []
    each = groups // 2
    for half in range(2):
        window = slice(half * each, (half + 1) * each)
        hidden = lax.dynamic_index_in_dim(moved, y_side ^ half, 1, keepdims=False).astype(F32)
        hidden = hidden + total_of([keep[1, window], came[1, window], from_x[window]])
        starts.append((hidden * gain).astype(BF16)[None])

    def make_table(earlier):
        ids, _ = after(route_ids, earlier)
        return route_table(ids, route_weights)[None]

    def own_tables(table):
        apart = own_order(groups, group) ^ group
        order = (apart >> 2) | (apart & 2) | ((apart & 1) << 2)
        return own_routes(jnp.take(table, order, axis=0, mode="clip"), group, experts)

    own_x, other_x, (slots, weights) = gather_blocks(*starts, make_table, own_tables)
    x = [piece for pair in zip(own_x, other_x) for piece in pair]
    invgain = (1.0 / norm_gain).reshape(groups * members, LANES)
    act, own_hidden, spread = gate_up(
        block_table(device, groups, member), slots, weights, invgain, x, w_gate, w_up, rows
    )

    cols = width // members

    def columns_of(to_core, chunk, chunks, orders):
        sides = jnp.stack([1 - x_side, x_side])
        blocks = (sides * 2 + to_core) * chunks + chunk
        places = [halving_places(to_core, group, groups, order) for order in orders]
        return jnp.concatenate([blocks] + places)

    chunks = len(ORDERS)
    chunk_cols = cols // chunks
    other = down(
        columns_of(1 - core, 0, 1, ORDERS), spread, act, w_down, rows, groups, cols, chunks
    )
    came = [flip(piece, lambda c: CORE) for piece in other]

    def terms_of(chunk, earlier):
        place = columns_of(core, chunk, chunks, ORDERS[chunk : chunk + 1])
        if earlier is not None:
            place, _ = after(place, earlier)
        (kept,) = down(place, spread, act, w_down, rows, groups, chunk_cols, 1)
        return [kept, came[chunk]]

    sums = reduce_chunks([functools.partial(terms_of, chunk) for chunk in range(chunks)])
    mixture = jnp.concatenate(sums, axis=1)
    return (own_hidden + mixture).astype(BF16)


def solution(mesh):
    groups, members = mesh.shape["expert"], mesh.shape["tensor"]
    placed = (
        P("expert", "tensor"),
        P("tensor", "expert"),
        P("expert", None),
        P(),
        P("expert", None),
        P("expert", None),
        P("expert", None, "tensor"),
        P("expert", None, "tensor"),
        P("expert", "tensor", None),
    )

    def run(*arrays):
        tokens, width = arrays[2].shape
        whole_tokens = (groups, members) == (8, 4) and width == groups * members * LANES
        body = per_device_tokens if whole_tokens else per_device_slots
        return jax.shard_map(
            body, mesh=mesh, in_specs=placed, out_specs=P("expert", "tensor"), check_vma=False
        )(*arrays)

    return run
```

```python
import functools

import jax
import jax.numpy as jnp
from jax import lax
from jax.experimental import pallas as pl
from jax.experimental.pallas import tpu as pltpu
from jax.sharding import PartitionSpec as P

EXPERTS = 64
CAP = 18
BF16 = jnp.bfloat16
F32 = jnp.float32
PAIR = 2
LANES = 128


def slot_places(ids, experts, capacity):
    row_count, top_count = ids.shape
    onehot = (ids[:, :, None] == jnp.arange(experts, dtype=jnp.int32)[None, None, :]).astype(
        jnp.int32
    )
    flattened = onehot.reshape(row_count * top_count, experts)
    before = jnp.cumsum(flattened, axis=0) - flattened
    slot_rank = jnp.sum(before * flattened, axis=1).reshape(row_count, top_count)
    return ids * capacity + slot_rank


def per_device_slots(
    attn_heads, out_proj, residual, norm_gain, route_ids, route_weights, w_gate, w_up, w_down
):
    model_width = residual.shape[1]
    groups = lax.axis_size("expert")
    members = lax.axis_size("tensor")
    member = lax.axis_index("tensor")
    per_group = w_gate.shape[0]
    slot_count = EXPERTS * CAP
    block_cols = model_width // members
    heads_out = jnp.dot(
        attn_heads,
        lax.all_gather(out_proj, "expert", axis=1, tiled=True),
        preferred_element_type=F32,
    )
    attn_out = lax.psum(heads_out.astype(BF16), "tensor").astype(F32)
    hidden = residual.astype(F32) + attn_out
    normed = (
        hidden * lax.rsqrt(jnp.mean(hidden * hidden, axis=-1, keepdims=True) + 1e-06) * norm_gain
    ).astype(BF16)
    slot_index = slot_places(route_ids, EXPERTS, CAP)
    slot_range = jnp.arange(slot_count, dtype=jnp.int32)
    slot_hits = jnp.sum(
        (slot_index[:, :, None] == slot_range[None, None, :]).astype(BF16), axis=1
    )
    buffer = jnp.einsum("rj,rd->jd", slot_hits, normed, preferred_element_type=F32).astype(BF16)
    buffer = buffer.reshape(groups, per_group, CAP, model_width)
    arrived = lax.all_to_all(buffer, "expert", split_axis=0, concat_axis=0, tiled=True)
    gate_acc = jnp.einsum("gxcd,xdf->gxcf", arrived, w_gate, preferred_element_type=F32)
    upper = jnp.einsum("gxcd,xdf->gxcf", arrived, w_up, preferred_element_type=F32)
    activation = (jax.nn.silu(gate_acc) * upper).astype(BF16)
    product_term = jnp.einsum("gxcf,xfd->gxcd", activation, w_down, preferred_element_type=F32)
    product_term = product_term.astype(BF16).reshape(groups, per_group, CAP, members, block_cols)
    expert_out = lax.psum_scatter(
        jnp.transpose(product_term, (3, 0, 1, 2, 4)), "tensor", scatter_dimension=0, tiled=True
    )[0]
    returned = lax.all_to_all(expert_out, "expert", split_axis=0, concat_axis=0, tiled=True)
    weights = route_weights / jnp.sum(route_weights, axis=-1, keepdims=True)
    picked = returned.reshape(slot_count, block_cols)[slot_index]
    mixture = jnp.sum(weights[:, :, None] * picked.astype(F32), axis=1)
    own_hidden = lax.dynamic_slice_in_dim(hidden, member * block_cols, block_cols, 1)
    return (own_hidden + mixture).astype(BF16)


def hits_of(slot_row, rows):
    places = lax.broadcasted_iota(jnp.int32, (rows, slot_row.shape[1]), 0)
    return places == slot_row


def project_kernel(info_ref, head_refs, weight_ref, send_ref, keep_ref):
    core, x_side = info_ref[0], info_ref[1]
    pieces = [ref.at[i] for ref in head_refs for i in range(ref.shape[0])]
    here = pieces[0].shape[0]
    each = len(pieces) // 2
    for part in range(2):
        result = jnp.dot(
            jnp.concatenate([ref[...] for ref in pieces[part * each : (part + 1) * each]]),
            weight_ref[...],
            preferred_element_type=F32,
        ).astype(BF16)
        for to_x in range(2):
            x_kept = (x_side == to_x).astype(jnp.int32)
            for to_core in range(2):
                start = (to_x * 2 + to_core) * LANES
                for out_ref, wanted in ((keep_ref, core == to_core), (send_ref, core != to_core)):

                    @pl.when(wanted)
                    def _(out_ref=out_ref, x_kept=x_kept, start=start, part=part, result=result):
                        for piece in range(each):
                            out_ref[x_kept, info_ref[2 + part * each + piece]] = result[
                                piece * here : (piece + 1) * here, start : start + LANES
                            ]


def project(info, pieces, out_proj):
    here = pieces[0].shape[1]
    groups = sum(piece.shape[0] for piece in pieces)
    out = jax.ShapeDtypeStruct((2, groups, here, LANES), BF16)
    vmem = pl.BlockSpec(memory_space=pltpu.VMEM)

    def kernel(info_ref, *refs):
        project_kernel(info_ref, refs[: len(pieces)], *refs[len(pieces) :])

    return pl.pallas_call(
        kernel,
        in_specs=[pl.BlockSpec(memory_space=pltpu.SMEM)] + [vmem] * (len(pieces) + 1),
        out_specs=[vmem, vmem],
        out_shape=[out, out],
        compiler_params=pltpu.CompilerParams(vmem_limit_bytes=24 * 1024 * 1024),
        cost_estimate=pl.CostEstimate(
            flops=2 * groups * here * out_proj.size,
            bytes_accessed=2 * (out_proj.size + 2 * groups * pieces[0][0].size),
            transcendentals=0,
        ),
        name="project",
    )(info, *pieces, out_proj)


def other_place(place):
    return (place >> 1) | ((place & 1) << 2)


def gate_up_kernel(
    experts, rows, width, info_ref, slot_ref, weight_ref, invgain_ref, x_refs, wg_ref, wu_ref,
    act_ref, hidden_ref, spread_ref, xs_ref, sq_ref, scale_ref, hits_ref
):
    expert = pl.program_id(0)
    arrays = len(x_refs) // 2
    each, parts, here, lanes = x_refs[0].shape
    blocks = arrays * each
    span = 2 * here
    member, z = info_ref[2 * blocks], info_ref[2 * blocks + 1]

    @pl.when(expert == 0)
    def _():
        sq_ref[...] = jnp.zeros_like(sq_ref)
        for part in range(parts):
            for e in range(experts):
                first = hits_of(slot_ref[e : e + 1, part * span : part * span + here], rows)
                second = hits_of(
                    slot_ref[e : e + 1, part * span + here : (part + 1) * span], rows
                )
                first = first.astype(F32).astype(BF16)
                second = second.astype(F32).astype(BF16)
                window = slice(e * rows, (e + 1) * rows)
                hits_ref[0, part, window, :] = jnp.concatenate([first, second], axis=1)
                hits_ref[1, part, window, :] = jnp.concatenate([second, first], axis=1)
            spread_ref[part] = jnp.transpose(hits_ref[0, part].astype(F32)).astype(BF16)

        def pair_of_blocks(low, carry):
            for array in range(arrays):
                own, other = x_refs[2 * array], x_refs[2 * array + 1]
                swapped = info_ref[blocks + array * each + low]
                places = (low, low + each // 2)
                features = [info_ref[array * each + place] for place in places]
                for place, feature in zip(places, features):
                    invgain = invgain_ref[pl.ds(feature, 1), :]
                    for part in range(parts):
                        for half, block in enumerate(
                            (own[place, part], other[other_place(place), part])
                        ):
                            value = block.astype(F32) * invgain
                            sq_ref[swapped, part, half] += value * value

                for part in range(parts):
                    both = jnp.concatenate(
                        [
                            jnp.concatenate([own[place, part], other[other_place(place), part]])
                            for place in places
                        ],
                        axis=1,
                    )
                    picked = jnp.dot(
                        hits_ref[swapped, part], both, preferred_element_type=F32
                    ).astype(BF16)
                    for number, feature in enumerate(features):
                        column = pl.multiple_of(feature * lanes, lanes)
                        for e in range(experts):
                            xs_ref[e, part * rows : (part + 1) * rows, pl.ds(column, lanes)] = (
                                picked[
                                    e * rows : (e + 1) * rows, number * lanes : (number + 1) * lanes
                                ]
                            )
            return carry

        lax.fori_loop(0, each // 2, pair_of_blocks, 0)

        def own_block(place, carry):
            for array in range(arrays):
                feature = info_ref[array * each + place]

                @pl.when(feature >> 3 == member)
                def _(array=array, feature=feature):
                    own, other = x_refs[2 * array], x_refs[2 * array + 1]
                    mine = jnp.where(
                        info_ref[blocks + array * each + place] == 0,
                        own[place, z].astype(F32),
                        other[other_place(place), z].astype(F32),
                    )
                    column = pl.multiple_of((feature & 7) * lanes, lanes)
                    hidden_ref[:, pl.ds(column, lanes)] = mine * invgain_ref[pl.ds(feature, 1), :]

            return carry

        lax.fori_loop(0, each, own_block, 0)
        pieces = [
            sq_ref[0, part, half] + sq_ref[1, part, 1 - half]
            for part in range(parts)
            for half in range(2)
        ]
        total = jnp.sum(
            jnp.transpose(jnp.concatenate(pieces, axis=0)), axis=0, keepdims=True
        )
        scale_ref[...] = jnp.broadcast_to(lax.rsqrt(total / width + 1e-06), scale_ref.shape)

    summed = jnp.dot(
        xs_ref[expert],
        jnp.concatenate([wg_ref[0], wu_ref[0]], axis=1),
        preferred_element_type=F32,
    )
    hidden_units = wg_ref.shape[2]
    for part in range(parts):
        window = slice(part * span, (part + 1) * span)
        hits = hits_of(slot_ref[pl.ds(expert, 1), window], rows)
        scale = jnp.sum(jnp.where(hits, scale_ref[0:1, window], 0.0), axis=1, keepdims=True)
        weight = jnp.sum(
            jnp.where(hits, weight_ref[pl.ds(expert, 1), window], 0.0), axis=1, keepdims=True
        )
        both_part = summed[part * rows : (part + 1) * rows, :]
        gate = both_part[:, :hidden_units] * scale
        upper = both_part[:, hidden_units:] * scale
        act = gate / (1.0 + jnp.exp(-gate)) * upper * weight
        act_ref[expert, part * rows : (part + 1) * rows, :] = act.astype(BF16)


def gate_up(info, slots, weights, invgain, x, w_gate, w_up, rows):
    experts, width, hidden_units = w_gate.shape
    each, parts, here, lanes = x[0].shape
    tokens = slots.shape[1]
    members = width // (each * lanes)

    def kernel(info_ref, slot_ref, weight_ref, invgain_ref, *rest):
        gate_up_kernel(
            experts, rows, width, info_ref, slot_ref, weight_ref, invgain_ref,
            rest[: len(x)], *rest[len(x) :]
        )

    def whole(shape):
        return pl.BlockSpec(
            shape, lambda e, info: (0,) * len(shape), pipeline_mode=pl.Buffered(1)
        )

    return pl.pallas_call(
        kernel,
        grid_spec=pltpu.PrefetchScalarGridSpec(
            num_scalar_prefetch=1,
            grid=(experts,),
            in_specs=[whole(slots.shape), whole(weights.shape), whole(invgain.shape)]
            + [pl.BlockSpec(memory_space=pltpu.VMEM)] * len(x)
            + [pl.BlockSpec((1, width, hidden_units), lambda e, info: (e, 0, 0))] * 2,
            out_specs=[
                pl.BlockSpec(memory_space=pltpu.VMEM),
                pl.BlockSpec(memory_space=pltpu.VMEM),
                pl.BlockSpec(memory_space=pltpu.VMEM),
            ],
            scratch_shapes=[
                pltpu.VMEM((experts, parts * rows, width), BF16),
                pltpu.VMEM((2, parts, 2, here, lanes), F32),
                pltpu.VMEM((8, tokens), F32),
                pltpu.VMEM((2, parts, experts * rows, 2 * here), BF16),
            ],
        ),
        out_shape=[
            jax.ShapeDtypeStruct((experts, parts * rows, hidden_units), BF16),
            jax.ShapeDtypeStruct((here, width // members), F32),
            jax.ShapeDtypeStruct((parts, 2 * here, experts * rows), BF16),
        ],
        compiler_params=pltpu.CompilerParams(
            vmem_limit_bytes=36 * 1024 * 1024, dimension_semantics=("arbitrary",)
        ),
        cost_estimate=pl.CostEstimate(
            flops=2 * experts * parts * rows * width * 2 * hidden_units,
            bytes_accessed=4 * experts * width * hidden_units + 2 * len(x) * x[0].size,
            transcendentals=0,
        ),
        name="gate_up",
    )(info, slots, weights, invgain, *x, w_gate, w_up)


def down_kernel(rows, place_ref, spread_ref, act_ref, wd0_ref, wd1_ref, *rest):
    out_refs, ys_ref = rest[:-1], rest[-1]
    out_cols = out_refs[0].shape[2]
    step = pl.program_id(0)
    experts, all_rows, _ = act_ref.shape
    per_step = wd0_ref.shape[0]
    parts = all_rows // rows
    groups = parts * PAIR
    for number in range(per_step):
        expert = step * per_step + number
        for side, wd_ref in enumerate((wd0_ref, wd1_ref)):
            result = jnp.dot(
                act_ref[expert], wd_ref[number], preferred_element_type=F32
            ).astype(BF16)
            for part in range(parts):
                ys_ref[side, part, expert] = result[part * rows : (part + 1) * rows, :]

    @pl.when(step == pl.num_programs(0) - 1)
    def _():
        for part in range(parts):
            for side in range(2):
                picked = ys_ref[side, part].reshape(experts * rows, ys_ref.shape[4])
                mixed = jnp.dot(
                    spread_ref[part], picked, preferred_element_type=F32
                ).astype(BF16)
                for i in range(PAIR):
                    for number, out_ref in enumerate(out_refs):
                        block = (number * 2 + side) * groups + part * PAIR + i
                        target = place_ref[2 + block]
                        out_ref[target] = mixed[
                            i * 128 : (i + 1) * 128, number * out_cols : (number + 1) * out_cols
                        ]


def down(place, spread, act, w_down, rows, groups, cols, chunks, per_step=2):
    experts, hidden_units, width = w_down.shape
    parts, span, _ = spread.shape
    here = parts * span // groups
    out = jax.ShapeDtypeStruct((2 * groups, here, cols // chunks), BF16)
    return pl.pallas_call(
        functools.partial(down_kernel, rows),
        grid_spec=pltpu.PrefetchScalarGridSpec(
            num_scalar_prefetch=1,
            grid=(experts // per_step,),
            in_specs=[
                pl.BlockSpec(memory_space=pltpu.VMEM),
                pl.BlockSpec(memory_space=pltpu.VMEM),
                pl.BlockSpec((per_step, hidden_units, cols), lambda e, p: (e, 0, p[0])),
                pl.BlockSpec((per_step, hidden_units, cols), lambda e, p: (e, 0, p[1])),
            ],
            out_specs=[pl.BlockSpec(out.shape, lambda e, p: (0, 0, 0))] * chunks,
            scratch_shapes=[pltpu.VMEM((2, parts, experts, rows, cols), BF16)],
        ),
        out_shape=[out] * chunks,
        compiler_params=pltpu.CompilerParams(
            vmem_limit_bytes=36 * 1024 * 1024, dimension_semantics=("arbitrary",)
        ),
        cost_estimate=pl.CostEstimate(
            flops=8 * experts * parts * rows * cols * hidden_units,
            bytes_accessed=4 * experts * cols * hidden_units + 4 * parts * span * cols,
            transcendentals=0,
        ),
        name="down_mix",
    )(place, spread, act, w_down, w_down)


def flip(array, bits_of):
    pairs = []
    for index in range(32):
        pairs.append((index, index ^ bits_of(index & 1)))
    return lax.ppermute(array, ("expert", "tensor"), pairs)


CORE, X, Y, ZLOW, ZHIGH = 1, 2, 4, 8, 16


def first_axis(core):
    return Y if core else X


def last_axis(core):
    return X if core else Y


def own_order(groups, group):
    order = jnp.arange(groups, dtype=jnp.int32)
    return order ^ (group & 1)


HALVING = {
    "first": first_axis,
    "last": last_axis,
    "low": lambda core: ZLOW,
    "high": lambda core: ZHIGH,
}
ORDERS = (("first", "low", "high", "last"), ("first", "last", "low", "high"))


def halving_places(to_core, group, groups, order):
    g = own_order(groups, group)[None, :]
    y_kept = ((g & 1) == (group & 1)).astype(jnp.int32)
    x_kept = jnp.arange(2, dtype=jnp.int32)[:, None]
    kept = {
        "first": jnp.where(to_core == 0, x_kept, y_kept),
        "last": jnp.where(to_core == 0, y_kept, x_kept),
        "low": (((g >> 1) & 1) == ((group >> 1) & 1)).astype(jnp.int32),
        "high": ((g >> 2) == (group >> 2)).astype(jnp.int32),
    }
    place = 0
    for axis in order:
        place = place * 2 + kept[axis]
    return place.reshape(-1)


def total_of(terms):
    total = terms[0].astype(F32)
    for term in terms[1:]:
        total = total + term.astype(F32)
    return total


def after(value, earlier):
    return lax.optimization_barrier((value, earlier))


def reduce_chunks(makers):
    terms, came = [None, None], {}

    def exchange(chunk, stage, earlier=None):
        half = terms[chunk][0].shape[0] // 2
        sent = total_of([term[:half] for term in terms[chunk]]).astype(BF16)
        if earlier is not None:
            sent, _ = after(sent, earlier)
        came[chunk, stage] = flip(sent, HALVING[ORDERS[chunk][stage]])
        terms[chunk] = [term[half:] for term in terms[chunk]] + [came[chunk, stage]]
        return sent

    terms[0] = makers[0](None)
    terms[1] = makers[1](exchange(0, 0))
    exchange(1, 0, came[0, 0])
    exchange(0, 1)
    exchange(1, 1, came[0, 1])
    exchange(0, 2)
    exchange(1, 2, came[0, 2])
    exchange(0, 3, came[1, 2])
    exchange(1, 3)
    return [total_of([term[0] for term in chunk]) for chunk in terms]


HEAD_STAGES = (
    lambda core: ZHIGH if core else Y,
    lambda core: ZLOW if core else ZHIGH,
    lambda core: Y if core else ZLOW,
)


def head_bits(place, core):
    bits = [(place >> stage) & 1 for stage in range(3)]
    return jnp.where(
        core == 0,
        bits[0] | (bits[1] << 2) | (bits[2] << 1),
        (bits[0] << 2) | (bits[1] << 1) | bits[2],
    )


def gather_heads(heads, beside):
    heads = heads[None]
    for number, bits_of in enumerate(HEAD_STAGES):
        if number == len(HEAD_STAGES) - 1:
            heads, beside = after(heads, beside)
        came = flip(heads, bits_of)
        if number == len(HEAD_STAGES) - 1:
            return [heads, came], beside
        heads = jnp.concatenate([heads, came], axis=0)


def route_table(route_ids, route_weights):
    shares = route_weights / jnp.sum(route_weights, axis=-1, keepdims=True)
    return jnp.concatenate([route_ids.astype(F32), shares], axis=1).T


def own_routes(table, group, experts):
    groups, both, here = table.shape
    top = both // 2
    own = group * experts + jnp.arange(experts, dtype=jnp.int32)
    ids = table[:, :top, :].astype(jnp.int32)
    match = ids[None] == own[:, None, None, None]
    named = jnp.any(match, axis=2)
    weights = jnp.sum(jnp.where(match, table[None, :, top:, :], 0.0), axis=2)
    span = PAIR * here
    order = jnp.arange(span)
    earlier = (order[:, None] < order[None, :]).astype(BF16)
    rank = jnp.dot(
        named.astype(BF16).reshape(experts * groups // PAIR, span),
        earlier,
        preferred_element_type=F32,
    )
    slots = jnp.where(named, rank.reshape(named.shape).astype(jnp.int32), -1)
    return slots.reshape(experts, groups * here), weights.reshape(experts, groups * here)


def block_table(device, groups, member):
    number = jnp.arange(32, dtype=jnp.int32)
    array, place = number >> 3, number & 7
    source_core = (device & 1) ^ (array >> 1)
    first = jnp.where(source_core == 0, X, Y)
    last = jnp.where(source_core == 0, Y, X)
    feature = (
        device
        ^ (array >> 1)
        ^ jnp.where(array & 1 == 1, first, 0)
        ^ jnp.where(place & 1 == 1, last, 0)
        ^ jnp.where(place & 2 == 2, ZHIGH, 0)
        ^ jnp.where(place & 4 == 4, ZLOW, 0)
    )
    swapped = ((feature ^ device) >> 2) & 1
    return jnp.concatenate([feature, swapped, jnp.stack([member, device >> 3])])


def gather_blocks(first, second, make_table, own_tables):
    def along(bits, block):
        return flip(block, lambda core: bits)

    def joined(held, came):
        return jnp.concatenate([held, came], axis=0)

    first_last = flip(first, last_axis)
    second_high = along(ZHIGH, second)
    second, _ = after(joined(second, second_high), first_last)
    second_low = along(ZLOW, second)
    first, _ = after(joined(first, first_last), second_high)
    first_high = along(ZHIGH, first)
    table = make_table(first_high)
    for bits in (ZHIGH, ZLOW, Y):
        table = joined(table, along(bits, table))
    second, first_high = after(joined(second, second_low), first_high)
    second_last = flip(second, last_axis)
    first = joined(first, first_high)
    first_low = along(ZLOW, first)
    second = joined(second, second_last)
    second_first = flip(second, first_axis)
    first_low, _ = after(first_low, second)
    beside = own_tables(table)
    first, (second_first, beside) = after(joined(first, first_low), (second_first, beside))
    first_first = flip(first, first_axis)
    return [
        [block, came, along(CORE, block), along(CORE, came)]
        for block, came in ((first, first_first), (second, second_first))
    ] + [beside]


def per_device_tokens(
    attn_heads, out_proj, residual, norm_gain, route_ids, route_weights, w_gate, w_up, w_down
):
    groups, members = lax.axis_size("expert"), lax.axis_size("tensor")
    group, member = lax.axis_index("expert"), lax.axis_index("tensor")
    device = group * members + member
    here, width = residual.shape
    experts = w_gate.shape[0]
    rows = -(-PAIR * CAP // 16) * 16
    x_side, core, y_side = member >> 1, member & 1, group & 1

    own_cols = lax.dynamic_index_in_dim(
        residual.reshape(here, groups, members, LANES), member, 2, keepdims=False
    )
    moved = lax.all_to_all(
        jnp.transpose(own_cols, (1, 0, 2)), "expert", split_axis=0, concat_axis=0, tiled=True
    ).reshape(groups // 2, 2, here, LANES)
    gain = lax.dynamic_index_in_dim(
        norm_gain.reshape(groups * members, LANES), device, 0, keepdims=False
    )

    pieces, moved = gather_heads(attn_heads, moved)
    numbers = jnp.arange(groups, dtype=jnp.int32)
    arrival = (head_bits(numbers, core) ^ group) ^ y_side
    info = jnp.concatenate(
        [jnp.stack([core, x_side]), ((arrival & 1) << 2) | (arrival >> 1)]
    )
    send, keep = project(info, pieces, out_proj)
    came = flip(send, lambda c: CORE)
    from_x = flip(total_of([keep[0], came[0]]).astype(BF16), lambda c: X)
    starts = []
    each = groups // 2
    for half in range(2):
        window = slice(half * each, (half + 1) * each)
        hidden = lax.dynamic_index_in_dim(moved, y_side ^ half, 1, keepdims=False).astype(F32)
        hidden = hidden + total_of([keep[1, window], came[1, window], from_x[window]])
        starts.append((hidden * gain).astype(BF16)[None])

    def make_table(earlier):
        ids, _ = after(route_ids, earlier)
        return route_table(ids, route_weights)[None]

    def own_tables(table):
        apart = own_order(groups, group) ^ group
        order = (apart >> 2) | (apart & 2) | ((apart & 1) << 2)
        return own_routes(jnp.take(table, order, axis=0, mode="clip"), group, experts)

    own_x, other_x, (slots, weights) = gather_blocks(*starts, make_table, own_tables)
    x = [piece for pair in zip(own_x, other_x) for piece in pair]
    invgain = (1.0 / norm_gain).reshape(groups * members, LANES)
    act, own_hidden, spread = gate_up(
        block_table(device, groups, member), slots, weights, invgain, x, w_gate, w_up, rows
    )

    cols = width // members

    def columns_of(to_core, chunk, chunks, orders):
        sides = jnp.stack([1 - x_side, x_side])
        blocks = (sides * 2 + to_core) * chunks + chunk
        places = [halving_places(to_core, group, groups, order) for order in orders]
        return jnp.concatenate([blocks] + places)

    chunks = len(ORDERS)
    chunk_cols = cols // chunks
    other = down(
        columns_of(1 - core, 0, 1, ORDERS), spread, act, w_down, rows, groups, cols, chunks
    )
    came = [flip(piece, lambda c: CORE) for piece in other]

    def terms_of(chunk, earlier):
        place = columns_of(core, chunk, chunks, ORDERS[chunk : chunk + 1])
        if earlier is not None:
            place, _ = after(place, earlier)
        (kept,) = down(place, spread, act, w_down, rows, groups, chunk_cols, 1)
        return [kept, came[chunk]]

    sums = reduce_chunks([functools.partial(terms_of, chunk) for chunk in range(chunks)])
    mixture = jnp.concatenate(sums, axis=1)
    return (own_hidden + mixture).astype(BF16)


def solution(mesh):
    groups, members = mesh.shape["expert"], mesh.shape["tensor"]
    placed = (
        P("expert", "tensor"),
        P("tensor", "expert"),
        P("expert", None),
        P(),
        P("expert", None),
        P("expert", None),
        P("expert", None, "tensor"),
        P("expert", None, "tensor"),
        P("expert", "tensor", None),
    )

    def run(*arrays):
        tokens, width = arrays[2].shape
        whole_tokens = (groups, members) == (8, 4) and width == groups * members * LANES
        body = per_device_tokens if whole_tokens else per_device_slots
        return jax.shard_map(
            body, mesh=mesh, in_specs=placed, out_specs=P("expert", "tensor"), check_vma=False
        )(*arrays)

    return run
```

```python
import functools

import jax
import jax.numpy as jnp
from jax import lax
from jax.experimental import pallas as pl
from jax.experimental.pallas import tpu as pltpu
from jax.sharding import PartitionSpec as P

EXPERTS = 64
CAP = 18
BF16 = jnp.bfloat16
F32 = jnp.float32
PAIR = 2
LANES = 128


def slot_places(ids, experts, capacity):
    row_count, top_count = ids.shape
    onehot = (ids[:, :, None] == jnp.arange(experts, dtype=jnp.int32)[None, None, :]).astype(
        jnp.int32
    )
    flattened = onehot.reshape(row_count * top_count, experts)
    before = jnp.cumsum(flattened, axis=0) - flattened
    slot_rank = jnp.sum(before * flattened, axis=1).reshape(row_count, top_count)
    return ids * capacity + slot_rank


def per_device_slots(
    attn_heads, out_proj, residual, norm_gain, route_ids, route_weights, w_gate, w_up, w_down
):
    model_width = residual.shape[1]
    groups = lax.axis_size("expert")
    members = lax.axis_size("tensor")
    member = lax.axis_index("tensor")
    per_group = w_gate.shape[0]
    slot_count = EXPERTS * CAP
    block_cols = model_width // members
    heads_out = jnp.dot(
        attn_heads,
        lax.all_gather(out_proj, "expert", axis=1, tiled=True),
        preferred_element_type=F32,
    )
    attn_out = lax.psum(heads_out.astype(BF16), "tensor").astype(F32)
    hidden = residual.astype(F32) + attn_out
    normed = (
        hidden * lax.rsqrt(jnp.mean(hidden * hidden, axis=-1, keepdims=True) + 1e-06) * norm_gain
    ).astype(BF16)
    slot_index = slot_places(route_ids, EXPERTS, CAP)
    slot_range = jnp.arange(slot_count, dtype=jnp.int32)
    slot_hits = jnp.sum(
        (slot_index[:, :, None] == slot_range[None, None, :]).astype(BF16), axis=1
    )
    buffer = jnp.einsum("rj,rd->jd", slot_hits, normed, preferred_element_type=F32).astype(BF16)
    buffer = buffer.reshape(groups, per_group, CAP, model_width)
    arrived = lax.all_to_all(buffer, "expert", split_axis=0, concat_axis=0, tiled=True)
    gate_acc = jnp.einsum("gxcd,xdf->gxcf", arrived, w_gate, preferred_element_type=F32)
    upper = jnp.einsum("gxcd,xdf->gxcf", arrived, w_up, preferred_element_type=F32)
    activation = (jax.nn.silu(gate_acc) * upper).astype(BF16)
    product_term = jnp.einsum("gxcf,xfd->gxcd", activation, w_down, preferred_element_type=F32)
    product_term = product_term.astype(BF16).reshape(groups, per_group, CAP, members, block_cols)
    expert_out = lax.psum_scatter(
        jnp.transpose(product_term, (3, 0, 1, 2, 4)), "tensor", scatter_dimension=0, tiled=True
    )[0]
    returned = lax.all_to_all(expert_out, "expert", split_axis=0, concat_axis=0, tiled=True)
    weights = route_weights / jnp.sum(route_weights, axis=-1, keepdims=True)
    picked = returned.reshape(slot_count, block_cols)[slot_index]
    mixture = jnp.sum(weights[:, :, None] * picked.astype(F32), axis=1)
    own_hidden = lax.dynamic_slice_in_dim(hidden, member * block_cols, block_cols, 1)
    return (own_hidden + mixture).astype(BF16)


def hits_of(slot_row, rows):
    places = lax.broadcasted_iota(jnp.int32, (rows, slot_row.shape[1]), 0)
    return places == slot_row


def project_kernel(info_ref, head_refs, weight_ref, send_ref, keep_ref):
    core, x_side = info_ref[0], info_ref[1]
    pieces = [ref.at[i] for ref in head_refs for i in range(ref.shape[0])]
    here = pieces[0].shape[0]
    each = len(pieces) // 2
    for part in range(2):
        result = jnp.dot(
            jnp.concatenate([ref[...] for ref in pieces[part * each : (part + 1) * each]]),
            weight_ref[...],
            preferred_element_type=F32,
        ).astype(BF16)
        for to_x in range(2):
            x_kept = (x_side == to_x).astype(jnp.int32)
            for to_core in range(2):
                start = (to_x * 2 + to_core) * LANES
                for out_ref, wanted in ((keep_ref, core == to_core), (send_ref, core != to_core)):

                    @pl.when(wanted)
                    def _(out_ref=out_ref, x_kept=x_kept, start=start, part=part, result=result):
                        for piece in range(each):
                            out_ref[x_kept, info_ref[2 + part * each + piece]] = result[
                                piece * here : (piece + 1) * here, start : start + LANES
                            ]


def project(info, pieces, out_proj):
    here = pieces[0].shape[1]
    groups = sum(piece.shape[0] for piece in pieces)
    out = jax.ShapeDtypeStruct((2, groups, here, LANES), BF16)
    vmem = pl.BlockSpec(memory_space=pltpu.VMEM)

    def kernel(info_ref, *refs):
        project_kernel(info_ref, refs[: len(pieces)], *refs[len(pieces) :])

    return pl.pallas_call(
        kernel,
        in_specs=[pl.BlockSpec(memory_space=pltpu.SMEM)] + [vmem] * (len(pieces) + 1),
        out_specs=[vmem, vmem],
        out_shape=[out, out],
        compiler_params=pltpu.CompilerParams(vmem_limit_bytes=24 * 1024 * 1024),
        cost_estimate=pl.CostEstimate(
            flops=2 * groups * here * out_proj.size,
            bytes_accessed=2 * (out_proj.size + 2 * groups * pieces[0][0].size),
            transcendentals=0,
        ),
        name="project",
    )(info, *pieces, out_proj)


def other_place(place):
    return (place >> 1) | ((place & 1) << 2)


def gate_up_kernel(
    experts, rows, width, info_ref, slot_ref, weight_ref, invgain_ref, x_refs, wg_ref, wu_ref,
    act_ref, hidden_ref, spread_ref, xs_ref, sq_ref, scale_ref, hits_ref
):
    expert = pl.program_id(0)
    arrays = len(x_refs) // 2
    each, parts, here, lanes = x_refs[0].shape
    blocks = arrays * each
    span = 2 * here
    member, z = info_ref[2 * blocks], info_ref[2 * blocks + 1]

    @pl.when(expert == 0)
    def _():
        sq_ref[...] = jnp.zeros_like(sq_ref)
        for part in range(parts):
            for e in range(experts):
                first = hits_of(slot_ref[e : e + 1, part * span : part * span + here], rows)
                second = hits_of(
                    slot_ref[e : e + 1, part * span + here : (part + 1) * span], rows
                )
                first = first.astype(F32).astype(BF16)
                second = second.astype(F32).astype(BF16)
                window = slice(e * rows, (e + 1) * rows)
                hits_ref[0, part, window, :] = jnp.concatenate([first, second], axis=1)
                hits_ref[1, part, window, :] = jnp.concatenate([second, first], axis=1)
            spread_ref[part] = jnp.transpose(hits_ref[0, part].astype(F32)).astype(BF16)

        def pair_of_blocks(low, carry):
            for array in range(arrays):
                own, other = x_refs[2 * array], x_refs[2 * array + 1]
                swapped = info_ref[blocks + array * each + low]
                places = (low, low + each // 2)
                features = [info_ref[array * each + place] for place in places]
                for place, feature in zip(places, features):
                    invgain = invgain_ref[pl.ds(feature, 1), :]
                    for part in range(parts):
                        for half, block in enumerate(
                            (own[place, part], other[other_place(place), part])
                        ):
                            value = block.astype(F32) * invgain
                            sq_ref[swapped, part, half] += value * value

                for part in range(parts):
                    both = jnp.concatenate(
                        [
                            jnp.concatenate([own[place, part], other[other_place(place), part]])
                            for place in places
                        ],
                        axis=1,
                    )
                    picked = jnp.dot(
                        hits_ref[swapped, part], both, preferred_element_type=F32
                    ).astype(BF16)
                    for number, feature in enumerate(features):
                        column = pl.multiple_of(feature * lanes, lanes)
                        for e in range(experts):
                            xs_ref[e, part * rows : (part + 1) * rows, pl.ds(column, lanes)] = (
                                picked[
                                    e * rows : (e + 1) * rows, number * lanes : (number + 1) * lanes
                                ]
                            )
            return carry

        lax.fori_loop(0, each // 2, pair_of_blocks, 0)

        def own_block(place, carry):
            for array in range(arrays):
                feature = info_ref[array * each + place]

                @pl.when(feature >> 3 == member)
                def _(array=array, feature=feature):
                    own, other = x_refs[2 * array], x_refs[2 * array + 1]
                    mine = jnp.where(
                        info_ref[blocks + array * each + place] == 0,
                        own[place, z].astype(F32),
                        other[other_place(place), z].astype(F32),
                    )
                    column = pl.multiple_of((feature & 7) * lanes, lanes)
                    hidden_ref[:, pl.ds(column, lanes)] = mine * invgain_ref[pl.ds(feature, 1), :]

            return carry

        lax.fori_loop(0, each, own_block, 0)
        pieces = [
            sq_ref[0, part, half] + sq_ref[1, part, 1 - half]
            for part in range(parts)
            for half in range(2)
        ]
        total = jnp.sum(
            jnp.transpose(jnp.concatenate(pieces, axis=0)), axis=0, keepdims=True
        )
        scale_ref[...] = jnp.broadcast_to(lax.rsqrt(total / width + 1e-06), scale_ref.shape)

    summed = jnp.dot(
        xs_ref[expert],
        jnp.concatenate([wg_ref[0], wu_ref[0]], axis=1),
        preferred_element_type=F32,
    )
    hidden_units = wg_ref.shape[2]
    for part in range(parts):
        window = slice(part * span, (part + 1) * span)
        hits = hits_of(slot_ref[pl.ds(expert, 1), window], rows)
        scale = jnp.sum(jnp.where(hits, scale_ref[0:1, window], 0.0), axis=1, keepdims=True)
        weight = jnp.sum(
            jnp.where(hits, weight_ref[pl.ds(expert, 1), window], 0.0), axis=1, keepdims=True
        )
        both_part = summed[part * rows : (part + 1) * rows, :]
        gate = both_part[:, :hidden_units] * scale
        upper = both_part[:, hidden_units:] * scale
        act = gate / (1.0 + jnp.exp(-gate)) * upper * weight
        act_ref[expert, part * rows : (part + 1) * rows, :] = act.astype(BF16)


def gate_up(info, slots, weights, invgain, x, w_gate, w_up, rows):
    experts, width, hidden_units = w_gate.shape
    each, parts, here, lanes = x[0].shape
    tokens = slots.shape[1]
    members = width // (each * lanes)

    def kernel(info_ref, slot_ref, weight_ref, invgain_ref, *rest):
        gate_up_kernel(
            experts, rows, width, info_ref, slot_ref, weight_ref, invgain_ref,
            rest[: len(x)], *rest[len(x) :]
        )

    def whole(shape):
        return pl.BlockSpec(
            shape, lambda e, info: (0,) * len(shape), pipeline_mode=pl.Buffered(1)
        )

    return pl.pallas_call(
        kernel,
        grid_spec=pltpu.PrefetchScalarGridSpec(
            num_scalar_prefetch=1,
            grid=(experts,),
            in_specs=[whole(slots.shape), whole(weights.shape), whole(invgain.shape)]
            + [pl.BlockSpec(memory_space=pltpu.VMEM)] * len(x)
            + [pl.BlockSpec((1, width, hidden_units), lambda e, info: (e, 0, 0))] * 2,
            out_specs=[
                pl.BlockSpec(memory_space=pltpu.VMEM),
                pl.BlockSpec(memory_space=pltpu.VMEM),
                pl.BlockSpec(memory_space=pltpu.VMEM),
            ],
            scratch_shapes=[
                pltpu.VMEM((experts, parts * rows, width), BF16),
                pltpu.VMEM((2, parts, 2, here, lanes), F32),
                pltpu.VMEM((8, tokens), F32),
                pltpu.VMEM((2, parts, experts * rows, 2 * here), BF16),
            ],
        ),
        out_shape=[
            jax.ShapeDtypeStruct((experts, parts * rows, hidden_units), BF16),
            jax.ShapeDtypeStruct((here, width // members), F32),
            jax.ShapeDtypeStruct((parts, 2 * here, experts * rows), BF16),
        ],
        compiler_params=pltpu.CompilerParams(
            vmem_limit_bytes=36 * 1024 * 1024, dimension_semantics=("arbitrary",)
        ),
        cost_estimate=pl.CostEstimate(
            flops=2 * experts * parts * rows * width * 2 * hidden_units,
            bytes_accessed=4 * experts * width * hidden_units + 2 * len(x) * x[0].size,
            transcendentals=0,
        ),
        name="gate_up",
    )(info, slots, weights, invgain, *x, w_gate, w_up)


def down_kernel(rows, place_ref, spread_ref, act_ref, wd0_ref, wd1_ref, *rest):
    out_refs, ys_ref = rest[:-1], rest[-1]
    out_cols = out_refs[0].shape[2]
    step = pl.program_id(0)
    experts, all_rows, _ = act_ref.shape
    per_step = wd0_ref.shape[0]
    parts = all_rows // rows
    groups = parts * PAIR
    for number in range(per_step):
        expert = step * per_step + number
        for side, wd_ref in enumerate((wd0_ref, wd1_ref)):
            result = jnp.dot(
                act_ref[expert], wd_ref[number], preferred_element_type=F32
            ).astype(BF16)
            for part in range(parts):
                ys_ref[side, part, expert] = result[part * rows : (part + 1) * rows, :]

    @pl.when(step == pl.num_programs(0) - 1)
    def _():
        for part in range(parts):
            for side in range(2):
                picked = ys_ref[side, part].reshape(experts * rows, ys_ref.shape[4])
                mixed = jnp.dot(
                    spread_ref[part], picked, preferred_element_type=F32
                ).astype(BF16)
                for i in range(PAIR):
                    for number, out_ref in enumerate(out_refs):
                        block = (number * 2 + side) * groups + part * PAIR + i
                        target = place_ref[2 + block]
                        out_ref[target] = mixed[
                            i * 128 : (i + 1) * 128, number * out_cols : (number + 1) * out_cols
                        ]


def down(place, spread, act, w_down, rows, groups, cols, chunks, per_step=2):
    experts, hidden_units, width = w_down.shape
    parts, span, _ = spread.shape
    here = parts * span // groups
    out = jax.ShapeDtypeStruct((2 * groups, here, cols // chunks), BF16)
    return pl.pallas_call(
        functools.partial(down_kernel, rows),
        grid_spec=pltpu.PrefetchScalarGridSpec(
            num_scalar_prefetch=1,
            grid=(experts // per_step,),
            in_specs=[
                pl.BlockSpec(memory_space=pltpu.VMEM),
                pl.BlockSpec(memory_space=pltpu.VMEM),
                pl.BlockSpec((per_step, hidden_units, cols), lambda e, p: (e, 0, p[0])),
                pl.BlockSpec((per_step, hidden_units, cols), lambda e, p: (e, 0, p[1])),
            ],
            out_specs=[pl.BlockSpec(out.shape, lambda e, p: (0, 0, 0))] * chunks,
            scratch_shapes=[pltpu.VMEM((2, parts, experts, rows, cols), BF16)],
        ),
        out_shape=[out] * chunks,
        compiler_params=pltpu.CompilerParams(
            vmem_limit_bytes=36 * 1024 * 1024, dimension_semantics=("arbitrary",)
        ),
        cost_estimate=pl.CostEstimate(
            flops=8 * experts * parts * rows * cols * hidden_units,
            bytes_accessed=4 * experts * cols * hidden_units + 4 * parts * span * cols,
            transcendentals=0,
        ),
        name="down_mix",
    )(place, spread, act, w_down, w_down)


def flip(array, bits_of):
    pairs = []
    for index in range(32):
        pairs.append((index, index ^ bits_of(index & 1)))
    return lax.ppermute(array, ("expert", "tensor"), pairs)


CORE, X, Y, ZLOW, ZHIGH = 1, 2, 4, 8, 16


def first_axis(core):
    return Y if core else X


def last_axis(core):
    return X if core else Y


def own_order(groups, group):
    order = jnp.arange(groups, dtype=jnp.int32)
    return order ^ (group & 1)


HALVING = {
    "first": first_axis,
    "last": last_axis,
    "low": lambda core: ZLOW,
    "high": lambda core: ZHIGH,
}
ORDERS = (("first", "low", "high", "last"), ("first", "last", "low", "high"))


def halving_places(to_core, group, groups, order):
    g = own_order(groups, group)[None, :]
    y_kept = ((g & 1) == (group & 1)).astype(jnp.int32)
    x_kept = jnp.arange(2, dtype=jnp.int32)[:, None]
    kept = {
        "first": jnp.where(to_core == 0, x_kept, y_kept),
        "last": jnp.where(to_core == 0, y_kept, x_kept),
        "low": (((g >> 1) & 1) == ((group >> 1) & 1)).astype(jnp.int32),
        "high": ((g >> 2) == (group >> 2)).astype(jnp.int32),
    }
    place = 0
    for axis in order:
        place = place * 2 + kept[axis]
    return place.reshape(-1)


def total_of(terms):
    total = terms[0].astype(F32)
    for term in terms[1:]:
        total = total + term.astype(F32)
    return total


def after(value, earlier):
    return lax.optimization_barrier((value, earlier))


def reduce_chunks(makers):
    terms, came = [None, None], {}

    def exchange(chunk, stage, earlier=None):
        half = terms[chunk][0].shape[0] // 2
        sent = total_of([term[:half] for term in terms[chunk]]).astype(BF16)
        if earlier is not None:
            sent, _ = after(sent, earlier)
        came[chunk, stage] = flip(sent, HALVING[ORDERS[chunk][stage]])
        terms[chunk] = [term[half:] for term in terms[chunk]] + [came[chunk, stage]]
        return sent

    terms[0] = makers[0](None)
    terms[1] = makers[1](exchange(0, 0))
    exchange(1, 0)
    exchange(0, 1)
    exchange(1, 1, came[0, 1])
    exchange(0, 2)
    exchange(1, 2, came[0, 2])
    exchange(0, 3, came[1, 2])
    exchange(1, 3)
    return [total_of([term[0] for term in chunk]) for chunk in terms]


HEAD_STAGES = (
    lambda core: ZHIGH if core else Y,
    lambda core: ZLOW if core else ZHIGH,
    lambda core: Y if core else ZLOW,
)


def head_bits(place, core):
    bits = [(place >> stage) & 1 for stage in range(3)]
    return jnp.where(
        core == 0,
        bits[0] | (bits[1] << 2) | (bits[2] << 1),
        (bits[0] << 2) | (bits[1] << 1) | bits[2],
    )


def gather_heads(heads, beside):
    heads = heads[None]
    for number, bits_of in enumerate(HEAD_STAGES):
        if number == len(HEAD_STAGES) - 1:
            heads, beside = after(heads, beside)
        came = flip(heads, bits_of)
        if number == len(HEAD_STAGES) - 1:
            return [heads, came], beside
        heads = jnp.concatenate([heads, came], axis=0)


def pack_kernel(member_ref, residual_ref, ids_ref, weights_ref, out_ref):
    groups, rows, lanes = out_ref.shape
    here, width = residual_ref.shape
    each = width // groups
    rest = weights_ref[...] / jnp.sum(weights_ref[...], axis=0, keepdims=True)
    parts = [ids_ref[...].astype(F32)]
    for _ in range(3):
        part = rest.astype(BF16).astype(F32)
        parts.append(part)
        rest = rest - part
    table = jnp.concatenate(parts, axis=0).astype(BF16)
    for group in range(groups):
        column = pl.multiple_of(group * each + member_ref[0] * lanes, lanes)
        out_ref[group, :here, :] = residual_ref[:, pl.ds(column, lanes)]
        out_ref[group, here:, :] = table


def pack(member, residual, route_ids, route_weights, groups):
    here, top = route_ids.shape
    vmem = pl.BlockSpec(memory_space=pltpu.VMEM)
    return pl.pallas_call(
        pack_kernel,
        in_specs=[pl.BlockSpec(memory_space=pltpu.SMEM), vmem, vmem, vmem],
        out_specs=vmem,
        out_shape=jax.ShapeDtypeStruct((groups, here + 4 * top, LANES), BF16),
        compiler_params=pltpu.CompilerParams(vmem_limit_bytes=16 * 1024 * 1024),
        cost_estimate=pl.CostEstimate(
            flops=0, bytes_accessed=3 * residual.size, transcendentals=0
        ),
        name="pack",
    )(member.reshape(1), residual, route_ids.T, route_weights.T)


def own_routes(table, group, experts):
    groups, rows, here = table.shape
    top = rows // 4
    own = group * experts + jnp.arange(experts, dtype=jnp.int32)
    table = table.astype(F32).reshape(groups, 4, top, here)
    ids = table[:, 0].astype(jnp.int32)
    match = ids[None] == own[:, None, None, None]
    named = jnp.any(match, axis=2)
    shares = table[:, 1] + table[:, 2] + table[:, 3]
    weights = jnp.sum(jnp.where(match, shares[None], 0.0), axis=2)
    span = PAIR * here
    order = jnp.arange(span)
    earlier = (order[:, None] < order[None, :]).astype(BF16)
    rank = jnp.dot(
        named.astype(BF16).reshape(experts * groups // PAIR, span),
        earlier,
        preferred_element_type=F32,
    )
    slots = jnp.where(named, rank.reshape(named.shape).astype(jnp.int32), -1)
    return slots.reshape(experts, groups * here), weights.reshape(experts, groups * here)


def block_table(device, groups, member):
    number = jnp.arange(32, dtype=jnp.int32)
    array, place = number >> 3, number & 7
    source_core = (device & 1) ^ (array >> 1)
    first = jnp.where(source_core == 0, X, Y)
    last = jnp.where(source_core == 0, Y, X)
    feature = (
        device
        ^ (array >> 1)
        ^ jnp.where(array & 1 == 1, first, 0)
        ^ jnp.where(place & 1 == 1, last, 0)
        ^ jnp.where(place & 2 == 2, ZHIGH, 0)
        ^ jnp.where(place & 4 == 4, ZLOW, 0)
    )
    swapped = ((feature ^ device) >> 2) & 1
    return jnp.concatenate([feature, swapped, jnp.stack([member, device >> 3])])


def gather_blocks(first, second):
    def along(bits, block):
        return flip(block, lambda core: bits)

    def joined(held, came):
        return jnp.concatenate([held, came], axis=0)

    first_last = flip(first, last_axis)
    second_high = along(ZHIGH, second)
    second, _ = after(joined(second, second_high), first_last)
    second_low = along(ZLOW, second)
    first, _ = after(joined(first, first_last), second_high)
    first_high = along(ZHIGH, first)
    second, first_high = after(joined(second, second_low), first_high)
    second_last = flip(second, last_axis)
    first = joined(first, first_high)
    first_low = along(ZLOW, first)
    second = joined(second, second_last)
    second_first = flip(second, first_axis)
    first_low, _ = after(first_low, second)
    first = joined(first, first_low)
    first_first = flip(first, first_axis)
    return [
        [block, came, along(CORE, block), along(CORE, came)]
        for block, came in ((first, first_first), (second, second_first))
    ]


def per_device_tokens(
    attn_heads, out_proj, residual, norm_gain, route_ids, route_weights, w_gate, w_up, w_down
):
    groups, members = lax.axis_size("expert"), lax.axis_size("tensor")
    group, member = lax.axis_index("expert"), lax.axis_index("tensor")
    device = group * members + member
    here, width = residual.shape
    experts = w_gate.shape[0]
    rows = -(-PAIR * CAP // 16) * 16
    x_side, core, y_side = member >> 1, member & 1, group & 1

    moved = lax.all_to_all(
        pack(member, residual, route_ids, route_weights, groups),
        "expert",
        split_axis=0,
        concat_axis=0,
        tiled=True,
    )
    gain = lax.dynamic_index_in_dim(
        norm_gain.reshape(groups * members, LANES), device, 0, keepdims=False
    )

    pieces, moved = gather_heads(attn_heads, moved)
    numbers = jnp.arange(groups, dtype=jnp.int32)
    arrival = (head_bits(numbers, core) ^ group) ^ y_side
    info = jnp.concatenate(
        [jnp.stack([core, x_side]), ((arrival & 1) << 2) | (arrival >> 1)]
    )
    table = jnp.take(moved[:, here:], own_order(groups, group), axis=0, mode="clip")
    moved = moved[:, :here].reshape(groups // 2, 2, here, LANES)
    slots, weights = own_routes(table, group, experts)
    info, (slots, weights) = after(info, (slots, weights))
    send, keep = project(info, pieces, out_proj)
    came = flip(send, lambda c: CORE)
    from_x = flip(total_of([keep[0], came[0]]).astype(BF16), lambda c: X)
    starts = []
    each = groups // 2
    for half in range(2):
        window = slice(half * each, (half + 1) * each)
        hidden = lax.dynamic_index_in_dim(moved, y_side ^ half, 1, keepdims=False).astype(F32)
        hidden = hidden + total_of([keep[1, window], came[1, window], from_x[window]])
        starts.append((hidden * gain).astype(BF16)[None])

    own_x, other_x = gather_blocks(*starts)
    x = [piece for pair in zip(own_x, other_x) for piece in pair]
    invgain = (1.0 / norm_gain).reshape(groups * members, LANES)
    act, own_hidden, spread = gate_up(
        block_table(device, groups, member), slots, weights, invgain, x, w_gate, w_up, rows
    )

    cols = width // members

    def columns_of(to_core, chunk, chunks, orders):
        sides = jnp.stack([1 - x_side, x_side])
        blocks = (sides * 2 + to_core) * chunks + chunk
        places = [halving_places(to_core, group, groups, order) for order in orders]
        return jnp.concatenate([blocks] + places)

    chunks = len(ORDERS)
    chunk_cols = cols // chunks
    other = down(
        columns_of(1 - core, 0, 1, ORDERS), spread, act, w_down, rows, groups, cols, chunks
    )
    came = [flip(piece, lambda c: CORE) for piece in other]

    def terms_of(chunk, earlier):
        place = columns_of(core, chunk, chunks, ORDERS[chunk : chunk + 1])
        if earlier is not None:
            place, _ = after(place, earlier)
        (kept,) = down(place, spread, act, w_down, rows, groups, chunk_cols, 1)
        return [kept, came[chunk]]

    sums = reduce_chunks([functools.partial(terms_of, chunk) for chunk in range(chunks)])
    mixture = jnp.concatenate(sums, axis=1)
    return (own_hidden + mixture).astype(BF16)


def solution(mesh):
    groups, members = mesh.shape["expert"], mesh.shape["tensor"]
    placed = (
        P("expert", "tensor"),
        P("tensor", "expert"),
        P("expert", None),
        P(),
        P("expert", None),
        P("expert", None),
        P("expert", None, "tensor"),
        P("expert", None, "tensor"),
        P("expert", "tensor", None),
    )

    def run(*arrays):
        tokens, width = arrays[2].shape
        whole_tokens = (groups, members) == (8, 4) and width == groups * members * LANES
        body = per_device_tokens if whole_tokens else per_device_slots
        return jax.shard_map(
            body, mesh=mesh, in_specs=placed, out_specs=P("expert", "tensor"), check_vma=False
        )(*arrays)

    return run
```

```python
import functools

import jax
import jax.numpy as jnp
from jax import lax
from jax.experimental import pallas as pl
from jax.experimental.pallas import tpu as pltpu
from jax.sharding import PartitionSpec as P

EXPERTS = 64
CAP = 18
BF16 = jnp.bfloat16
F32 = jnp.float32
PAIR = 2
LANES = 128


def slot_places(ids, experts, capacity):
    row_count, top_count = ids.shape
    onehot = (ids[:, :, None] == jnp.arange(experts, dtype=jnp.int32)[None, None, :]).astype(
        jnp.int32
    )
    flattened = onehot.reshape(row_count * top_count, experts)
    before = jnp.cumsum(flattened, axis=0) - flattened
    slot_rank = jnp.sum(before * flattened, axis=1).reshape(row_count, top_count)
    return ids * capacity + slot_rank


def per_device_slots(
    attn_heads, out_proj, residual, norm_gain, route_ids, route_weights, w_gate, w_up, w_down
):
    model_width = residual.shape[1]
    groups = lax.axis_size("expert")
    members = lax.axis_size("tensor")
    member = lax.axis_index("tensor")
    per_group = w_gate.shape[0]
    slot_count = EXPERTS * CAP
    block_cols = model_width // members
    heads_out = jnp.dot(
        attn_heads,
        lax.all_gather(out_proj, "expert", axis=1, tiled=True),
        preferred_element_type=F32,
    )
    attn_out = lax.psum(heads_out.astype(BF16), "tensor").astype(F32)
    hidden = residual.astype(F32) + attn_out
    normed = (
        hidden * lax.rsqrt(jnp.mean(hidden * hidden, axis=-1, keepdims=True) + 1e-06) * norm_gain
    ).astype(BF16)
    slot_index = slot_places(route_ids, EXPERTS, CAP)
    slot_range = jnp.arange(slot_count, dtype=jnp.int32)
    slot_hits = jnp.sum(
        (slot_index[:, :, None] == slot_range[None, None, :]).astype(BF16), axis=1
    )
    buffer = jnp.einsum("rj,rd->jd", slot_hits, normed, preferred_element_type=F32).astype(BF16)
    buffer = buffer.reshape(groups, per_group, CAP, model_width)
    arrived = lax.all_to_all(buffer, "expert", split_axis=0, concat_axis=0, tiled=True)
    gate_acc = jnp.einsum("gxcd,xdf->gxcf", arrived, w_gate, preferred_element_type=F32)
    upper = jnp.einsum("gxcd,xdf->gxcf", arrived, w_up, preferred_element_type=F32)
    activation = (jax.nn.silu(gate_acc) * upper).astype(BF16)
    product_term = jnp.einsum("gxcf,xfd->gxcd", activation, w_down, preferred_element_type=F32)
    product_term = product_term.astype(BF16).reshape(groups, per_group, CAP, members, block_cols)
    expert_out = lax.psum_scatter(
        jnp.transpose(product_term, (3, 0, 1, 2, 4)), "tensor", scatter_dimension=0, tiled=True
    )[0]
    returned = lax.all_to_all(expert_out, "expert", split_axis=0, concat_axis=0, tiled=True)
    weights = route_weights / jnp.sum(route_weights, axis=-1, keepdims=True)
    picked = returned.reshape(slot_count, block_cols)[slot_index]
    mixture = jnp.sum(weights[:, :, None] * picked.astype(F32), axis=1)
    own_hidden = lax.dynamic_slice_in_dim(hidden, member * block_cols, block_cols, 1)
    return (own_hidden + mixture).astype(BF16)


def hits_of(slot_row, rows):
    places = lax.broadcasted_iota(jnp.int32, (rows, slot_row.shape[1]), 0)
    return places == slot_row


def project_kernel(info_ref, head_refs, weight_ref, send_ref, keep_ref):
    core, x_side = info_ref[0], info_ref[1]
    pieces = [ref.at[i] for ref in head_refs for i in range(ref.shape[0])]
    here = pieces[0].shape[0]
    each = len(pieces) // 2
    for part in range(2):
        result = jnp.dot(
            jnp.concatenate([ref[...] for ref in pieces[part * each : (part + 1) * each]]),
            weight_ref[...],
            preferred_element_type=F32,
        ).astype(BF16)
        for to_x in range(2):
            x_kept = (x_side == to_x).astype(jnp.int32)
            for to_core in range(2):
                start = (to_x * 2 + to_core) * LANES
                for out_ref, wanted in ((keep_ref, core == to_core), (send_ref, core != to_core)):

                    @pl.when(wanted)
                    def _(out_ref=out_ref, x_kept=x_kept, start=start, part=part, result=result):
                        for piece in range(each):
                            out_ref[x_kept, info_ref[2 + part * each + piece]] = result[
                                piece * here : (piece + 1) * here, start : start + LANES
                            ]


def project(info, pieces, out_proj):
    here = pieces[0].shape[1]
    groups = sum(piece.shape[0] for piece in pieces)
    out = jax.ShapeDtypeStruct((2, groups, here, LANES), BF16)
    vmem = pl.BlockSpec(memory_space=pltpu.VMEM)

    def kernel(info_ref, *refs):
        project_kernel(info_ref, refs[: len(pieces)], *refs[len(pieces) :])

    return pl.pallas_call(
        kernel,
        in_specs=[pl.BlockSpec(memory_space=pltpu.SMEM)] + [vmem] * (len(pieces) + 1),
        out_specs=[vmem, vmem],
        out_shape=[out, out],
        compiler_params=pltpu.CompilerParams(vmem_limit_bytes=24 * 1024 * 1024),
        cost_estimate=pl.CostEstimate(
            flops=2 * groups * here * out_proj.size,
            bytes_accessed=2 * (out_proj.size + 2 * groups * pieces[0][0].size),
            transcendentals=0,
        ),
        name="project",
    )(info, *pieces, out_proj)


def gate_up_kernel(
    experts, rows, width, info_ref, slot_ref, weight_ref, invgain_ref, x_refs, wg_ref, wu_ref,
    act_ref, hidden_ref, spread_ref, xs_ref, sq_ref, scale_ref, hits_ref
):
    expert = pl.program_id(0)
    arrays = 4
    own_refs = (x_refs[:arrays], x_refs[arrays : 2 * arrays])
    other_refs = (x_refs[2 * arrays : 3 * arrays], x_refs[3 * arrays :])
    parts, here, lanes = x_refs[0].shape[1:]
    blocks = info_ref.shape[0] // 2 - 1
    each = blocks // arrays
    span = 2 * here
    member, z = info_ref[2 * blocks], info_ref[2 * blocks + 1]

    def block_at(array, last, high, low):
        return (
            array * each + low * 4 + high * 2 + last,
            own_refs[low][array].at[high * 2 + last],
            other_refs[last][array].at[low * 2 + high],
        )

    @pl.when(expert == 0)
    def _():
        sq_ref[...] = jnp.zeros_like(sq_ref)
        for part in range(parts):
            for e in range(experts):
                first = hits_of(slot_ref[e : e + 1, part * span : part * span + here], rows)
                second = hits_of(
                    slot_ref[e : e + 1, part * span + here : (part + 1) * span], rows
                )
                first = first.astype(F32).astype(BF16)
                second = second.astype(F32).astype(BF16)
                window = slice(e * rows, (e + 1) * rows)
                hits_ref[0, part, window, :] = jnp.concatenate([first, second], axis=1)
                hits_ref[1, part, window, :] = jnp.concatenate([second, first], axis=1)
            spread_ref[part] = jnp.transpose(hits_ref[0, part].astype(F32)).astype(BF16)

        def pairs_of_blocks(high, carry):
            for array in range(arrays):
                for last in range(2):
                    pair = [block_at(array, last, high, low) for low in range(2)]
                    swapped = info_ref[blocks + pair[0][0]]
                    features = [info_ref[place] for place, _, _ in pair]
                    for feature, (_, own, other) in zip(features, pair):
                        invgain = invgain_ref[pl.ds(feature, 1), :]
                        for part in range(parts):
                            for half, block in enumerate((own, other)):
                                value = block[part].astype(F32) * invgain
                                sq_ref[swapped, part, half] += value * value
                    for part in range(parts):
                        both = jnp.concatenate(
                            [
                                jnp.concatenate([own[part], other[part]], axis=0)
                                for _, own, other in pair
                            ],
                            axis=1,
                        )
                        picked = jnp.dot(
                            hits_ref[swapped, part], both, preferred_element_type=F32
                        ).astype(BF16)
                        for number, feature in enumerate(features):
                            column = pl.multiple_of(feature * lanes, lanes)
                            for e in range(experts):
                                xs_ref[
                                    e, part * rows : (part + 1) * rows, pl.ds(column, lanes)
                                ] = picked[
                                    e * rows : (e + 1) * rows, number * lanes : (number + 1) * lanes
                                ]
            return carry

        lax.fori_loop(0, 2, pairs_of_blocks, 0)

        def own_blocks(high, carry):
            for array in range(arrays):
                for last in range(2):
                    for low in range(2):
                        place, own, other = block_at(array, last, high, low)
                        feature = info_ref[place]

                        @pl.when(feature >> 3 == member)
                        def _(place=place, feature=feature, own=own, other=other):
                            mine = jnp.where(
                                info_ref[blocks + place] == 0,
                                own[z].astype(F32),
                                other[z].astype(F32),
                            )
                            column = pl.multiple_of((feature & 7) * lanes, lanes)
                            hidden_ref[:, pl.ds(column, lanes)] = (
                                mine * invgain_ref[pl.ds(feature, 1), :]
                            )

            return carry

        lax.fori_loop(0, 2, own_blocks, 0)
        pieces = [
            sq_ref[0, part, half] + sq_ref[1, part, 1 - half]
            for part in range(parts)
            for half in range(2)
        ]
        total = jnp.sum(
            jnp.transpose(jnp.concatenate(pieces, axis=0)), axis=0, keepdims=True
        )
        scale_ref[...] = jnp.broadcast_to(lax.rsqrt(total / width + 1e-06), scale_ref.shape)

    summed = jnp.dot(
        xs_ref[expert],
        jnp.concatenate([wg_ref[0], wu_ref[0]], axis=1),
        preferred_element_type=F32,
    )
    hidden_units = wg_ref.shape[2]
    for part in range(parts):
        window = slice(part * span, (part + 1) * span)
        hits = hits_of(slot_ref[pl.ds(expert, 1), window], rows)
        scale = jnp.sum(jnp.where(hits, scale_ref[0:1, window], 0.0), axis=1, keepdims=True)
        weight = jnp.sum(
            jnp.where(hits, weight_ref[pl.ds(expert, 1), window], 0.0), axis=1, keepdims=True
        )
        both_part = summed[part * rows : (part + 1) * rows, :]
        gate = both_part[:, :hidden_units] * scale
        upper = both_part[:, hidden_units:] * scale
        act = gate / (1.0 + jnp.exp(-gate)) * upper * weight
        act_ref[expert, part * rows : (part + 1) * rows, :] = act.astype(BF16)


def gate_up(info, slots, weights, invgain, x, w_gate, w_up, rows, members):
    experts, width, hidden_units = w_gate.shape
    parts, here, lanes = x[0].shape[1:]
    tokens = slots.shape[1]

    def kernel(info_ref, slot_ref, weight_ref, invgain_ref, *rest):
        gate_up_kernel(
            experts, rows, width, info_ref, slot_ref, weight_ref, invgain_ref,
            rest[: len(x)], *rest[len(x) :]
        )

    def whole(shape):
        return pl.BlockSpec(
            shape, lambda e, info: (0,) * len(shape), pipeline_mode=pl.Buffered(1)
        )

    return pl.pallas_call(
        kernel,
        grid_spec=pltpu.PrefetchScalarGridSpec(
            num_scalar_prefetch=1,
            grid=(experts,),
            in_specs=[whole(slots.shape), whole(weights.shape), whole(invgain.shape)]
            + [pl.BlockSpec(memory_space=pltpu.VMEM)] * len(x)
            + [pl.BlockSpec((1, width, hidden_units), lambda e, info: (e, 0, 0))] * 2,
            out_specs=[
                pl.BlockSpec(memory_space=pltpu.VMEM),
                pl.BlockSpec(memory_space=pltpu.VMEM),
                pl.BlockSpec(memory_space=pltpu.VMEM),
            ],
            scratch_shapes=[
                pltpu.VMEM((experts, parts * rows, width), BF16),
                pltpu.VMEM((2, parts, 2, here, lanes), F32),
                pltpu.VMEM((8, tokens), F32),
                pltpu.VMEM((2, parts, experts * rows, 2 * here), BF16),
            ],
        ),
        out_shape=[
            jax.ShapeDtypeStruct((experts, parts * rows, hidden_units), BF16),
            jax.ShapeDtypeStruct((here, width // members), F32),
            jax.ShapeDtypeStruct((parts, 2 * here, experts * rows), BF16),
        ],
        compiler_params=pltpu.CompilerParams(
            vmem_limit_bytes=36 * 1024 * 1024, dimension_semantics=("arbitrary",)
        ),
        cost_estimate=pl.CostEstimate(
            flops=2 * experts * parts * rows * width * 2 * hidden_units,
            bytes_accessed=4 * experts * width * hidden_units + 2 * len(x) * x[0].size,
            transcendentals=0,
        ),
        name="gate_up",
    )(info, slots, weights, invgain, *x, w_gate, w_up)


def down_kernel(rows, place_ref, spread_ref, act_ref, wd0_ref, wd1_ref, *rest):
    out_refs, ys_ref = rest[:-1], rest[-1]
    out_cols = out_refs[0].shape[2]
    step = pl.program_id(0)
    experts, all_rows, _ = act_ref.shape
    per_step = wd0_ref.shape[0]
    parts = all_rows // rows
    groups = parts * PAIR
    for number in range(per_step):
        expert = step * per_step + number
        for side, wd_ref in enumerate((wd0_ref, wd1_ref)):
            result = jnp.dot(
                act_ref[expert], wd_ref[number], preferred_element_type=F32
            ).astype(BF16)
            for part in range(parts):
                ys_ref[side, part, expert] = result[part * rows : (part + 1) * rows, :]

    @pl.when(step == pl.num_programs(0) - 1)
    def _():
        for part in range(parts):
            for side in range(2):
                picked = ys_ref[side, part].reshape(experts * rows, ys_ref.shape[4])
                mixed = jnp.dot(
                    spread_ref[part], picked, preferred_element_type=F32
                ).astype(BF16)
                for i in range(PAIR):
                    for number, out_ref in enumerate(out_refs):
                        block = (number * 2 + side) * groups + part * PAIR + i
                        target = place_ref[2 + block]
                        out_ref[target] = mixed[
                            i * 128 : (i + 1) * 128, number * out_cols : (number + 1) * out_cols
                        ]


def down(place, spread, act, w_down, rows, groups, cols, chunks, per_step=2):
    experts, hidden_units, width = w_down.shape
    parts, span, _ = spread.shape
    here = parts * span // groups
    out = jax.ShapeDtypeStruct((2 * groups, here, cols // chunks), BF16)
    return pl.pallas_call(
        functools.partial(down_kernel, rows),
        grid_spec=pltpu.PrefetchScalarGridSpec(
            num_scalar_prefetch=1,
            grid=(experts // per_step,),
            in_specs=[
                pl.BlockSpec(memory_space=pltpu.VMEM),
                pl.BlockSpec(memory_space=pltpu.VMEM),
                pl.BlockSpec((per_step, hidden_units, cols), lambda e, p: (e, 0, p[0])),
                pl.BlockSpec((per_step, hidden_units, cols), lambda e, p: (e, 0, p[1])),
            ],
            out_specs=[pl.BlockSpec(out.shape, lambda e, p: (0, 0, 0))] * chunks,
            scratch_shapes=[pltpu.VMEM((2, parts, experts, rows, cols), BF16)],
        ),
        out_shape=[out] * chunks,
        compiler_params=pltpu.CompilerParams(
            vmem_limit_bytes=36 * 1024 * 1024, dimension_semantics=("arbitrary",)
        ),
        cost_estimate=pl.CostEstimate(
            flops=8 * experts * parts * rows * cols * hidden_units,
            bytes_accessed=4 * experts * cols * hidden_units + 4 * parts * span * cols,
            transcendentals=0,
        ),
        name="down_mix",
    )(place, spread, act, w_down, w_down)


def flip(array, bits_of):
    pairs = []
    for index in range(32):
        pairs.append((index, index ^ bits_of(index & 1)))
    return lax.ppermute(array, ("expert", "tensor"), pairs)


CORE, X, Y, ZLOW, ZHIGH = 1, 2, 4, 8, 16


def first_axis(core):
    return Y if core else X


def last_axis(core):
    return X if core else Y


def own_order(groups, group):
    order = jnp.arange(groups, dtype=jnp.int32)
    return order ^ (group & 1)


HALVING = {
    "first": first_axis,
    "last": last_axis,
    "low": lambda core: ZLOW,
    "high": lambda core: ZHIGH,
}
ORDERS = (("first", "low", "high", "last"), ("first", "last", "low", "high"))


def halving_places(to_core, group, groups, order):
    g = own_order(groups, group)[None, :]
    y_kept = ((g & 1) == (group & 1)).astype(jnp.int32)
    x_kept = jnp.arange(2, dtype=jnp.int32)[:, None]
    kept = {
        "first": jnp.where(to_core == 0, x_kept, y_kept),
        "last": jnp.where(to_core == 0, y_kept, x_kept),
        "low": (((g >> 1) & 1) == ((group >> 1) & 1)).astype(jnp.int32),
        "high": ((g >> 2) == (group >> 2)).astype(jnp.int32),
    }
    place = 0
    for axis in order:
        place = place * 2 + kept[axis]
    return place.reshape(-1)


def total_of(terms):
    total = terms[0].astype(F32)
    for term in terms[1:]:
        total = total + term.astype(F32)
    return total


def after(value, earlier):
    return lax.optimization_barrier((value, earlier))


def reduce_chunks(makers):
    terms, sends, came = [None, None], [None, None], {}

    def split_exchange(chunk):
        whole = terms[chunk]
        quarter = whole[0].shape[0] // 4
        rows = [slice(i * quarter, (i + 1) * quarter) for i in range(4)]
        bits_of = HALVING[ORDERS[chunk][0]]
        early = total_of([term[rows[0]] for term in whole]).astype(BF16)
        late = total_of([term[rows[1]] for term in whole]).astype(BF16)
        early, late = after(early, late)
        early_came = flip(early, bits_of)
        late, early_came = after(late, early_came)
        sends[chunk] = [term[rows[2]] for term in whole] + [early_came]
        terms[chunk] = [term[rows[3]] for term in whole] + [flip(late, bits_of)]

    def exchange(chunk, stage, earlier=None):
        if sends[chunk] is None:
            half = terms[chunk][0].shape[0] // 2
            sends[chunk] = [term[:half] for term in terms[chunk]]
            terms[chunk] = [term[half:] for term in terms[chunk]]
        sent = total_of(sends[chunk]).astype(BF16)
        sends[chunk] = None
        if earlier is not None:
            sent, _ = after(sent, earlier)
        came[chunk, stage] = flip(sent, HALVING[ORDERS[chunk][stage]])
        terms[chunk] = terms[chunk] + [came[chunk, stage]]
        return sent

    terms[0] = makers[0](None)
    terms[1] = makers[1](exchange(0, 0))
    split_exchange(1)
    exchange(0, 1)
    exchange(1, 1)
    exchange(0, 2)
    exchange(1, 2)
    exchange(1, 3, came[0, 2])
    exchange(0, 3)
    return [total_of([term[0] for term in chunk]) for chunk in terms]


HEAD_STAGES = (
    lambda core: ZHIGH if core else Y,
    lambda core: ZLOW if core else ZHIGH,
    lambda core: Y if core else ZLOW,
)


def head_bits(place, core):
    bits = [(place >> stage) & 1 for stage in range(3)]
    return jnp.where(
        core == 0,
        bits[0] | (bits[1] << 2) | (bits[2] << 1),
        (bits[0] << 2) | (bits[1] << 1) | bits[2],
    )


def gather_heads(heads, beside):
    first, second, third = HEAD_STAGES
    heads = heads[None]
    heads = jnp.concatenate([heads, flip(heads, first)], axis=0)
    came = flip(heads, second)
    early = flip(heads, third)
    late, (early, beside) = after(came, (early, beside))
    return [heads, came, early, flip(late, third)], beside


def pack_kernel(member_ref, residual_ref, ids_ref, weights_ref, out_ref):
    groups, rows, lanes = out_ref.shape
    here, width = residual_ref.shape
    each = width // groups
    rest = weights_ref[...] / jnp.sum(weights_ref[...], axis=0, keepdims=True)
    parts = [ids_ref[...].astype(F32)]
    for _ in range(3):
        part = rest.astype(BF16).astype(F32)
        parts.append(part)
        rest = rest - part
    table = jnp.concatenate(parts, axis=0).astype(BF16)
    for group in range(groups):
        column = pl.multiple_of(group * each + member_ref[0] * lanes, lanes)
        out_ref[group, :here, :] = residual_ref[:, pl.ds(column, lanes)]
        out_ref[group, here:, :] = table


def pack(member, residual, route_ids, route_weights, groups):
    here, top = route_ids.shape
    vmem = pl.BlockSpec(memory_space=pltpu.VMEM)
    return pl.pallas_call(
        pack_kernel,
        in_specs=[pl.BlockSpec(memory_space=pltpu.SMEM), vmem, vmem, vmem],
        out_specs=vmem,
        out_shape=jax.ShapeDtypeStruct((groups, here + 4 * top, LANES), BF16),
        compiler_params=pltpu.CompilerParams(vmem_limit_bytes=16 * 1024 * 1024),
        cost_estimate=pl.CostEstimate(
            flops=0, bytes_accessed=3 * residual.size, transcendentals=0
        ),
        name="pack",
    )(member.reshape(1), residual, route_ids.T, route_weights.T)


def own_routes(table, group, experts):
    groups, rows, here = table.shape
    top = rows // 4
    own = group * experts + jnp.arange(experts, dtype=jnp.int32)
    table = table.astype(F32).reshape(groups, 4, top, here)
    ids = table[:, 0].astype(jnp.int32)
    match = ids[None] == own[:, None, None, None]
    named = jnp.any(match, axis=2)
    shares = table[:, 1] + table[:, 2] + table[:, 3]
    weights = jnp.sum(jnp.where(match, shares[None], 0.0), axis=2)
    span = PAIR * here
    order = jnp.arange(span)
    earlier = (order[:, None] < order[None, :]).astype(BF16)
    rank = jnp.dot(
        named.astype(BF16).reshape(experts * groups // PAIR, span),
        earlier,
        preferred_element_type=F32,
    )
    slots = jnp.where(named, rank.reshape(named.shape).astype(jnp.int32), -1)
    return slots.reshape(experts, groups * here), weights.reshape(experts, groups * here)


def block_table(device, groups, member):
    number = jnp.arange(32, dtype=jnp.int32)
    array, place = number >> 3, number & 7
    source_core = (device & 1) ^ (array >> 1)
    first = jnp.where(source_core == 0, X, Y)
    last = jnp.where(source_core == 0, Y, X)
    feature = (
        device
        ^ (array >> 1)
        ^ jnp.where(array & 1 == 1, first, 0)
        ^ jnp.where(place & 1 == 1, last, 0)
        ^ jnp.where(place & 2 == 2, ZHIGH, 0)
        ^ jnp.where(place & 4 == 4, ZLOW, 0)
    )
    swapped = ((feature ^ device) >> 2) & 1
    return jnp.concatenate([feature, swapped, jnp.stack([member, device >> 3])])


def gather_blocks(first, second):
    def along(bits, block):
        return flip(block, lambda core: bits)

    def joined(held, came):
        return jnp.concatenate([held, came], axis=0)

    first_last = flip(first, last_axis)
    second_high = along(ZHIGH, second)
    second, _ = after(joined(second, second_high), first_last)
    second_low = along(ZLOW, second)
    first, _ = after(joined(first, first_last), second_high)
    first_high = along(ZHIGH, first)
    second, first_high = after(joined(second, second_low), first_high)
    second_last = flip(second, last_axis)
    first = joined(first, first_high)
    first_low = along(ZLOW, first)
    halves = []
    for early, late in ((first, first_low), (second, second_last)):
        early_first = flip(early, first_axis)
        late, early_first = after(late, early_first)
        late_first = flip(late, first_axis)
        halves.append(
            [
                [block, came, along(CORE, block), along(CORE, came)]
                for block, came in ((early, early_first), (late, late_first))
            ]
        )
    return halves


def per_device_tokens(
    attn_heads, out_proj, residual, norm_gain, route_ids, route_weights, w_gate, w_up, w_down
):
    groups, members = lax.axis_size("expert"), lax.axis_size("tensor")
    group, member = lax.axis_index("expert"), lax.axis_index("tensor")
    device = group * members + member
    here, width = residual.shape
    experts = w_gate.shape[0]
    rows = -(-PAIR * CAP // 16) * 16
    x_side, core, y_side = member >> 1, member & 1, group & 1

    moved = lax.all_to_all(
        pack(member, residual, route_ids, route_weights, groups),
        "expert",
        split_axis=0,
        concat_axis=0,
        tiled=True,
    )
    gain = lax.dynamic_index_in_dim(
        norm_gain.reshape(groups * members, LANES), device, 0, keepdims=False
    )

    pieces, moved = gather_heads(attn_heads, moved)
    numbers = jnp.arange(groups, dtype=jnp.int32)
    arrival = (head_bits(numbers, core) ^ group) ^ y_side
    info = jnp.concatenate(
        [jnp.stack([core, x_side]), ((arrival & 1) << 2) | (arrival >> 1)]
    )
    table = jnp.take(moved[:, here:], own_order(groups, group), axis=0, mode="clip")
    moved = moved[:, :here].reshape(groups // 2, 2, here, LANES)
    slots, weights = own_routes(table, group, experts)
    info, (slots, weights) = after(info, (slots, weights))
    send, keep = project(info, pieces, out_proj)
    came = flip(send, lambda c: CORE)
    from_x = flip(total_of([keep[0], came[0]]).astype(BF16), lambda c: X)
    starts = []
    each = groups // 2
    for half in range(2):
        window = slice(half * each, (half + 1) * each)
        hidden = lax.dynamic_index_in_dim(moved, y_side ^ half, 1, keepdims=False).astype(F32)
        hidden = hidden + total_of([keep[1, window], came[1, window], from_x[window]])
        starts.append((hidden * gain).astype(BF16)[None])

    x = [block for half in gather_blocks(*starts) for part in half for block in part]
    invgain = (1.0 / norm_gain).reshape(groups * members, LANES)
    act, own_hidden, spread = gate_up(
        block_table(device, groups, member), slots, weights, invgain, x, w_gate, w_up, rows, members
    )

    cols = width // members

    def columns_of(to_core, chunk, chunks, orders):
        sides = jnp.stack([1 - x_side, x_side])
        blocks = (sides * 2 + to_core) * chunks + chunk
        places = [halving_places(to_core, group, groups, order) for order in orders]
        return jnp.concatenate([blocks] + places)

    chunks = len(ORDERS)
    chunk_cols = cols // chunks
    other = down(
        columns_of(1 - core, 0, 1, ORDERS), spread, act, w_down, rows, groups, cols, chunks
    )
    came = [flip(piece, lambda c: CORE) for piece in other]

    def terms_of(chunk, earlier):
        place = columns_of(core, chunk, chunks, ORDERS[chunk : chunk + 1])
        if earlier is not None:
            place, _ = after(place, earlier)
        (kept,) = down(place, spread, act, w_down, rows, groups, chunk_cols, 1)
        return [kept, came[chunk]]

    sums = reduce_chunks([functools.partial(terms_of, chunk) for chunk in range(chunks)])
    mixture = jnp.concatenate(sums, axis=1)
    return (own_hidden + mixture).astype(BF16)


def solution(mesh):
    groups, members = mesh.shape["expert"], mesh.shape["tensor"]
    placed = (
        P("expert", "tensor"),
        P("tensor", "expert"),
        P("expert", None),
        P(),
        P("expert", None),
        P("expert", None),
        P("expert", None, "tensor"),
        P("expert", None, "tensor"),
        P("expert", "tensor", None),
    )

    def run(*arrays):
        tokens, width = arrays[2].shape
        whole_tokens = (groups, members) == (8, 4) and width == groups * members * LANES
        body = per_device_tokens if whole_tokens else per_device_slots
        return jax.shard_map(
            body, mesh=mesh, in_specs=placed, out_specs=P("expert", "tensor"), check_vma=False
        )(*arrays)

    return run
```

```python
import functools

import jax
import jax.numpy as jnp
from jax import lax
from jax.experimental import pallas as pl
from jax.experimental.pallas import tpu as pltpu
from jax.sharding import PartitionSpec as P

EXPERTS = 64
CAP = 18
BF16 = jnp.bfloat16
F32 = jnp.float32
PAIR = 2
LANES = 128


def slot_places(ids, experts, capacity):
    row_count, top_count = ids.shape
    onehot = (ids[:, :, None] == jnp.arange(experts, dtype=jnp.int32)[None, None, :]).astype(
        jnp.int32
    )
    flattened = onehot.reshape(row_count * top_count, experts)
    before = jnp.cumsum(flattened, axis=0) - flattened
    slot_rank = jnp.sum(before * flattened, axis=1).reshape(row_count, top_count)
    return ids * capacity + slot_rank


def per_device_slots(
    attn_heads, out_proj, residual, norm_gain, route_ids, route_weights, w_gate, w_up, w_down
):
    model_width = residual.shape[1]
    groups = lax.axis_size("expert")
    members = lax.axis_size("tensor")
    member = lax.axis_index("tensor")
    per_group = w_gate.shape[0]
    slot_count = EXPERTS * CAP
    block_cols = model_width // members
    heads_out = jnp.dot(
        attn_heads,
        lax.all_gather(out_proj, "expert", axis=1, tiled=True),
        preferred_element_type=F32,
    )
    attn_out = lax.psum(heads_out.astype(BF16), "tensor").astype(F32)
    hidden = residual.astype(F32) + attn_out
    normed = (
        hidden * lax.rsqrt(jnp.mean(hidden * hidden, axis=-1, keepdims=True) + 1e-06) * norm_gain
    ).astype(BF16)
    slot_index = slot_places(route_ids, EXPERTS, CAP)
    slot_range = jnp.arange(slot_count, dtype=jnp.int32)
    slot_hits = jnp.sum(
        (slot_index[:, :, None] == slot_range[None, None, :]).astype(BF16), axis=1
    )
    buffer = jnp.einsum("rj,rd->jd", slot_hits, normed, preferred_element_type=F32).astype(BF16)
    buffer = buffer.reshape(groups, per_group, CAP, model_width)
    arrived = lax.all_to_all(buffer, "expert", split_axis=0, concat_axis=0, tiled=True)
    gate_acc = jnp.einsum("gxcd,xdf->gxcf", arrived, w_gate, preferred_element_type=F32)
    upper = jnp.einsum("gxcd,xdf->gxcf", arrived, w_up, preferred_element_type=F32)
    activation = (jax.nn.silu(gate_acc) * upper).astype(BF16)
    product_term = jnp.einsum("gxcf,xfd->gxcd", activation, w_down, preferred_element_type=F32)
    product_term = product_term.astype(BF16).reshape(groups, per_group, CAP, members, block_cols)
    expert_out = lax.psum_scatter(
        jnp.transpose(product_term, (3, 0, 1, 2, 4)), "tensor", scatter_dimension=0, tiled=True
    )[0]
    returned = lax.all_to_all(expert_out, "expert", split_axis=0, concat_axis=0, tiled=True)
    weights = route_weights / jnp.sum(route_weights, axis=-1, keepdims=True)
    picked = returned.reshape(slot_count, block_cols)[slot_index]
    mixture = jnp.sum(weights[:, :, None] * picked.astype(F32), axis=1)
    own_hidden = lax.dynamic_slice_in_dim(hidden, member * block_cols, block_cols, 1)
    return (own_hidden + mixture).astype(BF16)


def hits_of(slot_row, rows):
    places = lax.broadcasted_iota(jnp.int32, (rows, slot_row.shape[1]), 0)
    return places == slot_row


def project_kernel(info_ref, head_refs, weight_ref, send_ref, keep_ref):
    core, x_side = info_ref[0], info_ref[1]
    pieces = [ref.at[i] for ref in head_refs for i in range(ref.shape[0])]
    here = pieces[0].shape[0]
    each = len(pieces) // 2
    for part in range(2):
        result = jnp.dot(
            jnp.concatenate([ref[...] for ref in pieces[part * each : (part + 1) * each]]),
            weight_ref[...],
            preferred_element_type=F32,
        ).astype(BF16)
        for to_x in range(2):
            x_kept = (x_side == to_x).astype(jnp.int32)
            for to_core in range(2):
                start = (to_x * 2 + to_core) * LANES
                for out_ref, wanted in ((keep_ref, core == to_core), (send_ref, core != to_core)):

                    @pl.when(wanted)
                    def _(out_ref=out_ref, x_kept=x_kept, start=start, part=part, result=result):
                        for piece in range(each):
                            out_ref[x_kept, info_ref[2 + part * each + piece]] = result[
                                piece * here : (piece + 1) * here, start : start + LANES
                            ]


def project(info, pieces, out_proj):
    here = pieces[0].shape[1]
    groups = sum(piece.shape[0] for piece in pieces)
    out = jax.ShapeDtypeStruct((2, groups, here, LANES), BF16)
    vmem = pl.BlockSpec(memory_space=pltpu.VMEM)

    def kernel(info_ref, *refs):
        project_kernel(info_ref, refs[: len(pieces)], *refs[len(pieces) :])

    return pl.pallas_call(
        kernel,
        in_specs=[pl.BlockSpec(memory_space=pltpu.SMEM)] + [vmem] * (len(pieces) + 1),
        out_specs=[vmem, vmem],
        out_shape=[out, out],
        compiler_params=pltpu.CompilerParams(vmem_limit_bytes=24 * 1024 * 1024),
        cost_estimate=pl.CostEstimate(
            flops=2 * groups * here * out_proj.size,
            bytes_accessed=2 * (out_proj.size + 2 * groups * pieces[0][0].size),
            transcendentals=0,
        ),
        name="project",
    )(info, *pieces, out_proj)


def gate_up_kernel(
    experts, rows, width, info_ref, slot_ref, weight_ref, invgain_ref, x_refs, wg_ref, wu_ref,
    act_ref, hidden_ref, spread_ref, xs_ref, sq_ref, scale_ref, hits_ref
):
    expert = pl.program_id(0)
    arrays = 4
    own_refs = (x_refs[:arrays], x_refs[arrays : 2 * arrays])
    other_refs = (x_refs[2 * arrays : 3 * arrays], x_refs[3 * arrays :])
    parts, here, lanes = x_refs[0].shape[1:]
    blocks = info_ref.shape[0] // 2 - 1
    each = blocks // arrays
    span = 2 * here
    member, z = info_ref[2 * blocks], info_ref[2 * blocks + 1]

    def block_at(array, last, high, low):
        return (
            array * each + low * 4 + high * 2 + last,
            own_refs[low][array].at[high * 2 + last],
            other_refs[last][array].at[low * 2 + high],
        )

    @pl.when(expert == 0)
    def _():
        sq_ref[...] = jnp.zeros_like(sq_ref)
        for part in range(parts):
            for e in range(experts):
                first = hits_of(slot_ref[e : e + 1, part * span : part * span + here], rows)
                second = hits_of(
                    slot_ref[e : e + 1, part * span + here : (part + 1) * span], rows
                )
                first = first.astype(F32).astype(BF16)
                second = second.astype(F32).astype(BF16)
                window = slice(e * rows, (e + 1) * rows)
                hits_ref[0, part, window, :] = jnp.concatenate([first, second], axis=1)
                hits_ref[1, part, window, :] = jnp.concatenate([second, first], axis=1)
            spread_ref[part] = jnp.transpose(hits_ref[0, part].astype(F32)).astype(BF16)

        def pairs_of_blocks(high, carry):
            for array in range(arrays):
                for last in range(2):
                    pair = [block_at(array, last, high, low) for low in range(2)]
                    swapped = info_ref[blocks + pair[0][0]]
                    features = [info_ref[place] for place, _, _ in pair]
                    for feature, (_, own, other) in zip(features, pair):
                        invgain = invgain_ref[pl.ds(feature, 1), :]
                        for part in range(parts):
                            for half, block in enumerate((own, other)):
                                value = block[part].astype(F32) * invgain
                                sq_ref[swapped, part, half] += value * value
                    for part in range(parts):
                        both = jnp.concatenate(
                            [
                                jnp.concatenate([own[part], other[part]], axis=0)
                                for _, own, other in pair
                            ],
                            axis=1,
                        )
                        picked = jnp.dot(
                            hits_ref[swapped, part], both, preferred_element_type=F32
                        ).astype(BF16)
                        for number, feature in enumerate(features):
                            column = pl.multiple_of(feature * lanes, lanes)
                            for e in range(experts):
                                xs_ref[
                                    e, part * rows : (part + 1) * rows, pl.ds(column, lanes)
                                ] = picked[
                                    e * rows : (e + 1) * rows, number * lanes : (number + 1) * lanes
                                ]
            return carry

        lax.fori_loop(0, 2, pairs_of_blocks, 0)

        def own_blocks(high, carry):
            for array in range(arrays):
                for last in range(2):
                    for low in range(2):
                        place, own, other = block_at(array, last, high, low)
                        feature = info_ref[place]

                        @pl.when(feature >> 3 == member)
                        def _(place=place, feature=feature, own=own, other=other):
                            mine = jnp.where(
                                info_ref[blocks + place] == 0,
                                own[z].astype(F32),
                                other[z].astype(F32),
                            )
                            column = pl.multiple_of((feature & 7) * lanes, lanes)
                            hidden_ref[:, pl.ds(column, lanes)] = (
                                mine * invgain_ref[pl.ds(feature, 1), :]
                            )

            return carry

        lax.fori_loop(0, 2, own_blocks, 0)
        pieces = [
            sq_ref[0, part, half] + sq_ref[1, part, 1 - half]
            for part in range(parts)
            for half in range(2)
        ]
        total = jnp.sum(
            jnp.transpose(jnp.concatenate(pieces, axis=0)), axis=0, keepdims=True
        )
        scale_ref[...] = jnp.broadcast_to(lax.rsqrt(total / width + 1e-06), scale_ref.shape)

    summed = jnp.dot(
        xs_ref[expert],
        jnp.concatenate([wg_ref[0], wu_ref[0]], axis=1),
        preferred_element_type=F32,
    )
    hidden_units = wg_ref.shape[2]
    for part in range(parts):
        window = slice(part * span, (part + 1) * span)
        hits = hits_of(slot_ref[pl.ds(expert, 1), window], rows)
        scale = jnp.sum(jnp.where(hits, scale_ref[0:1, window], 0.0), axis=1, keepdims=True)
        weight = jnp.sum(
            jnp.where(hits, weight_ref[pl.ds(expert, 1), window], 0.0), axis=1, keepdims=True
        )
        both_part = summed[part * rows : (part + 1) * rows, :]
        gate = both_part[:, :hidden_units] * scale
        upper = both_part[:, hidden_units:] * scale
        act = gate / (1.0 + jnp.exp(-gate)) * upper * weight
        act_ref[expert, part * rows : (part + 1) * rows, :] = act.astype(BF16)


def gate_up(info, slots, weights, invgain, x, w_gate, w_up, rows, members):
    experts, width, hidden_units = w_gate.shape
    parts, here, lanes = x[0].shape[1:]
    tokens = slots.shape[1]

    def kernel(info_ref, slot_ref, weight_ref, invgain_ref, *rest):
        gate_up_kernel(
            experts, rows, width, info_ref, slot_ref, weight_ref, invgain_ref,
            rest[: len(x)], *rest[len(x) :]
        )

    def whole(shape):
        return pl.BlockSpec(
            shape, lambda e, info: (0,) * len(shape), pipeline_mode=pl.Buffered(1)
        )

    return pl.pallas_call(
        kernel,
        grid_spec=pltpu.PrefetchScalarGridSpec(
            num_scalar_prefetch=1,
            grid=(experts,),
            in_specs=[whole(slots.shape), whole(weights.shape), whole(invgain.shape)]
            + [pl.BlockSpec(memory_space=pltpu.VMEM)] * len(x)
            + [pl.BlockSpec((1, width, hidden_units), lambda e, info: (e, 0, 0))] * 2,
            out_specs=[
                pl.BlockSpec(memory_space=pltpu.VMEM),
                pl.BlockSpec(memory_space=pltpu.VMEM),
                pl.BlockSpec(memory_space=pltpu.VMEM),
            ],
            scratch_shapes=[
                pltpu.VMEM((experts, parts * rows, width), BF16),
                pltpu.VMEM((2, parts, 2, here, lanes), F32),
                pltpu.VMEM((8, tokens), F32),
                pltpu.VMEM((2, parts, experts * rows, 2 * here), BF16),
            ],
        ),
        out_shape=[
            jax.ShapeDtypeStruct((experts, parts * rows, hidden_units), BF16),
            jax.ShapeDtypeStruct((here, width // members), F32),
            jax.ShapeDtypeStruct((parts, 2 * here, experts * rows), BF16),
        ],
        compiler_params=pltpu.CompilerParams(
            vmem_limit_bytes=36 * 1024 * 1024, dimension_semantics=("arbitrary",)
        ),
        cost_estimate=pl.CostEstimate(
            flops=2 * experts * parts * rows * width * 2 * hidden_units,
            bytes_accessed=4 * experts * width * hidden_units + 2 * len(x) * x[0].size,
            transcendentals=0,
        ),
        name="gate_up",
    )(info, slots, weights, invgain, *x, w_gate, w_up)


def down_kernel(rows, place_ref, spread_ref, act_ref, wd0_ref, wd1_ref, *rest):
    out_refs, ys_ref = rest[:-1], rest[-1]
    out_cols = out_refs[0].shape[2]
    step = pl.program_id(0)
    experts, all_rows, _ = act_ref.shape
    per_step = wd0_ref.shape[0]
    parts = all_rows // rows
    groups = parts * PAIR
    for number in range(per_step):
        expert = step * per_step + number
        for side, wd_ref in enumerate((wd0_ref, wd1_ref)):
            result = jnp.dot(
                act_ref[expert], wd_ref[number], preferred_element_type=F32
            ).astype(BF16)
            for part in range(parts):
                ys_ref[side, part, expert] = result[part * rows : (part + 1) * rows, :]

    @pl.when(step == pl.num_programs(0) - 1)
    def _():
        for part in range(parts):
            for side in range(2):
                picked = ys_ref[side, part].reshape(experts * rows, ys_ref.shape[4])
                mixed = jnp.dot(
                    spread_ref[part], picked, preferred_element_type=F32
                ).astype(BF16)
                for i in range(PAIR):
                    for number, out_ref in enumerate(out_refs):
                        block = (number * 2 + side) * groups + part * PAIR + i
                        target = place_ref[2 + block]
                        out_ref[target] = mixed[
                            i * 128 : (i + 1) * 128, number * out_cols : (number + 1) * out_cols
                        ]


def down(place, spread, act, w_down, rows, groups, cols, chunks, per_step=2):
    experts, hidden_units, width = w_down.shape
    parts, span, _ = spread.shape
    here = parts * span // groups
    out = jax.ShapeDtypeStruct((2 * groups, here, cols // chunks), BF16)
    return pl.pallas_call(
        functools.partial(down_kernel, rows),
        grid_spec=pltpu.PrefetchScalarGridSpec(
            num_scalar_prefetch=1,
            grid=(experts // per_step,),
            in_specs=[
                pl.BlockSpec(memory_space=pltpu.VMEM),
                pl.BlockSpec(memory_space=pltpu.VMEM),
                pl.BlockSpec((per_step, hidden_units, cols), lambda e, p: (e, 0, p[0])),
                pl.BlockSpec((per_step, hidden_units, cols), lambda e, p: (e, 0, p[1])),
            ],
            out_specs=[pl.BlockSpec(out.shape, lambda e, p: (0, 0, 0))] * chunks,
            scratch_shapes=[pltpu.VMEM((2, parts, experts, rows, cols), BF16)],
        ),
        out_shape=[out] * chunks,
        compiler_params=pltpu.CompilerParams(
            vmem_limit_bytes=36 * 1024 * 1024, dimension_semantics=("arbitrary",)
        ),
        cost_estimate=pl.CostEstimate(
            flops=8 * experts * parts * rows * cols * hidden_units,
            bytes_accessed=4 * experts * cols * hidden_units + 4 * parts * span * cols,
            transcendentals=0,
        ),
        name="down_mix",
    )(place, spread, act, w_down, w_down)


def flip(array, bits_of):
    pairs = []
    for index in range(32):
        pairs.append((index, index ^ bits_of(index & 1)))
    return lax.ppermute(array, ("expert", "tensor"), pairs)


CORE, X, Y, ZLOW, ZHIGH = 1, 2, 4, 8, 16


def first_axis(core):
    return Y if core else X


def last_axis(core):
    return X if core else Y


def own_order(groups, group):
    order = jnp.arange(groups, dtype=jnp.int32)
    return order ^ (group & 1)


HALVING = {
    "first": first_axis,
    "last": last_axis,
    "low": lambda core: ZLOW,
    "high": lambda core: ZHIGH,
}
ORDERS = (("first", "low", "high", "last"), ("first", "last", "low", "high"))


def halving_places(to_core, group, groups, order):
    g = own_order(groups, group)[None, :]
    y_kept = ((g & 1) == (group & 1)).astype(jnp.int32)
    x_kept = jnp.arange(2, dtype=jnp.int32)[:, None]
    kept = {
        "first": jnp.where(to_core == 0, x_kept, y_kept),
        "last": jnp.where(to_core == 0, y_kept, x_kept),
        "low": (((g >> 1) & 1) == ((group >> 1) & 1)).astype(jnp.int32),
        "high": ((g >> 2) == (group >> 2)).astype(jnp.int32),
    }
    place = 0
    for axis in order:
        place = place * 2 + kept[axis]
    return place.reshape(-1)


def total_of(terms):
    total = terms[0].astype(F32)
    for term in terms[1:]:
        total = total + term.astype(F32)
    return total


def after(value, earlier):
    return lax.optimization_barrier((value, earlier))


def reduce_chunks(makers):
    terms, sends, came = [None, None], [None, None], {}

    def split_exchange(chunk):
        whole = terms[chunk]
        quarter = whole[0].shape[0] // 4
        rows = [slice(i * quarter, (i + 1) * quarter) for i in range(4)]
        bits_of = HALVING[ORDERS[chunk][0]]
        early = total_of([term[rows[0]] for term in whole]).astype(BF16)
        late = total_of([term[rows[1]] for term in whole]).astype(BF16)
        early, late = after(early, late)
        early_came, _ = after(flip(early, bits_of), exchange(0, 1))
        late, early_came = after(late, early_came)
        sends[chunk] = [term[rows[2]] for term in whole] + [early_came]
        terms[chunk] = [term[rows[3]] for term in whole] + [flip(late, bits_of)]

    def exchange(chunk, stage, earlier=None):
        if sends[chunk] is None:
            half = terms[chunk][0].shape[0] // 2
            sends[chunk] = [term[:half] for term in terms[chunk]]
            terms[chunk] = [term[half:] for term in terms[chunk]]
        sent = total_of(sends[chunk]).astype(BF16)
        sends[chunk] = None
        if earlier is not None:
            sent, _ = after(sent, earlier)
        came[chunk, stage] = flip(sent, HALVING[ORDERS[chunk][stage]])
        terms[chunk] = terms[chunk] + [came[chunk, stage]]
        return sent

    terms[0] = makers[0](None)
    terms[1] = makers[1](exchange(0, 0))
    split_exchange(1)
    exchange(1, 1)
    exchange(0, 2)
    exchange(1, 2)
    exchange(1, 3, came[0, 2])
    exchange(0, 3)
    return [total_of([term[0] for term in chunk]) for chunk in terms]


HEAD_STAGES = (
    lambda core: ZHIGH,
    lambda core: ZLOW if core else Y,
    lambda core: Y if core else ZLOW,
)


def head_bits(place, core):
    bits = [(place >> stage) & 1 for stage in range(3)]
    return jnp.where(
        core == 0,
        (bits[0] << 2) | bits[1] | (bits[2] << 1),
        (bits[0] << 2) | (bits[1] << 1) | bits[2],
    )


def gather_heads(heads, beside):
    first, second, third = HEAD_STAGES
    heads = heads[None]
    heads = jnp.concatenate([heads, flip(heads, first)], axis=0)
    came = flip(heads, second)
    early = flip(heads, third)
    late, (early, beside) = after(came, (early, beside))
    return [heads, came, early, flip(late, third)], beside


def pack_kernel(member_ref, residual_ref, ids_ref, weights_ref, out_ref):
    groups, rows, lanes = out_ref.shape
    here, width = residual_ref.shape
    each = width // groups
    rest = weights_ref[...] / jnp.sum(weights_ref[...], axis=0, keepdims=True)
    parts = [ids_ref[...].astype(F32)]
    for _ in range(3):
        part = rest.astype(BF16).astype(F32)
        parts.append(part)
        rest = rest - part
    table = jnp.concatenate(parts, axis=0).astype(BF16)
    for group in range(groups):
        column = pl.multiple_of(group * each + member_ref[0] * lanes, lanes)
        out_ref[group, :here, :] = residual_ref[:, pl.ds(column, lanes)]
        out_ref[group, here:, :] = table


def pack(member, residual, route_ids, route_weights, groups):
    here, top = route_ids.shape
    vmem = pl.BlockSpec(memory_space=pltpu.VMEM)
    return pl.pallas_call(
        pack_kernel,
        in_specs=[pl.BlockSpec(memory_space=pltpu.SMEM), vmem, vmem, vmem],
        out_specs=vmem,
        out_shape=jax.ShapeDtypeStruct((groups, here + 4 * top, LANES), BF16),
        compiler_params=pltpu.CompilerParams(vmem_limit_bytes=16 * 1024 * 1024),
        cost_estimate=pl.CostEstimate(
            flops=0, bytes_accessed=3 * residual.size, transcendentals=0
        ),
        name="pack",
    )(member.reshape(1), residual, route_ids.T, route_weights.T)


def own_routes(table, group, experts):
    groups, rows, here = table.shape
    top = rows // 4
    own = group * experts + jnp.arange(experts, dtype=jnp.int32)
    table = table.astype(F32).reshape(groups, 4, top, here)
    ids = table[:, 0].astype(jnp.int32)
    match = ids[None] == own[:, None, None, None]
    named = jnp.any(match, axis=2)
    shares = table[:, 1] + table[:, 2] + table[:, 3]
    weights = jnp.sum(jnp.where(match, shares[None], 0.0), axis=2)
    span = PAIR * here
    order = jnp.arange(span)
    earlier = (order[:, None] < order[None, :]).astype(BF16)
    rank = jnp.dot(
        named.astype(BF16).reshape(experts * groups // PAIR, span),
        earlier,
        preferred_element_type=F32,
    )
    slots = jnp.where(named, rank.reshape(named.shape).astype(jnp.int32), -1)
    return slots.reshape(experts, groups * here), weights.reshape(experts, groups * here)


def block_table(device, groups, member):
    number = jnp.arange(32, dtype=jnp.int32)
    array, place = number >> 3, number & 7
    source_core = (device & 1) ^ (array >> 1)
    first = jnp.where(source_core == 0, X, Y)
    last = jnp.where(source_core == 0, Y, X)
    feature = (
        device
        ^ (array >> 1)
        ^ jnp.where(array & 1 == 1, first, 0)
        ^ jnp.where(place & 1 == 1, last, 0)
        ^ jnp.where(place & 2 == 2, ZHIGH, 0)
        ^ jnp.where(place & 4 == 4, ZLOW, 0)
    )
    swapped = ((feature ^ device) >> 2) & 1
    return jnp.concatenate([feature, swapped, jnp.stack([member, device >> 3])])


def gather_blocks(first, second):
    def along(bits, block):
        return flip(block, lambda core: bits)

    def joined(held, came):
        return jnp.concatenate([held, came], axis=0)

    first_last = flip(first, last_axis)
    second_high = along(ZHIGH, second)
    second, _ = after(joined(second, second_high), first_last)
    second_low = along(ZLOW, second)
    first, _ = after(joined(first, first_last), second_high)
    first_high = along(ZHIGH, first)
    second, first_high = after(joined(second, second_low), first_high)
    second_last = flip(second, last_axis)
    first = joined(first, first_high)
    first_low = along(ZLOW, first)
    halves = []
    for early, late in ((first, first_low), (second, second_last)):
        early_first = flip(early, first_axis)
        late, early_first = after(late, early_first)
        late_first = flip(late, first_axis)
        halves.append(
            [
                [block, came, along(CORE, block), along(CORE, came)]
                for block, came in ((early, early_first), (late, late_first))
            ]
        )
    return halves


def per_device_tokens(
    attn_heads, out_proj, residual, norm_gain, route_ids, route_weights, w_gate, w_up, w_down
):
    groups, members = lax.axis_size("expert"), lax.axis_size("tensor")
    group, member = lax.axis_index("expert"), lax.axis_index("tensor")
    device = group * members + member
    here, width = residual.shape
    experts = w_gate.shape[0]
    rows = -(-PAIR * CAP // 16) * 16
    x_side, core, y_side = member >> 1, member & 1, group & 1

    moved = lax.all_to_all(
        pack(member, residual, route_ids, route_weights, groups),
        "expert",
        split_axis=0,
        concat_axis=0,
        tiled=True,
    )
    gain = lax.dynamic_index_in_dim(
        norm_gain.reshape(groups * members, LANES), device, 0, keepdims=False
    )

    pieces, moved = gather_heads(attn_heads, moved)
    numbers = jnp.arange(groups, dtype=jnp.int32)
    arrival = (head_bits(numbers, core) ^ group) ^ y_side
    info = jnp.concatenate(
        [jnp.stack([core, x_side]), ((arrival & 1) << 2) | (arrival >> 1)]
    )
    table = jnp.take(moved[:, here:], own_order(groups, group), axis=0, mode="clip")
    moved = moved[:, :here].reshape(groups // 2, 2, here, LANES)
    slots, weights = own_routes(table, group, experts)
    info, (slots, weights) = after(info, (slots, weights))
    send, keep = project(info, pieces, out_proj)
    came = flip(send, lambda c: CORE)
    from_x = flip(total_of([keep[0], came[0]]).astype(BF16), lambda c: X)
    starts = []
    each = groups // 2
    for half in range(2):
        window = slice(half * each, (half + 1) * each)
        hidden = lax.dynamic_index_in_dim(moved, y_side ^ half, 1, keepdims=False).astype(F32)
        hidden = hidden + total_of([keep[1, window], came[1, window], from_x[window]])
        starts.append((hidden * gain).astype(BF16)[None])

    x = [block for half in gather_blocks(*starts) for part in half for block in part]
    invgain = (1.0 / norm_gain).reshape(groups * members, LANES)
    act, own_hidden, spread = gate_up(
        block_table(device, groups, member), slots, weights, invgain, x, w_gate, w_up, rows, members
    )

    cols = width // members

    def columns_of(to_core, chunk, chunks, orders):
        sides = jnp.stack([1 - x_side, x_side])
        blocks = (sides * 2 + to_core) * chunks + chunk
        places = [halving_places(to_core, group, groups, order) for order in orders]
        return jnp.concatenate([blocks] + places)

    chunks = len(ORDERS)
    chunk_cols = cols // chunks
    other = down(
        columns_of(1 - core, 0, 1, ORDERS), spread, act, w_down, rows, groups, cols, chunks
    )
    came = [flip(piece, lambda c: CORE) for piece in other]

    def terms_of(chunk, earlier):
        place = columns_of(core, chunk, chunks, ORDERS[chunk : chunk + 1])
        if earlier is not None:
            place, _ = after(place, earlier)
        (kept,) = down(place, spread, act, w_down, rows, groups, chunk_cols, 1)
        return [kept, came[chunk]]

    sums = reduce_chunks([functools.partial(terms_of, chunk) for chunk in range(chunks)])
    mixture = jnp.concatenate(sums, axis=1)
    return (own_hidden + mixture).astype(BF16)


def solution(mesh):
    groups, members = mesh.shape["expert"], mesh.shape["tensor"]
    placed = (
        P("expert", "tensor"),
        P("tensor", "expert"),
        P("expert", None),
        P(),
        P("expert", None),
        P("expert", None),
        P("expert", None, "tensor"),
        P("expert", None, "tensor"),
        P("expert", "tensor", None),
    )

    def run(*arrays):
        tokens, width = arrays[2].shape
        whole_tokens = (groups, members) == (8, 4) and width == groups * members * LANES
        body = per_device_tokens if whole_tokens else per_device_slots
        return jax.shard_map(
            body, mesh=mesh, in_specs=placed, out_specs=P("expert", "tensor"), check_vma=False
        )(*arrays)

    return run
```

```python
import functools

import jax
import jax.numpy as jnp
from jax import lax
from jax.experimental import pallas as pl
from jax.experimental.pallas import tpu as pltpu
from jax.sharding import PartitionSpec as P

EXPERTS = 64
CAP = 18
BF16 = jnp.bfloat16
F32 = jnp.float32
PAIR = 2
LANES = 128


def slot_places(ids, experts, capacity):
    row_count, top_count = ids.shape
    onehot = (ids[:, :, None] == jnp.arange(experts, dtype=jnp.int32)[None, None, :]).astype(
        jnp.int32
    )
    flattened = onehot.reshape(row_count * top_count, experts)
    before = jnp.cumsum(flattened, axis=0) - flattened
    slot_rank = jnp.sum(before * flattened, axis=1).reshape(row_count, top_count)
    return ids * capacity + slot_rank


def per_device_slots(
    attn_heads, out_proj, residual, norm_gain, route_ids, route_weights, w_gate, w_up, w_down
):
    model_width = residual.shape[1]
    groups = lax.axis_size("expert")
    members = lax.axis_size("tensor")
    member = lax.axis_index("tensor")
    per_group = w_gate.shape[0]
    slot_count = EXPERTS * CAP
    block_cols = model_width // members
    heads_out = jnp.dot(
        attn_heads,
        lax.all_gather(out_proj, "expert", axis=1, tiled=True),
        preferred_element_type=F32,
    )
    attn_out = lax.psum(heads_out.astype(BF16), "tensor").astype(F32)
    hidden = residual.astype(F32) + attn_out
    normed = (
        hidden * lax.rsqrt(jnp.mean(hidden * hidden, axis=-1, keepdims=True) + 1e-06) * norm_gain
    ).astype(BF16)
    slot_index = slot_places(route_ids, EXPERTS, CAP)
    slot_range = jnp.arange(slot_count, dtype=jnp.int32)
    slot_hits = jnp.sum(
        (slot_index[:, :, None] == slot_range[None, None, :]).astype(BF16), axis=1
    )
    buffer = jnp.einsum("rj,rd->jd", slot_hits, normed, preferred_element_type=F32).astype(BF16)
    buffer = buffer.reshape(groups, per_group, CAP, model_width)
    arrived = lax.all_to_all(buffer, "expert", split_axis=0, concat_axis=0, tiled=True)
    gate_acc = jnp.einsum("gxcd,xdf->gxcf", arrived, w_gate, preferred_element_type=F32)
    upper = jnp.einsum("gxcd,xdf->gxcf", arrived, w_up, preferred_element_type=F32)
    activation = (jax.nn.silu(gate_acc) * upper).astype(BF16)
    product_term = jnp.einsum("gxcf,xfd->gxcd", activation, w_down, preferred_element_type=F32)
    product_term = product_term.astype(BF16).reshape(groups, per_group, CAP, members, block_cols)
    expert_out = lax.psum_scatter(
        jnp.transpose(product_term, (3, 0, 1, 2, 4)), "tensor", scatter_dimension=0, tiled=True
    )[0]
    returned = lax.all_to_all(expert_out, "expert", split_axis=0, concat_axis=0, tiled=True)
    weights = route_weights / jnp.sum(route_weights, axis=-1, keepdims=True)
    picked = returned.reshape(slot_count, block_cols)[slot_index]
    mixture = jnp.sum(weights[:, :, None] * picked.astype(F32), axis=1)
    own_hidden = lax.dynamic_slice_in_dim(hidden, member * block_cols, block_cols, 1)
    return (own_hidden + mixture).astype(BF16)


def hits_of(slot_row, rows):
    places = lax.broadcasted_iota(jnp.int32, (rows, slot_row.shape[1]), 0)
    return places == slot_row


def project_kernel(info_ref, head_refs, weight_ref, send_ref, keep_ref):
    core, x_side = info_ref[0], info_ref[1]
    pieces = [ref.at[i] for ref in head_refs for i in range(ref.shape[0])]
    here = pieces[0].shape[0]
    each = len(pieces) // 2
    for part in range(2):
        result = jnp.dot(
            jnp.concatenate([ref[...] for ref in pieces[part * each : (part + 1) * each]]),
            weight_ref[...],
            preferred_element_type=F32,
        ).astype(BF16)
        for to_x in range(2):
            x_kept = (x_side == to_x).astype(jnp.int32)
            for to_core in range(2):
                start = (to_x * 2 + to_core) * LANES
                for out_ref, wanted in ((keep_ref, core == to_core), (send_ref, core != to_core)):

                    @pl.when(wanted)
                    def _(out_ref=out_ref, x_kept=x_kept, start=start, part=part, result=result):
                        for piece in range(each):
                            out_ref[x_kept, info_ref[2 + part * each + piece]] = result[
                                piece * here : (piece + 1) * here, start : start + LANES
                            ]


def project(info, pieces, out_proj):
    here = pieces[0].shape[1]
    groups = sum(piece.shape[0] for piece in pieces)
    out = jax.ShapeDtypeStruct((2, groups, here, LANES), BF16)
    vmem = pl.BlockSpec(memory_space=pltpu.VMEM)

    def kernel(info_ref, *refs):
        project_kernel(info_ref, refs[: len(pieces)], *refs[len(pieces) :])

    return pl.pallas_call(
        kernel,
        in_specs=[pl.BlockSpec(memory_space=pltpu.SMEM)] + [vmem] * (len(pieces) + 1),
        out_specs=[vmem, vmem],
        out_shape=[out, out],
        compiler_params=pltpu.CompilerParams(vmem_limit_bytes=24 * 1024 * 1024),
        cost_estimate=pl.CostEstimate(
            flops=2 * groups * here * out_proj.size,
            bytes_accessed=2 * (out_proj.size + 2 * groups * pieces[0][0].size),
            transcendentals=0,
        ),
        name="project",
    )(info, *pieces, out_proj)


ARRAYS = 4
EARLY = (0, 2)
REST = (1, 3)


def block_at(x_refs, arrays, array, last, high, low):
    count, number = len(arrays), arrays.index(array)
    return (
        array * 8 + low * 4 + high * 2 + last,
        x_refs[low * count + number].at[high * 2 + last],
        x_refs[(2 + last) * count + number].at[low * 2 + high],
    )


def dispatch_blocks(arrays, x_refs, info_ref, invgain_ref, hits_ref, sq_ref, xs_ref, column_of):
    experts, all_rows, _ = xs_ref.shape
    parts, here, lanes = x_refs[0].shape[1:]
    rows = all_rows // parts
    blocks = info_ref.shape[0] // 2 - 1

    def pairs_of_blocks(high, carry):
        for array in arrays:
            for last in range(2):
                pair = [block_at(x_refs, arrays, array, last, high, low) for low in range(2)]
                swapped = info_ref[blocks + pair[0][0]]
                for place, own, other in pair:
                    invgain = invgain_ref[pl.ds(info_ref[place], 1), :]
                    for part in range(parts):
                        for half, block in enumerate((own, other)):
                            value = block[part].astype(F32) * invgain
                            sq_ref[swapped, part, half] += value * value
                for part in range(parts):
                    both = jnp.concatenate(
                        [
                            jnp.concatenate([own[part], other[part]], axis=0)
                            for _, own, other in pair
                        ],
                        axis=1,
                    )
                    picked = jnp.dot(
                        hits_ref[swapped, part], both, preferred_element_type=F32
                    ).astype(BF16)
                    for number, (place, _, _) in enumerate(pair):
                        column = pl.multiple_of(column_of(place) * lanes, lanes)
                        for e in range(experts):
                            xs_ref[e, part * rows : (part + 1) * rows, pl.ds(column, lanes)] = (
                                picked[
                                    e * rows : (e + 1) * rows, number * lanes : (number + 1) * lanes
                                ]
                            )
        return carry

    lax.fori_loop(0, 2, pairs_of_blocks, 0)


def early_kernel(
    rows, info_ref, slot_ref, invgain_ref, x_refs, xs_ref, sq_ref, hits_ref, spread_ref
):
    experts = xs_ref.shape[0]
    parts, here, lanes = x_refs[0].shape[1:]
    span = 2 * here
    sq_ref[...] = jnp.zeros_like(sq_ref)
    for part in range(parts):
        for e in range(experts):
            first = hits_of(slot_ref[e : e + 1, part * span : part * span + here], rows)
            second = hits_of(slot_ref[e : e + 1, part * span + here : (part + 1) * span], rows)
            first = first.astype(F32).astype(BF16)
            second = second.astype(F32).astype(BF16)
            window = slice(e * rows, (e + 1) * rows)
            hits_ref[0, part, window, :] = jnp.concatenate([first, second], axis=1)
            hits_ref[1, part, window, :] = jnp.concatenate([second, first], axis=1)
        spread_ref[part] = jnp.transpose(hits_ref[0, part].astype(F32)).astype(BF16)
    dispatch_blocks(
        EARLY, x_refs, info_ref, invgain_ref, hits_ref, sq_ref, xs_ref,
        lambda place: (place >> 4) * 8 + (place & 7),
    )


def early_dispatch(info, slots, invgain, x, experts, rows):
    parts, here, lanes = x[0].shape[1:]
    vmem = pl.BlockSpec(memory_space=pltpu.VMEM)

    def kernel(info_ref, slot_ref, invgain_ref, *rest):
        early_kernel(rows, info_ref, slot_ref, invgain_ref, rest[: len(x)], *rest[len(x) :])

    return pl.pallas_call(
        kernel,
        in_specs=[pl.BlockSpec(memory_space=pltpu.SMEM)] + [vmem] * (len(x) + 2),
        out_specs=[vmem] * 4,
        out_shape=[
            jax.ShapeDtypeStruct((experts, parts * rows, 8 * len(EARLY) * lanes), BF16),
            jax.ShapeDtypeStruct((2, parts, 2, here, lanes), F32),
            jax.ShapeDtypeStruct((2, parts, experts * rows, 2 * here), BF16),
            jax.ShapeDtypeStruct((parts, 2 * here, experts * rows), BF16),
        ],
        compiler_params=pltpu.CompilerParams(vmem_limit_bytes=24 * 1024 * 1024),
        cost_estimate=pl.CostEstimate(
            flops=4 * experts * rows * x[0].size * len(x) // 4,
            bytes_accessed=4 * x[0].size * len(x),
            transcendentals=0,
        ),
        name="early_dispatch",
    )(info, slots, invgain, *x)


def gate_up_kernel(
    rows, width, info_ref, slot_ref, weight_ref, invgain_ref, early_ref, early_sq_ref, hits_ref,
    x_refs, wg_ref, wu_ref, act_ref, hidden_ref, xs_ref, sq_ref, scale_ref
):
    expert = pl.program_id(0)
    experts = xs_ref.shape[0]
    parts, here, lanes = x_refs[0].shape[1:]
    blocks = info_ref.shape[0] // 2 - 1
    span = 2 * here
    member, z = info_ref[2 * blocks], info_ref[2 * blocks + 1]
    everything = tuple(range(ARRAYS))

    @pl.when(expert == 0)
    def _():
        sq_ref[...] = early_sq_ref[...]
        rest = [
            x_refs[part * ARRAYS + array] for part in range(len(x_refs) // ARRAYS) for array in REST
        ]
        dispatch_blocks(
            REST, rest, info_ref, invgain_ref, hits_ref, sq_ref, xs_ref,
            lambda place: info_ref[place],
        )

        def own_blocks(high, carry):
            for array in everything:
                for last in range(2):
                    for low in range(2):
                        place, own, other = block_at(x_refs, everything, array, last, high, low)
                        feature = info_ref[place]

                        @pl.when(feature >> 3 == member)
                        def _(place=place, feature=feature, own=own, other=other):
                            mine = jnp.where(
                                info_ref[blocks + place] == 0,
                                own[z].astype(F32),
                                other[z].astype(F32),
                            )
                            column = pl.multiple_of((feature & 7) * lanes, lanes)
                            hidden_ref[:, pl.ds(column, lanes)] = (
                                mine * invgain_ref[pl.ds(feature, 1), :]
                            )

            return carry

        lax.fori_loop(0, 2, own_blocks, 0)
        pieces = [
            sq_ref[0, part, half] + sq_ref[1, part, 1 - half]
            for part in range(parts)
            for half in range(2)
        ]
        total = jnp.sum(
            jnp.transpose(jnp.concatenate(pieces, axis=0)), axis=0, keepdims=True
        )
        scale_ref[...] = jnp.broadcast_to(lax.rsqrt(total / width + 1e-06), scale_ref.shape)

    def move(number, carry):
        feature = info_ref[(number >> 3) * 16 + (number & 7)]
        source = pl.multiple_of(number * lanes, lanes)
        target = pl.multiple_of(feature * lanes, lanes)
        xs_ref[expert, :, pl.ds(target, lanes)] = early_ref[0, :, pl.ds(source, lanes)]
        return carry

    lax.fori_loop(0, 8 * len(EARLY), move, 0)
    summed = jnp.dot(
        xs_ref[expert],
        jnp.concatenate([wg_ref[0], wu_ref[0]], axis=1),
        preferred_element_type=F32,
    )
    hidden_units = wg_ref.shape[2]
    for part in range(parts):
        window = slice(part * span, (part + 1) * span)
        hits = hits_of(slot_ref[pl.ds(expert, 1), window], rows)
        scale = jnp.sum(jnp.where(hits, scale_ref[0:1, window], 0.0), axis=1, keepdims=True)
        weight = jnp.sum(
            jnp.where(hits, weight_ref[pl.ds(expert, 1), window], 0.0), axis=1, keepdims=True
        )
        both_part = summed[part * rows : (part + 1) * rows, :]
        gate = both_part[:, :hidden_units] * scale
        upper = both_part[:, hidden_units:] * scale
        act = gate / (1.0 + jnp.exp(-gate)) * upper * weight
        act_ref[expert, part * rows : (part + 1) * rows, :] = act.astype(BF16)


def gate_up(info, slots, weights, invgain, early, x, w_gate, w_up, rows, members):
    experts, width, hidden_units = w_gate.shape
    parts, here, lanes = x[0].shape[1:]
    tokens = slots.shape[1]

    def kernel(*refs):
        gate_up_kernel(rows, width, *refs[:7], refs[7 : 7 + len(x)], *refs[7 + len(x) :])

    def whole(shape):
        return pl.BlockSpec(
            shape, lambda e, info: (0,) * len(shape), pipeline_mode=pl.Buffered(1)
        )

    return pl.pallas_call(
        kernel,
        grid_spec=pltpu.PrefetchScalarGridSpec(
            num_scalar_prefetch=1,
            grid=(experts,),
            in_specs=[whole(slots.shape), whole(weights.shape), whole(invgain.shape)]
            + [pl.BlockSpec((1,) + early[0].shape[1:], lambda e, info: (e, 0, 0))]
            + [pl.BlockSpec(memory_space=pltpu.VMEM)] * (len(early) - 1 + len(x))
            + [pl.BlockSpec((1, width, hidden_units), lambda e, info: (e, 0, 0))] * 2,
            out_specs=[
                pl.BlockSpec(memory_space=pltpu.VMEM),
                pl.BlockSpec(memory_space=pltpu.VMEM),
            ],
            scratch_shapes=[
                pltpu.VMEM((experts, parts * rows, width), BF16),
                pltpu.VMEM((2, parts, 2, here, lanes), F32),
                pltpu.VMEM((8, tokens), F32),
            ],
        ),
        out_shape=[
            jax.ShapeDtypeStruct((experts, parts * rows, hidden_units), BF16),
            jax.ShapeDtypeStruct((here, width // members), F32),
        ],
        compiler_params=pltpu.CompilerParams(
            vmem_limit_bytes=42 * 1024 * 1024, dimension_semantics=("arbitrary",)
        ),
        cost_estimate=pl.CostEstimate(
            flops=2 * experts * parts * rows * width * 2 * hidden_units,
            bytes_accessed=4 * experts * width * hidden_units + 2 * len(x) * x[0].size,
            transcendentals=0,
        ),
        name="gate_up",
    )(info, slots, weights, invgain, *early, *x, w_gate, w_up)


def down_kernel(rows, place_ref, spread_ref, act_ref, wd0_ref, wd1_ref, *rest):
    out_refs, ys_ref = rest[:-1], rest[-1]
    out_cols = out_refs[0].shape[2]
    step = pl.program_id(0)
    experts, all_rows, _ = act_ref.shape
    per_step = wd0_ref.shape[0]
    parts = all_rows // rows
    groups = parts * PAIR
    for number in range(per_step):
        expert = step * per_step + number
        for side, wd_ref in enumerate((wd0_ref, wd1_ref)):
            result = jnp.dot(
                act_ref[expert], wd_ref[number], preferred_element_type=F32
            ).astype(BF16)
            for part in range(parts):
                ys_ref[side, part, expert] = result[part * rows : (part + 1) * rows, :]

    @pl.when(step == pl.num_programs(0) - 1)
    def _():
        for part in range(parts):
            for side in range(2):
                picked = ys_ref[side, part].reshape(experts * rows, ys_ref.shape[4])
                mixed = jnp.dot(
                    spread_ref[part], picked, preferred_element_type=F32
                ).astype(BF16)
                for i in range(PAIR):
                    for number, out_ref in enumerate(out_refs):
                        block = (number * 2 + side) * groups + part * PAIR + i
                        target = place_ref[2 + block]
                        out_ref[target] = mixed[
                            i * 128 : (i + 1) * 128, number * out_cols : (number + 1) * out_cols
                        ]


def down(place, spread, act, w_down, rows, groups, cols, chunks, per_step=2):
    experts, hidden_units, width = w_down.shape
    parts, span, _ = spread.shape
    here = parts * span // groups
    out = jax.ShapeDtypeStruct((2 * groups, here, cols // chunks), BF16)
    return pl.pallas_call(
        functools.partial(down_kernel, rows),
        grid_spec=pltpu.PrefetchScalarGridSpec(
            num_scalar_prefetch=1,
            grid=(experts // per_step,),
            in_specs=[
                pl.BlockSpec(memory_space=pltpu.VMEM),
                pl.BlockSpec(memory_space=pltpu.VMEM),
                pl.BlockSpec((per_step, hidden_units, cols), lambda e, p: (e, 0, p[0])),
                pl.BlockSpec((per_step, hidden_units, cols), lambda e, p: (e, 0, p[1])),
            ],
            out_specs=[pl.BlockSpec(out.shape, lambda e, p: (0, 0, 0))] * chunks,
            scratch_shapes=[pltpu.VMEM((2, parts, experts, rows, cols), BF16)],
        ),
        out_shape=[out] * chunks,
        compiler_params=pltpu.CompilerParams(
            vmem_limit_bytes=36 * 1024 * 1024, dimension_semantics=("arbitrary",)
        ),
        cost_estimate=pl.CostEstimate(
            flops=8 * experts * parts * rows * cols * hidden_units,
            bytes_accessed=4 * experts * cols * hidden_units + 4 * parts * span * cols,
            transcendentals=0,
        ),
        name="down_mix",
    )(place, spread, act, w_down, w_down)


def flip(array, bits_of):
    pairs = []
    for index in range(32):
        pairs.append((index, index ^ bits_of(index & 1)))
    return lax.ppermute(array, ("expert", "tensor"), pairs)


CORE, X, Y, ZLOW, ZHIGH = 1, 2, 4, 8, 16


def first_axis(core):
    return Y if core else X


def last_axis(core):
    return X if core else Y


def own_order(groups, group):
    order = jnp.arange(groups, dtype=jnp.int32)
    return order ^ (group & 1)


HALVING = {
    "first": first_axis,
    "last": last_axis,
    "low": lambda core: ZLOW,
    "high": lambda core: ZHIGH,
}
ORDERS = (("first", "low", "high", "last"), ("first", "last", "low", "high"))


def halving_places(to_core, group, groups, order):
    g = own_order(groups, group)[None, :]
    y_kept = ((g & 1) == (group & 1)).astype(jnp.int32)
    x_kept = jnp.arange(2, dtype=jnp.int32)[:, None]
    kept = {
        "first": jnp.where(to_core == 0, x_kept, y_kept),
        "last": jnp.where(to_core == 0, y_kept, x_kept),
        "low": (((g >> 1) & 1) == ((group >> 1) & 1)).astype(jnp.int32),
        "high": ((g >> 2) == (group >> 2)).astype(jnp.int32),
    }
    place = 0
    for axis in order:
        place = place * 2 + kept[axis]
    return place.reshape(-1)


def total_of(terms):
    total = terms[0].astype(F32)
    for term in terms[1:]:
        total = total + term.astype(F32)
    return total


def after(value, earlier):
    return lax.optimization_barrier((value, earlier))


def reduce_chunks(makers):
    terms, sends, came = [None, None], [None, None], {}

    def split_exchange(chunk):
        whole = terms[chunk]
        quarter = whole[0].shape[0] // 4
        rows = [slice(i * quarter, (i + 1) * quarter) for i in range(4)]
        bits_of = HALVING[ORDERS[chunk][0]]
        early = total_of([term[rows[0]] for term in whole]).astype(BF16)
        late = total_of([term[rows[1]] for term in whole]).astype(BF16)
        early, late = after(early, late)
        early_came, _ = after(flip(early, bits_of), exchange(0, 1))
        late, early_came = after(late, early_came)
        sends[chunk] = [term[rows[2]] for term in whole] + [early_came]
        terms[chunk] = [term[rows[3]] for term in whole] + [flip(late, bits_of)]

    def exchange(chunk, stage, earlier=None):
        if sends[chunk] is None:
            half = terms[chunk][0].shape[0] // 2
            sends[chunk] = [term[:half] for term in terms[chunk]]
            terms[chunk] = [term[half:] for term in terms[chunk]]
        sent = total_of(sends[chunk]).astype(BF16)
        sends[chunk] = None
        if earlier is not None:
            sent, _ = after(sent, earlier)
        came[chunk, stage] = flip(sent, HALVING[ORDERS[chunk][stage]])
        terms[chunk] = terms[chunk] + [came[chunk, stage]]
        return sent

    terms[0] = makers[0](None)
    terms[1] = makers[1](exchange(0, 0))
    split_exchange(1)
    exchange(1, 1)
    exchange(0, 2)
    exchange(1, 2)
    exchange(1, 3, came[0, 2])
    exchange(0, 3)
    return [total_of([term[0] for term in chunk]) for chunk in terms]


HEAD_STAGES = (
    lambda core: ZHIGH,
    lambda core: ZLOW if core else Y,
    lambda core: Y if core else ZLOW,
)


def head_bits(place, core):
    bits = [(place >> stage) & 1 for stage in range(3)]
    return jnp.where(
        core == 0,
        (bits[0] << 2) | bits[1] | (bits[2] << 1),
        (bits[0] << 2) | (bits[1] << 1) | bits[2],
    )


def gather_heads(heads, beside):
    first, second, third = HEAD_STAGES
    heads = heads[None]
    heads = jnp.concatenate([heads, flip(heads, first)], axis=0)
    came = flip(heads, second)
    early = flip(heads, third)
    late, (early, beside) = after(came, (early, beside))
    return [heads, came, early, flip(late, third)], beside


def pack_kernel(member_ref, residual_ref, ids_ref, weights_ref, out_ref):
    groups, rows, lanes = out_ref.shape
    here, width = residual_ref.shape
    each = width // groups
    rest = weights_ref[...] / jnp.sum(weights_ref[...], axis=0, keepdims=True)
    parts = [ids_ref[...].astype(F32)]
    for _ in range(3):
        part = rest.astype(BF16).astype(F32)
        parts.append(part)
        rest = rest - part
    table = jnp.concatenate(parts, axis=0).astype(BF16)
    for group in range(groups):
        column = pl.multiple_of(group * each + member_ref[0] * lanes, lanes)
        out_ref[group, :here, :] = residual_ref[:, pl.ds(column, lanes)]
        out_ref[group, here:, :] = table


def pack(member, residual, route_ids, route_weights, groups):
    here, top = route_ids.shape
    vmem = pl.BlockSpec(memory_space=pltpu.VMEM)
    return pl.pallas_call(
        pack_kernel,
        in_specs=[pl.BlockSpec(memory_space=pltpu.SMEM), vmem, vmem, vmem],
        out_specs=vmem,
        out_shape=jax.ShapeDtypeStruct((groups, here + 4 * top, LANES), BF16),
        compiler_params=pltpu.CompilerParams(vmem_limit_bytes=16 * 1024 * 1024),
        cost_estimate=pl.CostEstimate(
            flops=0, bytes_accessed=3 * residual.size, transcendentals=0
        ),
        name="pack",
    )(member.reshape(1), residual, route_ids.T, route_weights.T)


def own_routes(table, group, experts):
    groups, rows, here = table.shape
    top = rows // 4
    own = group * experts + jnp.arange(experts, dtype=jnp.int32)
    table = table.astype(F32).reshape(groups, 4, top, here)
    ids = table[:, 0].astype(jnp.int32)
    match = ids[None] == own[:, None, None, None]
    named = jnp.any(match, axis=2)
    shares = table[:, 1] + table[:, 2] + table[:, 3]
    weights = jnp.sum(jnp.where(match, shares[None], 0.0), axis=2)
    span = PAIR * here
    order = jnp.arange(span)
    earlier = (order[:, None] < order[None, :]).astype(BF16)
    rank = jnp.dot(
        named.astype(BF16).reshape(experts * groups // PAIR, span),
        earlier,
        preferred_element_type=F32,
    )
    slots = jnp.where(named, rank.reshape(named.shape).astype(jnp.int32), -1)
    return slots.reshape(experts, groups * here), weights.reshape(experts, groups * here)


def block_table(device, groups, member):
    number = jnp.arange(32, dtype=jnp.int32)
    array, place = number >> 3, number & 7
    source_core = (device & 1) ^ (array >> 1)
    first = jnp.where(source_core == 0, X, Y)
    last = jnp.where(source_core == 0, Y, X)
    feature = (
        device
        ^ (array >> 1)
        ^ jnp.where(array & 1 == 1, first, 0)
        ^ jnp.where(place & 1 == 1, last, 0)
        ^ jnp.where(place & 2 == 2, ZHIGH, 0)
        ^ jnp.where(place & 4 == 4, ZLOW, 0)
    )
    swapped = ((feature ^ device) >> 2) & 1
    return jnp.concatenate([feature, swapped, jnp.stack([member, device >> 3])])


def gather_blocks(first, second, make_early):
    def along(bits, block):
        return flip(block, lambda core: bits)

    def joined(held, came):
        return jnp.concatenate([held, came], axis=0)

    first_last = flip(first, last_axis)
    second_high = along(ZHIGH, second)
    second, _ = after(joined(second, second_high), first_last)
    second_low = along(ZLOW, second)
    first, _ = after(joined(first, first_last), second_high)
    first_high = along(ZHIGH, first)
    second, first_high = after(joined(second, second_low), first_high)
    second_last = flip(second, last_axis)
    first = joined(first, first_high)
    first_low = along(ZLOW, first)
    halves = []
    for early, late in ((first, first_low), (second, second_last)):
        early_first = flip(early, first_axis)
        if halves:
            early_first, _ = after(early_first, halves[0][1][0])
        late, early_first = after(late, early_first)
        late_first = flip(late, first_axis)
        halves.append(
            (
                [early, early_first, along(CORE, early), along(CORE, early_first)],
                [late, late_first, along(CORE, late)],
            )
        )
    made = make_early([part[array] for half in halves for part in half for array in EARLY])
    x = []
    for early, late in halves:
        late_first, made = after(late[1], made)
        x += early + [late[0], late_first, late[2], along(CORE, late_first)]
    return x, made


def per_device_tokens(
    attn_heads, out_proj, residual, norm_gain, route_ids, route_weights, w_gate, w_up, w_down
):
    groups, members = lax.axis_size("expert"), lax.axis_size("tensor")
    group, member = lax.axis_index("expert"), lax.axis_index("tensor")
    device = group * members + member
    here, width = residual.shape
    experts = w_gate.shape[0]
    rows = -(-PAIR * CAP // 16) * 16
    x_side, core, y_side = member >> 1, member & 1, group & 1

    moved = lax.all_to_all(
        pack(member, residual, route_ids, route_weights, groups),
        "expert",
        split_axis=0,
        concat_axis=0,
        tiled=True,
    )
    gain = lax.dynamic_index_in_dim(
        norm_gain.reshape(groups * members, LANES), device, 0, keepdims=False
    )

    pieces, moved = gather_heads(attn_heads, moved)
    numbers = jnp.arange(groups, dtype=jnp.int32)
    arrival = (head_bits(numbers, core) ^ group) ^ y_side
    info = jnp.concatenate(
        [jnp.stack([core, x_side]), ((arrival & 1) << 2) | (arrival >> 1)]
    )
    table = jnp.take(moved[:, here:], own_order(groups, group), axis=0, mode="clip")
    moved = moved[:, :here].reshape(groups // 2, 2, here, LANES)
    slots, weights = own_routes(table, group, experts)
    info, (slots, weights) = after(info, (slots, weights))
    send, keep = project(info, pieces, out_proj)
    came = flip(send, lambda c: CORE)
    from_x = flip(total_of([keep[0], came[0]]).astype(BF16), lambda c: X)
    starts = []
    each = groups // 2
    for half in range(2):
        window = slice(half * each, (half + 1) * each)
        hidden = lax.dynamic_index_in_dim(moved, y_side ^ half, 1, keepdims=False).astype(F32)
        hidden = hidden + total_of([keep[1, window], came[1, window], from_x[window]])
        starts.append((hidden * gain).astype(BF16)[None])

    invgain = (1.0 / norm_gain).reshape(groups * members, LANES)
    table = block_table(device, groups, member)
    x, (*early, spread) = gather_blocks(
        *starts, lambda blocks: early_dispatch(table, slots, invgain, blocks, experts, rows)
    )
    act, own_hidden = gate_up(
        table, slots, weights, invgain, early, x, w_gate, w_up, rows, members
    )

    cols = width // members

    def columns_of(to_core, chunk, chunks, orders):
        sides = jnp.stack([1 - x_side, x_side])
        blocks = (sides * 2 + to_core) * chunks + chunk
        places = [halving_places(to_core, group, groups, order) for order in orders]
        return jnp.concatenate([blocks] + places)

    chunks = len(ORDERS)
    chunk_cols = cols // chunks
    other = down(
        columns_of(1 - core, 0, 1, ORDERS), spread, act, w_down, rows, groups, cols, chunks
    )
    came = [flip(piece, lambda c: CORE) for piece in other]

    def terms_of(chunk, earlier):
        place = columns_of(core, chunk, chunks, ORDERS[chunk : chunk + 1])
        if earlier is not None:
            place, _ = after(place, earlier)
        (kept,) = down(place, spread, act, w_down, rows, groups, chunk_cols, 1)
        return [kept, came[chunk]]

    sums = reduce_chunks([functools.partial(terms_of, chunk) for chunk in range(chunks)])
    mixture = jnp.concatenate(sums, axis=1)
    return (own_hidden + mixture).astype(BF16)


def solution(mesh):
    groups, members = mesh.shape["expert"], mesh.shape["tensor"]
    placed = (
        P("expert", "tensor"),
        P("tensor", "expert"),
        P("expert", None),
        P(),
        P("expert", None),
        P("expert", None),
        P("expert", None, "tensor"),
        P("expert", None, "tensor"),
        P("expert", "tensor", None),
    )

    def run(*arrays):
        tokens, width = arrays[2].shape
        whole_tokens = (groups, members) == (8, 4) and width == groups * members * LANES
        body = per_device_tokens if whole_tokens else per_device_slots
        return jax.shard_map(
            body, mesh=mesh, in_specs=placed, out_specs=P("expert", "tensor"), check_vma=False
        )(*arrays)

    return run
```

```python
import functools

import jax
import jax.numpy as jnp
from jax import lax
from jax.experimental import pallas as pl
from jax.experimental.pallas import tpu as pltpu
from jax.sharding import PartitionSpec as P

EXPERTS = 64
CAP = 18
BF16 = jnp.bfloat16
F32 = jnp.float32
PAIR = 2
LANES = 128
STREAMS = 4


def slot_places(ids, experts, capacity):
    row_count, top_count = ids.shape
    onehot = (ids[:, :, None] == jnp.arange(experts, dtype=jnp.int32)[None, None, :]).astype(
        jnp.int32
    )
    flattened = onehot.reshape(row_count * top_count, experts)
    before = jnp.cumsum(flattened, axis=0) - flattened
    slot_rank = jnp.sum(before * flattened, axis=1).reshape(row_count, top_count)
    return ids * capacity + slot_rank


def per_device_slots(
    attn_heads, out_proj, residual, norm_gain, route_ids, route_weights, w_gate, w_up, w_down
):
    model_width = residual.shape[1]
    groups = lax.axis_size("expert")
    members = lax.axis_size("tensor")
    member = lax.axis_index("tensor")
    per_group = w_gate.shape[0]
    slot_count = EXPERTS * CAP
    block_cols = model_width // members
    heads_out = jnp.dot(
        attn_heads,
        lax.all_gather(out_proj, "expert", axis=1, tiled=True),
        preferred_element_type=F32,
    )
    attn_out = lax.psum(heads_out.astype(BF16), "tensor").astype(F32)
    hidden = residual.astype(F32) + attn_out
    normed = (
        hidden * lax.rsqrt(jnp.mean(hidden * hidden, axis=-1, keepdims=True) + 1e-06) * norm_gain
    ).astype(BF16)
    slot_index = slot_places(route_ids, EXPERTS, CAP)
    slot_range = jnp.arange(slot_count, dtype=jnp.int32)
    slot_hits = jnp.sum(
        (slot_index[:, :, None] == slot_range[None, None, :]).astype(BF16), axis=1
    )
    buffer = jnp.einsum("rj,rd->jd", slot_hits, normed, preferred_element_type=F32).astype(BF16)
    buffer = buffer.reshape(groups, per_group, CAP, model_width)
    arrived = lax.all_to_all(buffer, "expert", split_axis=0, concat_axis=0, tiled=True)
    gate_acc = jnp.einsum("gxcd,xdf->gxcf", arrived, w_gate, preferred_element_type=F32)
    upper = jnp.einsum("gxcd,xdf->gxcf", arrived, w_up, preferred_element_type=F32)
    activation = (jax.nn.silu(gate_acc) * upper).astype(BF16)
    product_term = jnp.einsum("gxcf,xfd->gxcd", activation, w_down, preferred_element_type=F32)
    product_term = product_term.astype(BF16).reshape(groups, per_group, CAP, members, block_cols)
    expert_out = lax.psum_scatter(
        jnp.transpose(product_term, (3, 0, 1, 2, 4)), "tensor", scatter_dimension=0, tiled=True
    )[0]
    returned = lax.all_to_all(expert_out, "expert", split_axis=0, concat_axis=0, tiled=True)
    weights = route_weights / jnp.sum(route_weights, axis=-1, keepdims=True)
    picked = returned.reshape(slot_count, block_cols)[slot_index]
    mixture = jnp.sum(weights[:, :, None] * picked.astype(F32), axis=1)
    own_hidden = lax.dynamic_slice_in_dim(hidden, member * block_cols, block_cols, 1)
    return (own_hidden + mixture).astype(BF16)


def hits_of(slot_row, rows):
    places = lax.broadcasted_iota(jnp.int32, (rows, slot_row.shape[1]), 0)
    return places == slot_row


def project_kernel(info_ref, head_refs, weight_ref, send_ref, keep_ref):
    core, x_side = info_ref[0], info_ref[1]
    pieces = [ref.at[i] for ref in head_refs for i in range(ref.shape[0])]
    here = pieces[0].shape[0]
    each = len(pieces) // 2
    for part in range(2):
        result = jnp.dot(
            jnp.concatenate([ref[...] for ref in pieces[part * each : (part + 1) * each]]),
            weight_ref[...],
            preferred_element_type=F32,
        ).astype(BF16)
        for to_x in range(2):
            x_kept = (x_side == to_x).astype(jnp.int32)
            for to_core in range(2):
                start = (to_x * 2 + to_core) * LANES
                for out_ref, wanted in ((keep_ref, core == to_core), (send_ref, core != to_core)):

                    @pl.when(wanted)
                    def _(out_ref=out_ref, x_kept=x_kept, start=start, part=part, result=result):
                        for piece in range(each):
                            out_ref[x_kept, info_ref[2 + part * each + piece]] = result[
                                piece * here : (piece + 1) * here, start : start + LANES
                            ]


def project(info, pieces, out_proj):
    here = pieces[0].shape[1]
    groups = sum(piece.shape[0] for piece in pieces)
    out = jax.ShapeDtypeStruct((2, groups, here, LANES), BF16)
    vmem = pl.BlockSpec(memory_space=pltpu.VMEM)

    def kernel(info_ref, *refs):
        project_kernel(info_ref, refs[: len(pieces)], *refs[len(pieces) :])

    return pl.pallas_call(
        kernel,
        in_specs=[pl.BlockSpec(memory_space=pltpu.SMEM)] + [vmem] * (len(pieces) + 1),
        out_specs=[vmem, vmem],
        out_shape=[out, out],
        compiler_params=pltpu.CompilerParams(vmem_limit_bytes=24 * 1024 * 1024),
        cost_estimate=pl.CostEstimate(
            flops=2 * groups * here * out_proj.size,
            bytes_accessed=2 * (out_proj.size + 2 * groups * pieces[0][0].size),
            transcendentals=0,
        ),
        name="project",
    )(info, *pieces, out_proj)


def gate_up_kernel(
    experts, rows, width, info_ref, slot_ref, weight_ref, invgain_ref, x_refs, wg_refs, wu_refs,
    act_ref, hidden_ref, spread_ref, xs_ref, sq_ref, scale_ref, hits_ref
):
    expert = pl.program_id(0)
    arrays = 4
    own_refs = (x_refs[:arrays], x_refs[arrays : 2 * arrays])
    other_refs = (x_refs[2 * arrays : 3 * arrays], x_refs[3 * arrays :])
    parts, here, lanes = x_refs[0].shape[1:]
    blocks = info_ref.shape[0] // 2 - 1
    each = blocks // arrays
    span = 2 * here
    member, z = info_ref[2 * blocks], info_ref[2 * blocks + 1]

    def block_at(array, last, high, low):
        return (
            array * each + low * 4 + high * 2 + last,
            own_refs[low][array].at[high * 2 + last],
            other_refs[last][array].at[low * 2 + high],
        )

    @pl.when(expert == 0)
    def _():
        sq_ref[...] = jnp.zeros_like(sq_ref)
        for part in range(parts):
            for e in range(experts):
                first = hits_of(slot_ref[e : e + 1, part * span : part * span + here], rows)
                second = hits_of(
                    slot_ref[e : e + 1, part * span + here : (part + 1) * span], rows
                )
                first = first.astype(F32).astype(BF16)
                second = second.astype(F32).astype(BF16)
                window = slice(e * rows, (e + 1) * rows)
                hits_ref[0, part, window, :] = jnp.concatenate([first, second], axis=1)
                hits_ref[1, part, window, :] = jnp.concatenate([second, first], axis=1)
            spread_ref[part] = jnp.transpose(hits_ref[0, part].astype(F32)).astype(BF16)

        def pairs_of_blocks(high, carry):
            for array in range(arrays):
                for last in range(2):
                    pair = [block_at(array, last, high, low) for low in range(2)]
                    swapped = info_ref[blocks + pair[0][0]]
                    features = [info_ref[place] for place, _, _ in pair]
                    for feature, (_, own, other) in zip(features, pair):
                        invgain = invgain_ref[pl.ds(feature, 1), :]
                        for part in range(parts):
                            for half, block in enumerate((own, other)):
                                value = block[part].astype(F32) * invgain
                                sq_ref[swapped, part, half] += value * value
                    for part in range(parts):
                        both = jnp.concatenate(
                            [
                                jnp.concatenate([own[part], other[part]], axis=0)
                                for _, own, other in pair
                            ],
                            axis=1,
                        )
                        picked = jnp.dot(
                            hits_ref[swapped, part], both, preferred_element_type=F32
                        ).astype(BF16)
                        for number, feature in enumerate(features):
                            column = pl.multiple_of(feature * lanes, lanes)
                            for e in range(experts):
                                xs_ref[
                                    e, part * rows : (part + 1) * rows, pl.ds(column, lanes)
                                ] = picked[
                                    e * rows : (e + 1) * rows, number * lanes : (number + 1) * lanes
                                ]
            return carry

        lax.fori_loop(0, 2, pairs_of_blocks, 0)

        def own_blocks(high, carry):
            for array in range(arrays):
                for last in range(2):
                    for low in range(2):
                        place, own, other = block_at(array, last, high, low)
                        feature = info_ref[place]

                        @pl.when(feature >> 3 == member)
                        def _(place=place, feature=feature, own=own, other=other):
                            mine = jnp.where(
                                info_ref[blocks + place] == 0,
                                own[z].astype(F32),
                                other[z].astype(F32),
                            )
                            column = pl.multiple_of((feature & 7) * lanes, lanes)
                            hidden_ref[:, pl.ds(column, lanes)] = (
                                mine * invgain_ref[pl.ds(feature, 1), :]
                            )

            return carry

        lax.fori_loop(0, 2, own_blocks, 0)
        pieces = [
            sq_ref[0, part, half] + sq_ref[1, part, 1 - half]
            for part in range(parts)
            for half in range(2)
        ]
        total = jnp.sum(
            jnp.transpose(jnp.concatenate(pieces, axis=0)), axis=0, keepdims=True
        )
        scale_ref[...] = jnp.broadcast_to(lax.rsqrt(total / width + 1e-06), scale_ref.shape)

    both = [
        jnp.concatenate([wg_ref[0], wu_ref[0]], axis=1) for wg_ref, wu_ref in zip(wg_refs, wu_refs)
    ]
    summed = jnp.dot(
        xs_ref[expert], jnp.concatenate(both, axis=0), preferred_element_type=F32
    )
    hidden_units = wg_refs[0].shape[2]
    for part in range(parts):
        window = slice(part * span, (part + 1) * span)
        hits = hits_of(slot_ref[pl.ds(expert, 1), window], rows)
        scale = jnp.sum(jnp.where(hits, scale_ref[0:1, window], 0.0), axis=1, keepdims=True)
        weight = jnp.sum(
            jnp.where(hits, weight_ref[pl.ds(expert, 1), window], 0.0), axis=1, keepdims=True
        )
        both_part = summed[part * rows : (part + 1) * rows, :]
        gate = both_part[:, :hidden_units] * scale
        upper = both_part[:, hidden_units:] * scale
        act = gate / (1.0 + jnp.exp(-gate)) * upper * weight
        act_ref[expert, part * rows : (part + 1) * rows, :] = act.astype(BF16)


def gate_up(info, slots, weights, invgain, x, w_gate, w_up, rows, members):
    experts, width, hidden_units = w_gate.shape
    parts, here, lanes = x[0].shape[1:]
    tokens = slots.shape[1]

    def kernel(info_ref, slot_ref, weight_ref, invgain_ref, *rest):
        gate_up_kernel(
            experts, rows, width, info_ref, slot_ref, weight_ref, invgain_ref,
            rest[: len(x)], rest[len(x) : len(x) + STREAMS],
            rest[len(x) + STREAMS : len(x) + 2 * STREAMS], *rest[len(x) + 2 * STREAMS :]
        )

    def stream(number):
        return pl.BlockSpec(
            (1, width // STREAMS, hidden_units), lambda e, info: (e, number, 0)
        )

    def whole(shape):
        return pl.BlockSpec(
            shape, lambda e, info: (0,) * len(shape), pipeline_mode=pl.Buffered(1)
        )

    return pl.pallas_call(
        kernel,
        grid_spec=pltpu.PrefetchScalarGridSpec(
            num_scalar_prefetch=1,
            grid=(experts,),
            in_specs=[whole(slots.shape), whole(weights.shape), whole(invgain.shape)]
            + [pl.BlockSpec(memory_space=pltpu.VMEM)] * len(x)
            + [stream(number) for number in range(STREAMS)] * 2,
            out_specs=[
                pl.BlockSpec(memory_space=pltpu.VMEM),
                pl.BlockSpec(memory_space=pltpu.VMEM),
                pl.BlockSpec(memory_space=pltpu.VMEM),
            ],
            scratch_shapes=[
                pltpu.VMEM((experts, parts * rows, width), BF16),
                pltpu.VMEM((2, parts, 2, here, lanes), F32),
                pltpu.VMEM((8, tokens), F32),
                pltpu.VMEM((2, parts, experts * rows, 2 * here), BF16),
            ],
        ),
        out_shape=[
            jax.ShapeDtypeStruct((experts, parts * rows, hidden_units), BF16),
            jax.ShapeDtypeStruct((here, width // members), F32),
            jax.ShapeDtypeStruct((parts, 2 * here, experts * rows), BF16),
        ],
        compiler_params=pltpu.CompilerParams(
            vmem_limit_bytes=36 * 1024 * 1024, dimension_semantics=("arbitrary",)
        ),
        cost_estimate=pl.CostEstimate(
            flops=2 * experts * parts * rows * width * 2 * hidden_units,
            bytes_accessed=4 * experts * width * hidden_units + 2 * len(x) * x[0].size,
            transcendentals=0,
        ),
        name="gate_up",
    )(info, slots, weights, invgain, *x, *[w_gate] * STREAMS, *[w_up] * STREAMS)


def down_kernel(rows, place_ref, spread_ref, act_ref, wd_refs, *rest):
    out_refs, ys_ref = rest[:-1], rest[-1]
    out_cols = out_refs[0].shape[2]
    step = pl.program_id(0)
    experts, all_rows, _ = act_ref.shape
    per_step = len(wd_refs) // 2
    parts = all_rows // rows
    groups = parts * PAIR
    for number in range(per_step):
        expert = step * per_step + number
        for side in range(2):
            result = jnp.dot(
                act_ref[expert], wd_refs[2 * number + side][0], preferred_element_type=F32
            ).astype(BF16)
            for part in range(parts):
                ys_ref[side, part, expert] = result[part * rows : (part + 1) * rows, :]

    @pl.when(step == pl.num_programs(0) - 1)
    def _():
        for part in range(parts):
            for side in range(2):
                picked = ys_ref[side, part].reshape(experts * rows, ys_ref.shape[4])
                mixed = jnp.dot(
                    spread_ref[part], picked, preferred_element_type=F32
                ).astype(BF16)
                for i in range(PAIR):
                    for number, out_ref in enumerate(out_refs):
                        block = (number * 2 + side) * groups + part * PAIR + i
                        target = place_ref[2 + block]
                        out_ref[target] = mixed[
                            i * 128 : (i + 1) * 128, number * out_cols : (number + 1) * out_cols
                        ]


def down(place, spread, act, w_down, rows, groups, cols, chunks, per_step=2):
    experts, hidden_units, width = w_down.shape
    parts, span, _ = spread.shape
    here = parts * span // groups
    out = jax.ShapeDtypeStruct((2 * groups, here, cols // chunks), BF16)

    def kernel(place_ref, spread_ref, act_ref, *rest):
        down_kernel(
            rows, place_ref, spread_ref, act_ref, rest[: 2 * per_step], *rest[2 * per_step :]
        )

    def stream(number, side):
        return pl.BlockSpec(
            (1, hidden_units, cols), lambda e, p: (e * per_step + number, 0, p[side])
        )

    return pl.pallas_call(
        kernel,
        grid_spec=pltpu.PrefetchScalarGridSpec(
            num_scalar_prefetch=1,
            grid=(experts // per_step,),
            in_specs=[
                pl.BlockSpec(memory_space=pltpu.VMEM),
                pl.BlockSpec(memory_space=pltpu.VMEM),
            ]
            + [stream(number, side) for number in range(per_step) for side in range(2)],
            out_specs=[pl.BlockSpec(out.shape, lambda e, p: (0, 0, 0))] * chunks,
            scratch_shapes=[pltpu.VMEM((2, parts, experts, rows, cols), BF16)],
        ),
        out_shape=[out] * chunks,
        compiler_params=pltpu.CompilerParams(
            vmem_limit_bytes=36 * 1024 * 1024, dimension_semantics=("arbitrary",)
        ),
        cost_estimate=pl.CostEstimate(
            flops=8 * experts * parts * rows * cols * hidden_units,
            bytes_accessed=4 * experts * cols * hidden_units + 4 * parts * span * cols,
            transcendentals=0,
        ),
        name="down_mix",
    )(place, spread, act, *[w_down] * (2 * per_step))


def flip(array, bits_of):
    pairs = []
    for index in range(32):
        pairs.append((index, index ^ bits_of(index & 1)))
    return lax.ppermute(array, ("expert", "tensor"), pairs)


CORE, X, Y, ZLOW, ZHIGH = 1, 2, 4, 8, 16


def first_axis(core):
    return Y if core else X


def last_axis(core):
    return X if core else Y


def own_order(groups, group):
    order = jnp.arange(groups, dtype=jnp.int32)
    return order ^ (group & 1)


HALVING = {
    "first": first_axis,
    "last": last_axis,
    "low": lambda core: ZLOW,
    "high": lambda core: ZHIGH,
}
ORDERS = (("first", "low", "high", "last"), ("first", "last", "low", "high"))


def halving_places(to_core, group, groups, order):
    g = own_order(groups, group)[None, :]
    y_kept = ((g & 1) == (group & 1)).astype(jnp.int32)
    x_kept = jnp.arange(2, dtype=jnp.int32)[:, None]
    kept = {
        "first": jnp.where(to_core == 0, x_kept, y_kept),
        "last": jnp.where(to_core == 0, y_kept, x_kept),
        "low": (((g >> 1) & 1) == ((group >> 1) & 1)).astype(jnp.int32),
        "high": ((g >> 2) == (group >> 2)).astype(jnp.int32),
    }
    place = 0
    for axis in order:
        place = place * 2 + kept[axis]
    return place.reshape(-1)


def total_of(terms):
    total = terms[0].astype(F32)
    for term in terms[1:]:
        total = total + term.astype(F32)
    return total


def after(value, earlier):
    return lax.optimization_barrier((value, earlier))


def reduce_chunks(makers):
    terms, sends, came = [None, None], [None, None], {}

    def split_exchange(chunk):
        whole = terms[chunk]
        quarter = whole[0].shape[0] // 4
        rows = [slice(i * quarter, (i + 1) * quarter) for i in range(4)]
        bits_of = HALVING[ORDERS[chunk][0]]
        early = total_of([term[rows[0]] for term in whole]).astype(BF16)
        late = total_of([term[rows[1]] for term in whole]).astype(BF16)
        early, late = after(early, late)
        early_came, _ = after(flip(early, bits_of), exchange(0, 1))
        late, early_came = after(late, early_came)
        sends[chunk] = [term[rows[2]] for term in whole] + [early_came]
        terms[chunk] = [term[rows[3]] for term in whole] + [flip(late, bits_of)]

    def exchange(chunk, stage, earlier=None):
        if sends[chunk] is None:
            half = terms[chunk][0].shape[0] // 2
            sends[chunk] = [term[:half] for term in terms[chunk]]
            terms[chunk] = [term[half:] for term in terms[chunk]]
        sent = total_of(sends[chunk]).astype(BF16)
        sends[chunk] = None
        if earlier is not None:
            sent, _ = after(sent, earlier)
        came[chunk, stage] = flip(sent, HALVING[ORDERS[chunk][stage]])
        terms[chunk] = terms[chunk] + [came[chunk, stage]]
        return sent

    terms[0] = makers[0](None)
    terms[1] = makers[1](exchange(0, 0))
    split_exchange(1)
    exchange(1, 1)
    exchange(0, 2)
    exchange(1, 2)
    exchange(1, 3, came[0, 2])
    exchange(0, 3)
    return [total_of([term[0] for term in chunk]) for chunk in terms]


HEAD_STAGES = (
    lambda core: ZHIGH,
    lambda core: ZLOW if core else Y,
    lambda core: Y if core else ZLOW,
)


def head_bits(place, core):
    bits = [(place >> stage) & 1 for stage in range(3)]
    return jnp.where(
        core == 0,
        (bits[0] << 2) | bits[1] | (bits[2] << 1),
        (bits[0] << 2) | (bits[1] << 1) | bits[2],
    )


def gather_heads(heads, beside):
    first, second, third = HEAD_STAGES
    heads = heads[None]
    heads = jnp.concatenate([heads, flip(heads, first)], axis=0)
    came = flip(heads, second)
    early = flip(heads, third)
    late, (early, beside) = after(came, (early, beside))
    return [heads, came, early, flip(late, third)], beside


def pack_kernel(member_ref, residual_ref, ids_ref, weights_ref, out_ref):
    groups, rows, lanes = out_ref.shape
    here, width = residual_ref.shape
    each = width // groups
    rest = weights_ref[...] / jnp.sum(weights_ref[...], axis=0, keepdims=True)
    parts = [ids_ref[...].astype(F32)]
    for _ in range(3):
        part = rest.astype(BF16).astype(F32)
        parts.append(part)
        rest = rest - part
    table = jnp.concatenate(parts, axis=0).astype(BF16)
    for group in range(groups):
        column = pl.multiple_of(group * each + member_ref[0] * lanes, lanes)
        out_ref[group, :here, :] = residual_ref[:, pl.ds(column, lanes)]
        out_ref[group, here:, :] = table


def pack(member, residual, route_ids, route_weights, groups):
    here, top = route_ids.shape
    vmem = pl.BlockSpec(memory_space=pltpu.VMEM)
    return pl.pallas_call(
        pack_kernel,
        in_specs=[pl.BlockSpec(memory_space=pltpu.SMEM), vmem, vmem, vmem],
        out_specs=vmem,
        out_shape=jax.ShapeDtypeStruct((groups, here + 4 * top, LANES), BF16),
        compiler_params=pltpu.CompilerParams(vmem_limit_bytes=16 * 1024 * 1024),
        cost_estimate=pl.CostEstimate(
            flops=0, bytes_accessed=3 * residual.size, transcendentals=0
        ),
        name="pack",
    )(member.reshape(1), residual, route_ids.T, route_weights.T)


def own_routes(table, group, experts):
    groups, rows, here = table.shape
    top = rows // 4
    own = group * experts + jnp.arange(experts, dtype=jnp.int32)
    table = table.astype(F32).reshape(groups, 4, top, here)
    ids = table[:, 0].astype(jnp.int32)
    match = ids[None] == own[:, None, None, None]
    named = jnp.any(match, axis=2)
    shares = table[:, 1] + table[:, 2] + table[:, 3]
    weights = jnp.sum(jnp.where(match, shares[None], 0.0), axis=2)
    span = PAIR * here
    order = jnp.arange(span)
    earlier = (order[:, None] < order[None, :]).astype(BF16)
    rank = jnp.dot(
        named.astype(BF16).reshape(experts * groups // PAIR, span),
        earlier,
        preferred_element_type=F32,
    )
    slots = jnp.where(named, rank.reshape(named.shape).astype(jnp.int32), -1)
    return slots.reshape(experts, groups * here), weights.reshape(experts, groups * here)


def block_table(device, groups, member):
    number = jnp.arange(32, dtype=jnp.int32)
    array, place = number >> 3, number & 7
    source_core = (device & 1) ^ (array >> 1)
    first = jnp.where(source_core == 0, X, Y)
    last = jnp.where(source_core == 0, Y, X)
    feature = (
        device
        ^ (array >> 1)
        ^ jnp.where(array & 1 == 1, first, 0)
        ^ jnp.where(place & 1 == 1, last, 0)
        ^ jnp.where(place & 2 == 2, ZHIGH, 0)
        ^ jnp.where(place & 4 == 4, ZLOW, 0)
    )
    swapped = ((feature ^ device) >> 2) & 1
    return jnp.concatenate([feature, swapped, jnp.stack([member, device >> 3])])


def gather_blocks(first, second):
    def along(bits, block):
        return flip(block, lambda core: bits)

    def joined(held, came):
        return jnp.concatenate([held, came], axis=0)

    first_last = flip(first, last_axis)
    second_high = along(ZHIGH, second)
    second, _ = after(joined(second, second_high), first_last)
    second_low = along(ZLOW, second)
    first, _ = after(joined(first, first_last), second_high)
    first_high = along(ZHIGH, first)
    second, first_high = after(joined(second, second_low), first_high)
    second_last = flip(second, last_axis)
    first = joined(first, first_high)
    first_low = along(ZLOW, first)
    halves = []
    for early, late in ((first, first_low), (second, second_last)):
        early_first = flip(early, first_axis)
        late, early_first = after(late, early_first)
        late_first = flip(late, first_axis)
        halves.append(
            [
                [block, came, along(CORE, block), along(CORE, came)]
                for block, came in ((early, early_first), (late, late_first))
            ]
        )
    return halves


def per_device_tokens(
    attn_heads, out_proj, residual, norm_gain, route_ids, route_weights, w_gate, w_up, w_down
):
    groups, members = lax.axis_size("expert"), lax.axis_size("tensor")
    group, member = lax.axis_index("expert"), lax.axis_index("tensor")
    device = group * members + member
    here, width = residual.shape
    experts = w_gate.shape[0]
    rows = -(-PAIR * CAP // 16) * 16
    x_side, core, y_side = member >> 1, member & 1, group & 1

    moved = lax.all_to_all(
        pack(member, residual, route_ids, route_weights, groups),
        "expert",
        split_axis=0,
        concat_axis=0,
        tiled=True,
    )
    gain = lax.dynamic_index_in_dim(
        norm_gain.reshape(groups * members, LANES), device, 0, keepdims=False
    )

    pieces, moved = gather_heads(attn_heads, moved)
    numbers = jnp.arange(groups, dtype=jnp.int32)
    arrival = (head_bits(numbers, core) ^ group) ^ y_side
    info = jnp.concatenate(
        [jnp.stack([core, x_side]), ((arrival & 1) << 2) | (arrival >> 1)]
    )
    table = jnp.take(moved[:, here:], own_order(groups, group), axis=0, mode="clip")
    moved = moved[:, :here].reshape(groups // 2, 2, here, LANES)
    slots, weights = own_routes(table, group, experts)
    info, (slots, weights) = after(info, (slots, weights))
    send, keep = project(info, pieces, out_proj)
    came = flip(send, lambda c: CORE)
    from_x = flip(total_of([keep[0], came[0]]).astype(BF16), lambda c: X)
    starts = []
    each = groups // 2
    for half in range(2):
        window = slice(half * each, (half + 1) * each)
        hidden = lax.dynamic_index_in_dim(moved, y_side ^ half, 1, keepdims=False).astype(F32)
        hidden = hidden + total_of([keep[1, window], came[1, window], from_x[window]])
        starts.append((hidden * gain).astype(BF16)[None])

    x = [block for half in gather_blocks(*starts) for part in half for block in part]
    invgain = (1.0 / norm_gain).reshape(groups * members, LANES)
    act, own_hidden, spread = gate_up(
        block_table(device, groups, member), slots, weights, invgain, x, w_gate, w_up, rows, members
    )

    cols = width // members

    def columns_of(to_core, chunk, chunks, orders):
        sides = jnp.stack([1 - x_side, x_side])
        blocks = (sides * 2 + to_core) * chunks + chunk
        places = [halving_places(to_core, group, groups, order) for order in orders]
        return jnp.concatenate([blocks] + places)

    chunks = len(ORDERS)
    chunk_cols = cols // chunks
    other = down(
        columns_of(1 - core, 0, 1, ORDERS), spread, act, w_down, rows, groups, cols, chunks
    )
    came = [flip(piece, lambda c: CORE) for piece in other]

    def terms_of(chunk, earlier):
        place = columns_of(core, chunk, chunks, ORDERS[chunk : chunk + 1])
        if earlier is not None:
            place, _ = after(place, earlier)
        (kept,) = down(place, spread, act, w_down, rows, groups, chunk_cols, 1)
        return [kept, came[chunk]]

    sums = reduce_chunks([functools.partial(terms_of, chunk) for chunk in range(chunks)])
    mixture = jnp.concatenate(sums, axis=1)
    return (own_hidden + mixture).astype(BF16)


def solution(mesh):
    groups, members = mesh.shape["expert"], mesh.shape["tensor"]
    placed = (
        P("expert", "tensor"),
        P("tensor", "expert"),
        P("expert", None),
        P(),
        P("expert", None),
        P("expert", None),
        P("expert", None, "tensor"),
        P("expert", None, "tensor"),
        P("expert", "tensor", None),
    )

    def run(*arrays):
        tokens, width = arrays[2].shape
        whole_tokens = (groups, members) == (8, 4) and width == groups * members * LANES
        body = per_device_tokens if whole_tokens else per_device_slots
        return jax.shard_map(
            body, mesh=mesh, in_specs=placed, out_specs=P("expert", "tensor"), check_vma=False
        )(*arrays)

    return run
```

```python
import functools

import jax
import jax.numpy as jnp
from jax import lax
from jax.experimental import pallas as pl
from jax.experimental.pallas import tpu as pltpu
from jax.sharding import PartitionSpec as P

EXPERTS = 64
CAP = 18
BF16 = jnp.bfloat16
F32 = jnp.float32
PAIR = 2
LANES = 128


def slot_places(ids, experts, capacity):
    row_count, top_count = ids.shape
    onehot = (ids[:, :, None] == jnp.arange(experts, dtype=jnp.int32)[None, None, :]).astype(
        jnp.int32
    )
    flattened = onehot.reshape(row_count * top_count, experts)
    before = jnp.cumsum(flattened, axis=0) - flattened
    slot_rank = jnp.sum(before * flattened, axis=1).reshape(row_count, top_count)
    return ids * capacity + slot_rank


def per_device_slots(
    attn_heads, out_proj, residual, norm_gain, route_ids, route_weights, w_gate, w_up, w_down
):
    model_width = residual.shape[1]
    groups = lax.axis_size("expert")
    members = lax.axis_size("tensor")
    member = lax.axis_index("tensor")
    per_group = w_gate.shape[0]
    slot_count = EXPERTS * CAP
    block_cols = model_width // members
    heads_out = jnp.dot(
        attn_heads,
        lax.all_gather(out_proj, "expert", axis=1, tiled=True),
        preferred_element_type=F32,
    )
    attn_out = lax.psum(heads_out.astype(BF16), "tensor").astype(F32)
    hidden = residual.astype(F32) + attn_out
    normed = (
        hidden * lax.rsqrt(jnp.mean(hidden * hidden, axis=-1, keepdims=True) + 1e-06) * norm_gain
    ).astype(BF16)
    slot_index = slot_places(route_ids, EXPERTS, CAP)
    slot_range = jnp.arange(slot_count, dtype=jnp.int32)
    slot_hits = jnp.sum(
        (slot_index[:, :, None] == slot_range[None, None, :]).astype(BF16), axis=1
    )
    buffer = jnp.einsum("rj,rd->jd", slot_hits, normed, preferred_element_type=F32).astype(BF16)
    buffer = buffer.reshape(groups, per_group, CAP, model_width)
    arrived = lax.all_to_all(buffer, "expert", split_axis=0, concat_axis=0, tiled=True)
    gate_acc = jnp.einsum("gxcd,xdf->gxcf", arrived, w_gate, preferred_element_type=F32)
    upper = jnp.einsum("gxcd,xdf->gxcf", arrived, w_up, preferred_element_type=F32)
    activation = (jax.nn.silu(gate_acc) * upper).astype(BF16)
    product_term = jnp.einsum("gxcf,xfd->gxcd", activation, w_down, preferred_element_type=F32)
    product_term = product_term.astype(BF16).reshape(groups, per_group, CAP, members, block_cols)
    expert_out = lax.psum_scatter(
        jnp.transpose(product_term, (3, 0, 1, 2, 4)), "tensor", scatter_dimension=0, tiled=True
    )[0]
    returned = lax.all_to_all(expert_out, "expert", split_axis=0, concat_axis=0, tiled=True)
    weights = route_weights / jnp.sum(route_weights, axis=-1, keepdims=True)
    picked = returned.reshape(slot_count, block_cols)[slot_index]
    mixture = jnp.sum(weights[:, :, None] * picked.astype(F32), axis=1)
    own_hidden = lax.dynamic_slice_in_dim(hidden, member * block_cols, block_cols, 1)
    return (own_hidden + mixture).astype(BF16)


def hits_of(slot_row, rows):
    places = lax.broadcasted_iota(jnp.int32, (rows, slot_row.shape[1]), 0)
    return places == slot_row


def project_kernel(info_ref, head_refs, weight_ref, send_ref, keep_ref):
    core, x_side = info_ref[0], info_ref[1]
    pieces = [ref.at[i] for ref in head_refs for i in range(ref.shape[0])]
    here = pieces[0].shape[0]
    each = len(pieces) // 2
    for part in range(2):
        result = jnp.dot(
            jnp.concatenate([ref[...] for ref in pieces[part * each : (part + 1) * each]]),
            weight_ref[...],
            preferred_element_type=F32,
        ).astype(BF16)
        for to_x in range(2):
            x_kept = (x_side == to_x).astype(jnp.int32)
            for to_core in range(2):
                start = (to_x * 2 + to_core) * LANES
                for out_ref, wanted in ((keep_ref, core == to_core), (send_ref, core != to_core)):

                    @pl.when(wanted)
                    def _(out_ref=out_ref, x_kept=x_kept, start=start, part=part, result=result):
                        for piece in range(each):
                            out_ref[x_kept, info_ref[2 + part * each + piece]] = result[
                                piece * here : (piece + 1) * here, start : start + LANES
                            ]


def project(info, pieces, out_proj):
    here = pieces[0].shape[1]
    groups = sum(piece.shape[0] for piece in pieces)
    out = jax.ShapeDtypeStruct((2, groups, here, LANES), BF16)
    vmem = pl.BlockSpec(memory_space=pltpu.VMEM)

    def kernel(info_ref, *refs):
        project_kernel(info_ref, refs[: len(pieces)], *refs[len(pieces) :])

    return pl.pallas_call(
        kernel,
        in_specs=[pl.BlockSpec(memory_space=pltpu.SMEM)] + [vmem] * (len(pieces) + 1),
        out_specs=[vmem, vmem],
        out_shape=[out, out],
        compiler_params=pltpu.CompilerParams(vmem_limit_bytes=24 * 1024 * 1024),
        cost_estimate=pl.CostEstimate(
            flops=2 * groups * here * out_proj.size,
            bytes_accessed=2 * (out_proj.size + 2 * groups * pieces[0][0].size),
            transcendentals=0,
        ),
        name="project",
    )(info, *pieces, out_proj)


def gate_up_kernel(
    experts, rows, width, info_ref, slot_ref, weight_ref, invgain_ref, x_refs, wg_ref, wu_ref,
    act_ref, hidden_ref, spread_ref, xs_ref, sq_ref, scale_ref, hits_ref
):
    expert = pl.program_id(0)
    arrays = 4
    own_refs = (x_refs[:arrays], x_refs[arrays : 2 * arrays])
    other_refs = (x_refs[2 * arrays : 3 * arrays], x_refs[3 * arrays :])
    parts, here, lanes = x_refs[0].shape[1:]
    blocks = info_ref.shape[0] // 2 - 1
    each = blocks // arrays
    span = 2 * here
    member, z = info_ref[2 * blocks], info_ref[2 * blocks + 1]

    def block_at(array, last, high, low):
        return (
            array * each + low * 4 + high * 2 + last,
            own_refs[low][array].at[high * 2 + last],
            other_refs[last][array].at[low * 2 + high],
        )

    @pl.when(expert == 0)
    def _():
        sq_ref[...] = jnp.zeros_like(sq_ref)
        for part in range(parts):
            for e in range(experts):
                first = hits_of(slot_ref[e : e + 1, part * span : part * span + here], rows)
                second = hits_of(
                    slot_ref[e : e + 1, part * span + here : (part + 1) * span], rows
                )
                first = first.astype(F32).astype(BF16)
                second = second.astype(F32).astype(BF16)
                window = slice(e * rows, (e + 1) * rows)
                hits_ref[0, part, window, :] = jnp.concatenate([first, second], axis=1)
                hits_ref[1, part, window, :] = jnp.concatenate([second, first], axis=1)
            spread_ref[part] = jnp.transpose(hits_ref[0, part].astype(F32)).astype(BF16)

        def pairs_of_blocks(high, carry):
            for array in range(arrays):
                for last in range(2):
                    pair = [block_at(array, last, high, low) for low in range(2)]
                    swapped = info_ref[blocks + pair[0][0]]
                    features = [info_ref[place] for place, _, _ in pair]
                    for feature, (_, own, other) in zip(features, pair):
                        invgain = invgain_ref[pl.ds(feature, 1), :]
                        for part in range(parts):
                            for half, block in enumerate((own, other)):
                                value = block[part].astype(F32) * invgain
                                sq_ref[swapped, part, half] += value * value
                    for part in range(parts):
                        both = jnp.concatenate(
                            [
                                jnp.concatenate([own[part], other[part]], axis=0)
                                for _, own, other in pair
                            ],
                            axis=1,
                        )
                        picked = jnp.dot(
                            hits_ref[swapped, part], both, preferred_element_type=F32
                        ).astype(BF16)
                        for number, feature in enumerate(features):
                            column = pl.multiple_of(feature * lanes, lanes)
                            for e in range(experts):
                                xs_ref[
                                    e, part * rows : (part + 1) * rows, pl.ds(column, lanes)
                                ] = picked[
                                    e * rows : (e + 1) * rows, number * lanes : (number + 1) * lanes
                                ]
            return carry

        lax.fori_loop(0, 2, pairs_of_blocks, 0)

        def own_blocks(high, carry):
            for array in range(arrays):
                for last in range(2):
                    for low in range(2):
                        place, own, other = block_at(array, last, high, low)
                        feature = info_ref[place]

                        @pl.when(feature >> 3 == member)
                        def _(place=place, feature=feature, own=own, other=other):
                            mine = jnp.where(
                                info_ref[blocks + place] == 0,
                                own[z].astype(F32),
                                other[z].astype(F32),
                            )
                            column = pl.multiple_of((feature & 7) * lanes, lanes)
                            hidden_ref[:, pl.ds(column, lanes)] = (
                                mine * invgain_ref[pl.ds(feature, 1), :]
                            )

            return carry

        lax.fori_loop(0, 2, own_blocks, 0)
        pieces = [
            sq_ref[0, part, half] + sq_ref[1, part, 1 - half]
            for part in range(parts)
            for half in range(2)
        ]
        total = jnp.sum(
            jnp.transpose(jnp.concatenate(pieces, axis=0)), axis=0, keepdims=True
        )
        scale_ref[...] = jnp.broadcast_to(lax.rsqrt(total / width + 1e-06), scale_ref.shape)

    summed = jnp.dot(
        xs_ref[expert],
        jnp.concatenate([wg_ref[0], wu_ref[0]], axis=1),
        preferred_element_type=F32,
    )
    hidden_units = wg_ref.shape[2]
    for part in range(parts):
        window = slice(part * span, (part + 1) * span)
        hits = hits_of(slot_ref[pl.ds(expert, 1), window], rows)
        scale = jnp.sum(jnp.where(hits, scale_ref[0:1, window], 0.0), axis=1, keepdims=True)
        weight = jnp.sum(
            jnp.where(hits, weight_ref[pl.ds(expert, 1), window], 0.0), axis=1, keepdims=True
        )
        both_part = summed[part * rows : (part + 1) * rows, :]
        gate = both_part[:, :hidden_units] * scale
        upper = both_part[:, hidden_units:] * scale
        act = gate / (1.0 + jnp.exp(-gate)) * upper * weight
        act_ref[expert, part * rows : (part + 1) * rows, :] = act.astype(BF16)


def gate_up(info, slots, weights, invgain, x, w_gate, w_up, rows, members):
    experts, width, hidden_units = w_gate.shape
    parts, here, lanes = x[0].shape[1:]
    tokens = slots.shape[1]

    def kernel(info_ref, slot_ref, weight_ref, invgain_ref, *rest):
        gate_up_kernel(
            experts, rows, width, info_ref, slot_ref, weight_ref, invgain_ref,
            rest[: len(x)], *rest[len(x) :]
        )

    def whole(shape):
        return pl.BlockSpec(
            shape, lambda e, info: (0,) * len(shape), pipeline_mode=pl.Buffered(1)
        )

    return pl.pallas_call(
        kernel,
        grid_spec=pltpu.PrefetchScalarGridSpec(
            num_scalar_prefetch=1,
            grid=(experts,),
            in_specs=[whole(slots.shape), whole(weights.shape), whole(invgain.shape)]
            + [pl.BlockSpec(memory_space=pltpu.VMEM)] * len(x)
            + [pl.BlockSpec((1, width, hidden_units), lambda e, info: (e, 0, 0))] * 2,
            out_specs=[
                pl.BlockSpec(memory_space=pltpu.VMEM),
                pl.BlockSpec(memory_space=pltpu.VMEM),
                pl.BlockSpec(memory_space=pltpu.VMEM),
            ],
            scratch_shapes=[
                pltpu.VMEM((experts, parts * rows, width), BF16),
                pltpu.VMEM((2, parts, 2, here, lanes), F32),
                pltpu.VMEM((8, tokens), F32),
                pltpu.VMEM((2, parts, experts * rows, 2 * here), BF16),
            ],
        ),
        out_shape=[
            jax.ShapeDtypeStruct((experts, parts * rows, hidden_units), BF16),
            jax.ShapeDtypeStruct((here, width // members), F32),
            jax.ShapeDtypeStruct((parts, 2 * here, experts * rows), BF16),
        ],
        compiler_params=pltpu.CompilerParams(
            vmem_limit_bytes=36 * 1024 * 1024, dimension_semantics=("arbitrary",)
        ),
        cost_estimate=pl.CostEstimate(
            flops=2 * experts * parts * rows * width * 2 * hidden_units,
            bytes_accessed=4 * experts * width * hidden_units + 2 * len(x) * x[0].size,
            transcendentals=0,
        ),
        name="gate_up",
    )(info, slots, weights, invgain, *x, w_gate, w_up)


def down_kernel(rows, place_ref, spread_ref, act_ref, wd0_ref, wd1_ref, *rest):
    out_refs, ys_ref = rest[:-1], rest[-1]
    out_cols = out_refs[0].shape[2]
    step = pl.program_id(0)
    experts, all_rows, _ = act_ref.shape
    per_step = wd0_ref.shape[0]
    parts = all_rows // rows
    groups = parts * PAIR
    for number in range(per_step):
        expert = step * per_step + number
        for side, wd_ref in enumerate((wd0_ref, wd1_ref)):
            result = jnp.dot(
                act_ref[expert], wd_ref[number], preferred_element_type=F32
            ).astype(BF16)
            for part in range(parts):
                ys_ref[side, part, expert] = result[part * rows : (part + 1) * rows, :]

    @pl.when(step == pl.num_programs(0) - 1)
    def _():
        for part in range(parts):
            for side in range(2):
                picked = ys_ref[side, part].reshape(experts * rows, ys_ref.shape[4])
                mixed = jnp.dot(
                    spread_ref[part], picked, preferred_element_type=F32
                ).astype(BF16)
                for i in range(PAIR):
                    for number, out_ref in enumerate(out_refs):
                        block = (number * 2 + side) * groups + part * PAIR + i
                        target = place_ref[2 + block]
                        out_ref[target] = mixed[
                            i * 128 : (i + 1) * 128, number * out_cols : (number + 1) * out_cols
                        ]


def down(place, spread, act, w_down, rows, groups, cols, chunks, per_step=2):
    experts, hidden_units, width = w_down.shape
    parts, span, _ = spread.shape
    here = parts * span // groups
    out = jax.ShapeDtypeStruct((2 * groups, here, cols // chunks), BF16)
    return pl.pallas_call(
        functools.partial(down_kernel, rows),
        grid_spec=pltpu.PrefetchScalarGridSpec(
            num_scalar_prefetch=1,
            grid=(experts // per_step,),
            in_specs=[
                pl.BlockSpec(memory_space=pltpu.VMEM),
                pl.BlockSpec(memory_space=pltpu.VMEM),
                pl.BlockSpec((per_step, hidden_units, cols), lambda e, p: (e, 0, p[0])),
                pl.BlockSpec((per_step, hidden_units, cols), lambda e, p: (e, 0, p[1])),
            ],
            out_specs=[pl.BlockSpec(out.shape, lambda e, p: (0, 0, 0))] * chunks,
            scratch_shapes=[pltpu.VMEM((2, parts, experts, rows, cols), BF16)],
        ),
        out_shape=[out] * chunks,
        compiler_params=pltpu.CompilerParams(
            vmem_limit_bytes=36 * 1024 * 1024, dimension_semantics=("arbitrary",)
        ),
        cost_estimate=pl.CostEstimate(
            flops=8 * experts * parts * rows * cols * hidden_units,
            bytes_accessed=4 * experts * cols * hidden_units + 4 * parts * span * cols,
            transcendentals=0,
        ),
        name="down_mix",
    )(place, spread, act, w_down, w_down)


def flip(array, bits_of):
    pairs = []
    for index in range(32):
        pairs.append((index, index ^ bits_of(index & 1)))
    return lax.ppermute(array, ("expert", "tensor"), pairs)


CORE, X, Y, ZLOW, ZHIGH = 1, 2, 4, 8, 16


def first_axis(core):
    return Y if core else X


def last_axis(core):
    return X if core else Y


def own_order(groups, group):
    order = jnp.arange(groups, dtype=jnp.int32)
    return order ^ (group & 1)


HALVING = {
    "first": first_axis,
    "last": last_axis,
    "low": lambda core: ZLOW,
    "high": lambda core: ZHIGH,
}
ORDERS = (("first", "low", "high", "last"), ("first", "last", "low", "high"))


def halving_places(to_core, group, groups, order):
    g = own_order(groups, group)[None, :]
    y_kept = ((g & 1) == (group & 1)).astype(jnp.int32)
    x_kept = jnp.arange(2, dtype=jnp.int32)[:, None]
    kept = {
        "first": jnp.where(to_core == 0, x_kept, y_kept),
        "last": jnp.where(to_core == 0, y_kept, x_kept),
        "low": (((g >> 1) & 1) == ((group >> 1) & 1)).astype(jnp.int32),
        "high": ((g >> 2) == (group >> 2)).astype(jnp.int32),
    }
    place = 0
    for axis in order:
        place = place * 2 + kept[axis]
    return place.reshape(-1)


def total_of(terms):
    total = terms[0].astype(F32)
    for term in terms[1:]:
        total = total + term.astype(F32)
    return total


def after(value, earlier):
    return lax.optimization_barrier((value, earlier))


def reduce_chunks(makers):
    terms, sends, came = [None, None], [None, None], {}

    def split_exchange(chunk):
        whole = terms[chunk]
        quarter = whole[0].shape[0] // 4
        rows = [slice(i * quarter, (i + 1) * quarter) for i in range(4)]
        bits_of = HALVING[ORDERS[chunk][0]]
        early = total_of([term[rows[0]] for term in whole]).astype(BF16)
        late = total_of([term[rows[1]] for term in whole]).astype(BF16)
        early, late = after(early, late)
        early_came, _ = after(flip(early, bits_of), exchange(0, 1))
        late, early_came = after(late, early_came)
        sends[chunk] = [term[rows[2]] for term in whole] + [early_came]
        terms[chunk] = [term[rows[3]] for term in whole] + [flip(late, bits_of)]

    def exchange(chunk, stage, earlier=None):
        if sends[chunk] is None:
            half = terms[chunk][0].shape[0] // 2
            sends[chunk] = [term[:half] for term in terms[chunk]]
            terms[chunk] = [term[half:] for term in terms[chunk]]
        sent = total_of(sends[chunk]).astype(BF16)
        sends[chunk] = None
        if earlier is not None:
            sent, _ = after(sent, earlier)
        came[chunk, stage] = flip(sent, HALVING[ORDERS[chunk][stage]])
        terms[chunk] = terms[chunk] + [came[chunk, stage]]
        return sent

    terms[0] = makers[0](None)
    terms[1] = makers[1](exchange(0, 0))
    split_exchange(1)
    exchange(1, 1)
    exchange(0, 2)
    exchange(1, 2)
    exchange(1, 3, came[0, 2])
    exchange(0, 3)
    return [total_of([term[0] for term in chunk]) for chunk in terms]


HEAD_STAGES = (
    lambda core: ZHIGH,
    lambda core: ZLOW if core else Y,
    lambda core: Y if core else ZLOW,
)


def head_bits(place, core):
    bits = [(place >> stage) & 1 for stage in range(3)]
    return jnp.where(
        core == 0,
        (bits[0] << 2) | bits[1] | (bits[2] << 1),
        (bits[0] << 2) | (bits[1] << 1) | bits[2],
    )


def gather_heads(heads, make_beside):
    first, second, third = HEAD_STAGES
    heads = heads[None]
    came = flip(heads, first)
    beside = make_beside(came)
    heads = jnp.concatenate([heads, came], axis=0)
    came = flip(heads, second)
    early = flip(heads, third)
    late, (early, beside) = after(came, (early, beside))
    return [heads, came, early, flip(late, third)], beside


def pack_kernel(member_ref, residual_ref, ids_ref, weights_ref, out_ref):
    groups, rows, lanes = out_ref.shape
    here, width = residual_ref.shape
    each = width // groups
    rest = weights_ref[...] / jnp.sum(weights_ref[...], axis=0, keepdims=True)
    parts = [ids_ref[...].astype(F32)]
    for _ in range(3):
        part = rest.astype(BF16).astype(F32)
        parts.append(part)
        rest = rest - part
    table = jnp.concatenate(parts, axis=0).astype(BF16)
    for group in range(groups):
        column = pl.multiple_of(group * each + member_ref[0] * lanes, lanes)
        out_ref[group, :here, :] = residual_ref[:, pl.ds(column, lanes)]
        out_ref[group, here:, :] = table


def pack(member, residual, route_ids, route_weights, groups):
    here, top = route_ids.shape
    vmem = pl.BlockSpec(memory_space=pltpu.VMEM)
    return pl.pallas_call(
        pack_kernel,
        in_specs=[pl.BlockSpec(memory_space=pltpu.SMEM), vmem, vmem, vmem],
        out_specs=vmem,
        out_shape=jax.ShapeDtypeStruct((groups, here + 4 * top, LANES), BF16),
        compiler_params=pltpu.CompilerParams(vmem_limit_bytes=16 * 1024 * 1024),
        cost_estimate=pl.CostEstimate(
            flops=0, bytes_accessed=3 * residual.size, transcendentals=0
        ),
        name="pack",
    )(member.reshape(1), residual, route_ids.T, route_weights.T)


def own_routes(table, group, experts):
    groups, rows, here = table.shape
    top = rows // 4
    own = group * experts + jnp.arange(experts, dtype=jnp.int32)
    table = table.astype(F32).reshape(groups, 4, top, here)
    ids = table[:, 0].astype(jnp.int32)
    match = ids[None] == own[:, None, None, None]
    named = jnp.any(match, axis=2)
    shares = table[:, 1] + table[:, 2] + table[:, 3]
    weights = jnp.sum(jnp.where(match, shares[None], 0.0), axis=2)
    span = PAIR * here
    order = jnp.arange(span)
    earlier = (order[:, None] < order[None, :]).astype(BF16)
    rank = jnp.dot(
        named.astype(BF16).reshape(experts * groups // PAIR, span),
        earlier,
        preferred_element_type=F32,
    )
    slots = jnp.where(named, rank.reshape(named.shape).astype(jnp.int32), -1)
    return slots.reshape(experts, groups * here), weights.reshape(experts, groups * here)


def block_table(device, groups, member):
    number = jnp.arange(32, dtype=jnp.int32)
    array, place = number >> 3, number & 7
    source_core = (device & 1) ^ (array >> 1)
    first = jnp.where(source_core == 0, X, Y)
    last = jnp.where(source_core == 0, Y, X)
    feature = (
        device
        ^ (array >> 1)
        ^ jnp.where(array & 1 == 1, first, 0)
        ^ jnp.where(place & 1 == 1, last, 0)
        ^ jnp.where(place & 2 == 2, ZHIGH, 0)
        ^ jnp.where(place & 4 == 4, ZLOW, 0)
    )
    swapped = ((feature ^ device) >> 2) & 1
    return jnp.concatenate([feature, swapped, jnp.stack([member, device >> 3])])


def gather_blocks(first, second):
    def along(bits, block):
        return flip(block, lambda core: bits)

    def joined(held, came):
        return jnp.concatenate([held, came], axis=0)

    first_last = flip(first, last_axis)
    second_high = along(ZHIGH, second)
    second, _ = after(joined(second, second_high), first_last)
    second_low = along(ZLOW, second)
    first, _ = after(joined(first, first_last), second_high)
    first_high = along(ZHIGH, first)
    second, first_high = after(joined(second, second_low), first_high)
    second_last = flip(second, last_axis)
    first = joined(first, first_high)
    first_low = along(ZLOW, first)
    halves = []
    for early, late in ((first, first_low), (second, second_last)):
        early_first = flip(early, first_axis)
        late, early_first = after(late, early_first)
        late_first = flip(late, first_axis)
        halves.append(
            [
                [block, came, along(CORE, block), along(CORE, came)]
                for block, came in ((early, early_first), (late, late_first))
            ]
        )
    return halves


def per_device_tokens(
    attn_heads, out_proj, residual, norm_gain, route_ids, route_weights, w_gate, w_up, w_down
):
    groups, members = lax.axis_size("expert"), lax.axis_size("tensor")
    group, member = lax.axis_index("expert"), lax.axis_index("tensor")
    device = group * members + member
    here, width = residual.shape
    experts = w_gate.shape[0]
    rows = -(-PAIR * CAP // 16) * 16
    x_side, core, y_side = member >> 1, member & 1, group & 1

    def exchange_residual(earlier):
        own, _ = after(member, earlier)
        packed = pack(own, residual, route_ids, route_weights, groups)
        return lax.all_to_all(packed, "expert", split_axis=0, concat_axis=0, tiled=True)

    gain = lax.dynamic_index_in_dim(
        norm_gain.reshape(groups * members, LANES), device, 0, keepdims=False
    )

    pieces, moved = gather_heads(attn_heads, exchange_residual)
    numbers = jnp.arange(groups, dtype=jnp.int32)
    arrival = (head_bits(numbers, core) ^ group) ^ y_side
    info = jnp.concatenate(
        [jnp.stack([core, x_side]), ((arrival & 1) << 2) | (arrival >> 1)]
    )
    table = jnp.take(moved[:, here:], own_order(groups, group), axis=0, mode="clip")
    moved = moved[:, :here].reshape(groups // 2, 2, here, LANES)
    slots, weights = own_routes(table, group, experts)
    info, (slots, weights) = after(info, (slots, weights))
    send, keep = project(info, pieces, out_proj)
    came = flip(send, lambda c: CORE)
    from_x = flip(total_of([keep[0], came[0]]).astype(BF16), lambda c: X)
    starts = []
    each = groups // 2
    for half in range(2):
        window = slice(half * each, (half + 1) * each)
        hidden = lax.dynamic_index_in_dim(moved, y_side ^ half, 1, keepdims=False).astype(F32)
        hidden = hidden + total_of([keep[1, window], came[1, window], from_x[window]])
        starts.append((hidden * gain).astype(BF16)[None])

    x = [block for half in gather_blocks(*starts) for part in half for block in part]
    invgain = (1.0 / norm_gain).reshape(groups * members, LANES)
    act, own_hidden, spread = gate_up(
        block_table(device, groups, member), slots, weights, invgain, x, w_gate, w_up, rows, members
    )

    cols = width // members

    def columns_of(to_core, chunk, chunks, orders):
        sides = jnp.stack([1 - x_side, x_side])
        blocks = (sides * 2 + to_core) * chunks + chunk
        places = [halving_places(to_core, group, groups, order) for order in orders]
        return jnp.concatenate([blocks] + places)

    chunks = len(ORDERS)
    chunk_cols = cols // chunks
    other = down(
        columns_of(1 - core, 0, 1, ORDERS), spread, act, w_down, rows, groups, cols, chunks
    )
    came = [flip(piece, lambda c: CORE) for piece in other]

    def terms_of(chunk, earlier):
        place = columns_of(core, chunk, chunks, ORDERS[chunk : chunk + 1])
        if earlier is not None:
            place, _ = after(place, earlier)
        (kept,) = down(place, spread, act, w_down, rows, groups, chunk_cols, 1)
        return [kept, came[chunk]]

    sums = reduce_chunks([functools.partial(terms_of, chunk) for chunk in range(chunks)])
    mixture = jnp.concatenate(sums, axis=1)
    return (own_hidden + mixture).astype(BF16)


def solution(mesh):
    groups, members = mesh.shape["expert"], mesh.shape["tensor"]
    placed = (
        P("expert", "tensor"),
        P("tensor", "expert"),
        P("expert", None),
        P(),
        P("expert", None),
        P("expert", None),
        P("expert", None, "tensor"),
        P("expert", None, "tensor"),
        P("expert", "tensor", None),
    )

    def run(*arrays):
        tokens, width = arrays[2].shape
        whole_tokens = (groups, members) == (8, 4) and width == groups * members * LANES
        body = per_device_tokens if whole_tokens else per_device_slots
        return jax.shard_map(
            body, mesh=mesh, in_specs=placed, out_specs=P("expert", "tensor"), check_vma=False
        )(*arrays)

    return run
```
